32 devices in a mesh: seq: 8 (over z, y), tp: 4 (over x, core).
Axes of the slice: x: 2, y: 2, z: 4, core: 2. Of those that a mesh axis runs over, the one named last changes fastest.
Arguments:
- normed_input: bfloat16 [4096, 5376], P('seq', 'tp'), may hold values from -6 to 6
- query: bfloat16 [4096, 4096], P('seq', 'tp'), may hold values from -220 to 220, as said below
- key: bfloat16 [4096, 2048], P('seq', 'tp'), may hold values from -7 to 7
- value: bfloat16 [4096, 2048], P('seq', 'tp'), may hold values from -6 to 6
- adapter_down_maps: bfloat16 [64, 16, 5376], P(None, None, 'tp'), may hold values from -0.078125 to 0.078125
- adapter_up_maps: bfloat16 [64, 16, 2048], P(None, None, 'tp'), may hold values from -1.5 to 1.5
- block_adapter_choice: int32 [2], replicated, may hold values from 0 to 63
Outputs:
- attended: bfloat16 [4096, 4096], P('seq', 'tp')
The draws below stay inside these ranges and needn't reach their ends.
Inputs may be any that keep to these rules, and one draw needn't show every extreme that they name: `query`: queries; some may be aligned with nearby keys.
All inputs are finite; a program needn't handle non-finite values.
Results may differ from the reference program's by a relative error of at most 0.014.
Values may be sent and summed in bfloat16 or wider, within the bound.
No kernel may reach another device: no remote copies, remote signals or barrier semaphores. Data moves between devices by JAX's collectives and lax.ppermute only.
A program may use at most 128 MiB of HBM per device.

```python
import math
import jax
import jax.numpy as jnp
import numpy as np
from jax import lax

MODEL_WIDTH = 5376
HEADS = 32
KEY_VALUE_HEADS = 16
HEAD_WIDTH = 128
WINDOW = 1024
ADAPTER_COUNT = 64
ADAPTER_RANK = 16
SEG_LEN = 2048
TOKENS = 4096
SEGMENTS = 2


def query_key_pair(key):
    base = jax.random.fold_in(key, 11)
    key_k, key_q = jax.random.split(base, 2)
    keys_drawn = jnp.clip(jax.random.normal(key_k, (TOKENS, KEY_VALUE_HEADS * HEAD_WIDTH), jnp.float32), -6.0, 6.0)
    queries = jnp.clip(jax.random.normal(key_q, (TOKENS, HEADS, HEAD_WIDTH), jnp.float32), -6.0, 6.0)
    return (queries.reshape(TOKENS, HEADS * HEAD_WIDTH), keys_drawn)


def draw_query(key, part):
    return query_key_pair(key)[0].astype(jnp.bfloat16)


def draw_key(key, part):
    return query_key_pair(key)[1].astype(jnp.bfloat16)


def levels(own_key, shape, cuts, least, top_value):
    factor_of = 1.0
    for dim, parts in cuts:
        heights = jax.random.uniform(jax.random.fold_in(jax.random.fold_in(own_key, 6), dim), (parts,), jnp.float32, least / len(cuts), top_value / len(cuts))
        factor_of = factor_of * jnp.repeat(jnp.exp(heights), shape[dim] // parts).reshape((-1,) + (1,) * (len(shape) - 1 - dim))
    return factor_of


def cumulative_ranks(number_of, lean):
    portions = [(1 << 20) // math.isqrt(grade ** lean) + 1 for grade in range(1, number_of + 1)]
    width = 1 + sum(portions) // (1 << 30)
    return np.cumsum(np.array([max(1, weight // width) for weight in portions]))


def ranked_ids(key, extent, amount, skew):
    grid = cumulative_ranks(amount, skew)
    lot = jax.random.randint(jax.random.fold_in(key, 1), extent, 0, int(grid[amount - 1]))
    standing = jnp.searchsorted(jnp.asarray(grid, jnp.int32), lot, side="right")
    return jax.random.permutation(jax.random.fold_in(key, 2), amount)[standing].astype(jnp.int32)


def bell_draw(own_key, shape, deviation, most, cuts=(), kind=jnp.bfloat16):
    result = jax.random.normal(own_key, shape, jnp.float32) * deviation
    if len(cuts) > 0:
        result = levels(own_key, shape, cuts, -0.22, 0.18) * result
    return jnp.clip(result, min=-most, max=most).astype(kind)


def setup_inputs(seed: int = 0) -> dict:
    key_list = jax.random.split(jax.random.key(seed), 8)
    normed_input = bell_draw(key_list[0], (TOKENS, MODEL_WIDTH), 1.0, 6.0, ((0, 8), (1, 4)))
    query = draw_query(jax.random.fold_in(key_list[7], 71), 0)
    key = draw_key(jax.random.fold_in(key_list[7], 71), 0)
    value = bell_draw(key_list[3], (TOKENS, KEY_VALUE_HEADS * HEAD_WIDTH), 1.0, 6.0, ((0, 8), (1, 4)))
    adapter_down_maps = bell_draw(key_list[4], (ADAPTER_COUNT, ADAPTER_RANK, MODEL_WIDTH), MODEL_WIDTH ** -0.5, 0.078125, ((2, 4),))
    adapter_up_maps = bell_draw(key_list[5], (ADAPTER_COUNT, ADAPTER_RANK, KEY_VALUE_HEADS * HEAD_WIDTH), ADAPTER_RANK ** -0.5, 1.5, ((2, 4),))
    block_adapter_choice = ranked_ids(key_list[6], (SEGMENTS,), ADAPTER_COUNT, 2)
    return {"normed_input": normed_input, "query": query, "key": key, "value": value, "adapter_down_maps": adapter_down_maps, "adapter_up_maps": adapter_up_maps, "block_adapter_choice": block_adapter_choice}


query_scale = 168.0 ** -0.5


def reference(normed_input, query, key, value, adapter_down_maps, adapter_up_maps, block_adapter_choice):
    nseg = block_adapter_choice.shape[0]
    columns = value.shape[1]

    def segment_values(seg):
        first = (seg * SEG_LEN).astype(jnp.int32)
        token_rows = lax.dynamic_slice_in_dim(normed_input, first, SEG_LEN, 0)
        adapter_index = block_adapter_choice[seg]
        rank_activation = jnp.dot(token_rows, adapter_down_maps[adapter_index].T, preferred_element_type=jnp.float32).astype(jnp.bfloat16)
        base = lax.dynamic_slice_in_dim(value, first, SEG_LEN, 0)
        value_update = jnp.dot(rank_activation, adapter_up_maps[adapter_index], preferred_element_type=jnp.float32)
        return (base.astype(jnp.float32) + value_update).astype(jnp.bfloat16)

    value_full = lax.map(segment_values, jnp.arange(nseg, dtype=jnp.int32)).reshape(TOKENS, columns)
    group = HEADS // KEY_VALUE_HEADS
    qblock = min(512, TOKENS)
    span = qblock + WINDOW
    key_pad = jnp.concatenate([jnp.zeros((WINDOW, columns), jnp.bfloat16), key], axis=0)
    val_pad = jnp.concatenate([jnp.zeros((WINDOW, columns), jnp.bfloat16), value_full], axis=0)

    def one_block(blk):
        first = (blk * qblock).astype(jnp.int32)
        qrows = lax.dynamic_slice_in_dim(query, first, qblock, 0).astype(jnp.float32)
        qrows = qrows.reshape(qblock, KEY_VALUE_HEADS, group, HEAD_WIDTH)
        krows = lax.dynamic_slice_in_dim(key_pad, first, span, 0).astype(jnp.float32).reshape(span, KEY_VALUE_HEADS, HEAD_WIDTH)
        vrows = lax.dynamic_slice_in_dim(val_pad, first, span, 0).astype(jnp.float32).reshape(span, KEY_VALUE_HEADS, HEAD_WIDTH)
        scores = jnp.einsum("qkgd,lkd->kgql", qrows, krows) * query_scale
        qpos = first + jnp.arange(qblock, dtype=jnp.int32)[:, None]
        kpos = first - WINDOW + jnp.arange(span, dtype=jnp.int32)[None, :]
        usable = (kpos <= qpos) & (qpos - kpos < WINDOW) & (kpos >= 0)
        scores = jnp.where(usable, scores, -1e30)
        top = jnp.max(scores, axis=-1, keepdims=True)
        expo = jnp.exp(scores - top)
        weights = (expo / jnp.sum(expo, axis=-1, keepdims=True)).astype(jnp.bfloat16)
        out = jnp.einsum("kgql,lkd->qkgd", weights.astype(jnp.float32), vrows)
        return out.astype(jnp.bfloat16).reshape(qblock, HEADS * HEAD_WIDTH)

    blocks = lax.map(one_block, jnp.arange(TOKENS // qblock, dtype=jnp.int32))
    return blocks.reshape(TOKENS, HEADS * HEAD_WIDTH)
```

```python
import functools

import jax
import jax.numpy as jnp
from jax import lax
from jax.experimental import pallas as pl
from jax.experimental.pallas import tpu as pltpu
from jax.sharding import PartitionSpec as P

HEAD_WIDTH = 128
WINDOW = 1024
SEG_LEN = 2048
SCALE = 168.0 ** (-0.5)
LOG2_E = 1.4426950408889634
EXPONENT = SCALE * LOG2_E
MASKED = -1e30
QROWS = 256
LANES = 128
VMEM = 48 * 1024 * 1024


def params(steps=0):
    return pltpu.CompilerParams(vmem_limit_bytes=VMEM, dimension_semantics=("arbitrary",) * steps)


def dot(left, right, left_dim, right_dim):
    return lax.dot_general(
        left, right, (((left_dim,), (right_dim,)), ((), ())), preferred_element_type=jnp.float32
    )


def latent_kernel(ids, input_t, down, out):
    out[...] = dot(down[0], input_t[...], 1, 0)


def latent_share(ids, input_t, down_maps):
    features, tok = input_t.shape
    rank = down_maps.shape[1]
    return pl.pallas_call(
        latent_kernel,
        grid_spec=pltpu.PrefetchScalarGridSpec(
            num_scalar_prefetch=1,
            grid=(1,),
            in_specs=[
                pl.BlockSpec((features, tok), lambda i, ids: (0, 0)),
                pl.BlockSpec((1, rank, features), lambda i, ids: (ids[0], 0, 0)),
            ],
            out_specs=pl.BlockSpec((rank, tok), lambda i, ids: (0, 0)),
        ),
        out_shape=jax.ShapeDtypeStruct((rank, tok), jnp.float32),
        compiler_params=params(1),
        name="latent_share",
    )(ids, input_t, down_maps)


def adapt_kernel(ids, mine, theirs, up, value, out):
    latent = (mine[...] + theirs[...]).astype(jnp.bfloat16)
    update = dot(latent, up[0], 0, 0)
    out[...] = (value[...].astype(jnp.float32) + update).astype(jnp.bfloat16)


def adapt(ids, mine, theirs, up_maps, value):
    rank, tok = mine.shape
    columns = value.shape[1]
    whole = lambda i, ids: (0, 0)
    return pl.pallas_call(
        adapt_kernel,
        grid_spec=pltpu.PrefetchScalarGridSpec(
            num_scalar_prefetch=1,
            grid=(1,),
            in_specs=[
                pl.BlockSpec((rank, tok), whole),
                pl.BlockSpec((rank, tok), whole),
                pl.BlockSpec((1, rank, columns), lambda i, ids: (ids[0], 0, 0)),
                pl.BlockSpec((tok, columns), whole),
            ],
            out_specs=pl.BlockSpec((tok, columns), whole),
        ),
        out_shape=jax.ShapeDtypeStruct((tok, columns), jnp.bfloat16),
        compiler_params=params(1),
        name="adapt_values",
    )(ids, mine, theirs, up_maps, value)


def put_lane(lane, which, column, rest):
    return jnp.where(lane == which, column, rest)


def near_far_kernel(group, ids, q, k, v, k_far, out, weights_far, tops, sums):
    far_there = ids[1] >= 2
    tok = q.shape[0]
    lane = lax.broadcasted_iota(jnp.int32, (QROWS, LANES), 1)
    row = lax.broadcasted_iota(jnp.int32, (QROWS, QROWS), 0)
    col = lax.broadcasted_iota(jnp.int32, (QROWS, QROWS), 1)
    causal = col <= row
    beyond = (col > row) & far_there
    parts = tok // QROWS
    for i in range(parts):
        rows = slice(i * QROWS, (i + 1) * QROWS)
        top_all = jnp.zeros((QROWS, LANES), jnp.float32)
        sum_all = jnp.zeros((QROWS, LANES), jnp.float32)
        for h in range(group):
            columns = slice(h * HEAD_WIDTH, (h + 1) * HEAD_WIDTH)
            qh = q[rows, columns]
            near, far = [], []
            for j in range(i + 1):
                s = dot(qh, k[j * QROWS : (j + 1) * QROWS, :], 1, 1)
                near.append(jnp.where(causal, s, MASKED) if j == i else s)
            for j in range(i, parts):
                s = dot(qh, k_far[j * QROWS : (j + 1) * QROWS, :], 1, 1)
                far.append(jnp.where(beyond if j == i else far_there, s, MASKED))
            top = functools.reduce(jnp.maximum, near + far)
            top = jnp.max(top, axis=1, keepdims=True)
            near = [jnp.exp2((s - top) * EXPONENT) for s in near]
            far = [jnp.exp2((s - top) * EXPONENT) for s in far]
            total = functools.reduce(jnp.add, near + far)
            total = jnp.sum(total, axis=1, keepdims=True)
            acc = None
            for j, p in enumerate(near):
                part = dot(p.astype(jnp.bfloat16), v[j * QROWS : (j + 1) * QROWS, :], 1, 0)
                acc = part if acc is None else acc + part
            out[rows, columns] = acc
            for j, p in enumerate(far):
                weights_far[h, rows, (i + j) * QROWS : (i + j + 1) * QROWS] = p.astype(jnp.bfloat16)
            top_all = put_lane(lane, h, top, top_all)
            sum_all = put_lane(lane, h, total, sum_all)
        tops[0, rows, :] = top_all
        sums[0, rows, :] = sum_all


def near_far(ids, query, key, value, key_far):
    tok, columns = key.shape
    kv_heads = columns // HEAD_WIDTH
    heads = query.shape[1] // HEAD_WIDTH
    group = heads // kv_heads
    by_column = lambda g, ids: (0, g)
    by_head = lambda g, ids: (g, 0, 0)
    kv_block = pl.BlockSpec((tok, HEAD_WIDTH), by_column)
    q_block = pl.BlockSpec((tok, group * HEAD_WIDTH), by_column)
    stat_block = pl.BlockSpec((1, tok, LANES), by_head)
    stat = jax.ShapeDtypeStruct((kv_heads, tok, LANES), jnp.float32)
    return pl.pallas_call(
        functools.partial(near_far_kernel, group),
        grid_spec=pltpu.PrefetchScalarGridSpec(
            num_scalar_prefetch=1,
            grid=(kv_heads,),
            in_specs=[q_block, kv_block, kv_block, kv_block],
            out_specs=[q_block, pl.BlockSpec((group, tok, tok), by_head), stat_block, stat_block],
        ),
        out_shape=[
            jax.ShapeDtypeStruct(query.shape, jnp.float32),
            jax.ShapeDtypeStruct((heads, tok, tok), jnp.bfloat16),
            stat,
            stat,
        ],
        compiler_params=params(1),
        name="near_far",
    )(ids, query, key, value, key_far)


def middle_kernel(group, ids, q, k_mid, tops, sums, weights, shrink, inverse):
    there = ids[1] >= 1
    tok = q.shape[0]
    lane = lax.broadcasted_iota(jnp.int32, (QROWS, LANES), 1)
    for i in range(tok // QROWS):
        rows = slice(i * QROWS, (i + 1) * QROWS)
        shrink_all = jnp.zeros((QROWS, LANES), jnp.float32)
        inverse_all = jnp.zeros((QROWS, LANES), jnp.float32)
        for h in range(group):
            qh = q[rows, h * HEAD_WIDTH : (h + 1) * HEAD_WIDTH]
            s = dot(qh, k_mid[...], 1, 1)
            s = jnp.where(there, s, MASKED)
            before = tops[0, rows, h : h + 1]
            top = jnp.maximum(before, jnp.max(s, axis=1, keepdims=True))
            less = jnp.exp2((before - top) * EXPONENT)
            p = jnp.exp2((s - top) * EXPONENT)
            total = sums[0, rows, h : h + 1] * less + jnp.sum(p, axis=1, keepdims=True)
            weights[h, rows, :] = p.astype(jnp.bfloat16)
            one = 1.0 / total
            shrink_all = put_lane(lane, h, less * one, shrink_all)
            inverse_all = put_lane(lane, h, one, inverse_all)
        shrink[0, rows, :] = shrink_all
        inverse[0, rows, :] = inverse_all


def middle(ids, query, key_mid, tops, sums):
    tok, columns = key_mid.shape
    kv_heads = columns // HEAD_WIDTH
    heads = query.shape[1] // HEAD_WIDTH
    group = heads // kv_heads
    by_column = lambda g, ids: (0, g)
    by_head = lambda g, ids: (g, 0, 0)
    stat_block = pl.BlockSpec((1, tok, LANES), by_head)
    stat = jax.ShapeDtypeStruct(tops.shape, jnp.float32)
    return pl.pallas_call(
        functools.partial(middle_kernel, group),
        grid_spec=pltpu.PrefetchScalarGridSpec(
            num_scalar_prefetch=1,
            grid=(kv_heads,),
            in_specs=[
                pl.BlockSpec((tok, group * HEAD_WIDTH), by_column),
                pl.BlockSpec((tok, HEAD_WIDTH), by_column),
                stat_block,
                stat_block,
            ],
            out_specs=[pl.BlockSpec((group, tok, tok), by_head), stat_block, stat_block],
        ),
        out_shape=[jax.ShapeDtypeStruct((heads, tok, tok), jnp.bfloat16), stat, stat],
        compiler_params=params(1),
        name="middle",
    )(ids, query, key_mid, tops, sums)


def finish_kernel(group, own, weights_far, weights_mid, v_far, v_mid, shrink, inverse, out):
    tok = own.shape[0]
    for i in range(tok // QROWS):
        rows = slice(i * QROWS, (i + 1) * QROWS)
        for h in range(group):
            columns = slice(h * HEAD_WIDTH, (h + 1) * HEAD_WIDTH)
            far = dot(weights_far[h, rows, i * QROWS :], v_far[i * QROWS :, :], 1, 0)
            mid = dot(weights_mid[h, rows, :], v_mid[...], 1, 0)
            less, one = shrink[0, rows, h : h + 1], inverse[0, rows, h : h + 1]
            total = (own[rows, columns] + far) * less + mid * one
            out[rows, columns] = total.astype(jnp.bfloat16)


def finish(own, weights_far, weights_mid, value_far, value_mid, shrink, inverse):
    tok, columns = value_far.shape
    kv_heads = columns // HEAD_WIDTH
    group = weights_far.shape[0] // kv_heads
    by_column = lambda g: (0, g)
    by_head = lambda g: (g, 0, 0)
    weight_block = pl.BlockSpec((group, tok, tok), by_head)
    kv_block = pl.BlockSpec((tok, HEAD_WIDTH), by_column)
    q_block = pl.BlockSpec((tok, group * HEAD_WIDTH), by_column)
    stat_block = pl.BlockSpec((1, tok, LANES), by_head)
    return pl.pallas_call(
        functools.partial(finish_kernel, group),
        grid=(kv_heads,),
        in_specs=[q_block, weight_block, weight_block, kv_block, kv_block, stat_block, stat_block],
        out_specs=q_block,
        out_shape=jax.ShapeDtypeStruct(own.shape, jnp.bfloat16),
        compiler_params=params(1),
        name="finish",
    )(own, weights_far, weights_mid, value_far, value_mid, shrink, inverse)


def shifted(array, steps):
    count = lax.axis_size("seq")
    return lax.ppermute(array, "seq", [(source, source + steps) for source in range(count - steps)])


def exchanged(array, axis, bit):
    count = lax.axis_size(axis)
    return lax.ppermute(array, axis, [(source, source ^ bit) for source in range(count)])


def on_device(
    normed_input, query, key, value, adapter_down_maps, adapter_up_maps, block_adapter_choice
):
    tok = query.shape[0]
    assert 2 * tok == WINDOW and SEG_LEN % tok == 0
    place = lax.axis_index("seq")
    adapter = lax.dynamic_index_in_dim(
        block_adapter_choice, place * tok // SEG_LEN, keepdims=False
    )
    ids = jnp.stack([adapter, place]).astype(jnp.int32)

    key_far = shifted(key, 2)
    latent = latent_share(ids, normed_input.T, adapter_down_maps)
    bit = 1
    while 2 * bit < lax.axis_size("tp"):
        latent = latent + exchanged(latent, "tp", bit)
        bit *= 2
    value_full = adapt(ids, latent, exchanged(latent, "tp", bit), adapter_up_maps, value)
    value_mid = shifted(value_full, 1)
    value_far = shifted(value_full, 2)
    key_mid = exchanged(jnp.where(place % 2 == 0, key, key_far), "seq", 1)

    own, weights_far, tops, sums = near_far(ids, query, key, value_full, key_far)
    weights_mid, shrink, inverse = middle(ids, query, key_mid, tops, sums)
    return finish(own, weights_far, weights_mid, value_far, value_mid, shrink, inverse)


def solution(mesh):
    placed = (
        P("seq", "tp"),
        P("seq", "tp"),
        P("seq", "tp"),
        P("seq", "tp"),
        P(None, None, "tp"),
        P(None, None, "tp"),
        P(),
    )
    return jax.shard_map(
        on_device, mesh=mesh, in_specs=placed, out_specs=P("seq", "tp"), check_vma=False
    )
```

```python
import functools

import jax
import jax.numpy as jnp
from jax import lax
from jax.experimental import pallas as pl
from jax.experimental.pallas import tpu as pltpu
from jax.sharding import PartitionSpec as P

HEAD_WIDTH = 128
WINDOW = 1024
SEG_LEN = 2048
SCALE = 168.0 ** (-0.5)
LOG2_E = 1.4426950408889634
EXPONENT = SCALE * LOG2_E
MASKED = -1e30
QROWS = 256


def params(steps, mib):
    return pltpu.CompilerParams(
        vmem_limit_bytes=mib * 1024 * 1024, dimension_semantics=("arbitrary",) * steps
    )


def dot(left, right, left_dim, right_dim):
    return lax.dot_general(
        left, right, (((left_dim,), (right_dim,)), ((), ())), preferred_element_type=jnp.float32
    )


def in_hbm(array):
    return pltpu.with_memory_space_constraint(array, pltpu.HBM)


def adapter_of(place, choice, tok):
    return choice[lax.div(place[0] * tok, SEG_LEN)]


def latent_kernel(pieces, place, choice, input_t, down, out, rows, map_rows, sems):
    tok = out.shape[1]
    copies = [
        pltpu.make_async_copy(
            down.at[adapter_of(place, choice, tok)], map_rows, sems.at[len(pieces)]
        )
    ]
    for n, (first, last) in enumerate(pieces):
        part = pl.ds(first, last - first)
        copies.append(pltpu.make_async_copy(input_t.at[part], rows.at[part], sems.at[n]))
    for copy in copies:
        copy.start()
    copies[0].wait()
    total = None
    for (first, last), copy in zip(pieces, copies[1:]):
        copy.wait()
        product = dot(map_rows[:, first:last], rows[first:last, :], 1, 0)
        total = product if total is None else total + product
    out[...] = total


def latent_share(place, choice, input_t, down_maps):
    features, tok = input_t.shape
    rank = down_maps.shape[1]
    pieces = [(first, min(first + 512, features)) for first in range(0, features, 512)]
    return pl.pallas_call(
        functools.partial(latent_kernel, pieces),
        grid_spec=pltpu.PrefetchScalarGridSpec(
            num_scalar_prefetch=2,
            grid=(1,),
            in_specs=[
                pl.BlockSpec(memory_space=pltpu.HBM),
                pl.BlockSpec(memory_space=pltpu.HBM),
            ],
            out_specs=pl.BlockSpec((rank, tok), lambda i, *_: (0, 0)),
            scratch_shapes=[
                pltpu.VMEM((features, tok), input_t.dtype),
                pltpu.VMEM((rank, features), down_maps.dtype),
                pltpu.SemaphoreType.DMA((len(pieces) + 1,)),
            ],
        ),
        out_shape=jax.ShapeDtypeStruct((rank, tok), jnp.float32),
        compiler_params=params(1, 8),
        name="latent_share",
    )(place, choice, in_hbm(input_t), in_hbm(down_maps))


def adapt_kernel(place, choice, mine, theirs, up, value, out, map_rows, sem):
    copy = pltpu.make_async_copy(up.at[adapter_of(place, choice, out.shape[0])], map_rows, sem)
    copy.start()
    latent = (mine[...] + theirs[...]).astype(jnp.bfloat16)
    copy.wait()
    update = dot(latent, map_rows[...], 0, 0)
    out[...] = (value[...].astype(jnp.float32) + update).astype(jnp.bfloat16)


def adapt(place, choice, mine, theirs, up_maps, value):
    rank, tok = mine.shape
    columns = value.shape[1]
    whole = lambda i, *_: (0, 0)
    return pl.pallas_call(
        adapt_kernel,
        grid_spec=pltpu.PrefetchScalarGridSpec(
            num_scalar_prefetch=2,
            grid=(1,),
            in_specs=[
                pl.BlockSpec((rank, tok), whole),
                pl.BlockSpec((rank, tok), whole),
                pl.BlockSpec(memory_space=pltpu.HBM),
                pl.BlockSpec((tok, columns), whole),
            ],
            out_specs=pl.BlockSpec((tok, columns), whole),
            scratch_shapes=[
                pltpu.VMEM((rank, columns), up_maps.dtype),
                pltpu.SemaphoreType.DMA,
            ],
        ),
        out_shape=jax.ShapeDtypeStruct((tok, columns), jnp.bfloat16),
        compiler_params=params(1, 8),
        name="adapt_values",
    )(place, choice, mine, theirs, in_hbm(up_maps), value)


def weights_of(scores, top):
    return jnp.exp2((scores - top) * EXPONENT)


def tops_of(scores):
    return functools.reduce(
        jnp.maximum, [jnp.max(s, axis=0, keepdims=True) for s in scores]
    )


def sums_of(weights):
    return functools.reduce(jnp.add, [jnp.sum(p, axis=0, keepdims=True) for p in weights])


def near_far_kernel(group, place, q, k, v, k_far, out, weights_far, tops, sums):
    far_there = place[0] >= 2
    tok = q.shape[0]
    key = lax.broadcasted_iota(jnp.int32, (QROWS, QROWS), 0)
    query = lax.broadcasted_iota(jnp.int32, (QROWS, QROWS), 1)
    causal = key <= query
    v_t = v[...].T
    parts = tok // QROWS
    blocks = [slice(i * QROWS, (i + 1) * QROWS) for i in range(parts)]
    for i in range(parts):
        for h in range(group):
            columns = slice(h * HEAD_WIDTH, (h + 1) * HEAD_WIDTH)
            qh = q[blocks[i], columns]
            near = [dot(k[blocks[j], :], qh, 1, 1) for j in range(i + 1)]
            far = [dot(k_far[blocks[j], :], qh, 1, 1) for j in range(i, parts)]
            near[i] = jnp.where(causal, near[i], MASKED)
            far[0] = jnp.where(causal, MASKED, far[0])
            top = jnp.maximum(tops_of(near), jnp.where(far_there, tops_of(far), MASKED))
            far_top = jnp.where(far_there, top, -MASKED)
            near = [weights_of(s, top) for s in near]
            far = [weights_of(s, far_top) for s in far]
            tops[0, h : h + 1, blocks[i]] = top
            sums[0, h : h + 1, blocks[i]] = sums_of(near + far)
            acc = None
            for j, p in enumerate(near):
                part = dot(v_t[:, blocks[j]], p.astype(jnp.bfloat16), 1, 0)
                acc = part if acc is None else acc + part
            out[columns, blocks[i]] = acc
            for j, p in enumerate(far):
                weights_far[h, blocks[i + j], blocks[i]] = p.astype(jnp.bfloat16)


def near_far(place, query, key, value, key_far):
    tok, columns = key.shape
    kv_heads = columns // HEAD_WIDTH
    heads = query.shape[1] // HEAD_WIDTH
    group = heads // kv_heads
    by_column = lambda g, *_: (0, g)
    by_head = lambda g, *_: (g, 0, 0)
    kv_block = pl.BlockSpec((tok, HEAD_WIDTH), by_column)
    stat_block = pl.BlockSpec((1, 8, tok), by_head)
    stat = jax.ShapeDtypeStruct((kv_heads, 8, tok), jnp.float32)
    return pl.pallas_call(
        functools.partial(near_far_kernel, group),
        grid_spec=pltpu.PrefetchScalarGridSpec(
            num_scalar_prefetch=1,
            grid=(kv_heads,),
            in_specs=[
                pl.BlockSpec((tok, group * HEAD_WIDTH), by_column),
                kv_block,
                kv_block,
                kv_block,
            ],
            out_specs=[
                pl.BlockSpec((group * HEAD_WIDTH, tok), lambda g, *_: (g, 0)),
                pl.BlockSpec((group, tok, tok), by_head),
                stat_block,
                stat_block,
            ],
        ),
        out_shape=[
            jax.ShapeDtypeStruct((heads * HEAD_WIDTH, tok), jnp.float32),
            jax.ShapeDtypeStruct((heads, tok, tok), jnp.bfloat16),
            stat,
            stat,
        ],
        compiler_params=params(1, 14),
        name="near_far",
    )(place, query, key, value, key_far)


def middle_kernel(group, place, q, k_mid, tops, sums, weights, shrink, inverse):
    there = place[0] >= 1
    tok = q.shape[0]
    blocks = [slice(i * QROWS, (i + 1) * QROWS) for i in range(tok // QROWS)]
    for b in blocks:
        for h in range(group):
            qh = q[b, h * HEAD_WIDTH : (h + 1) * HEAD_WIDTH]
            scores = [dot(k_mid[keys, :], qh, 1, 1) for keys in blocks]
            before = tops[0, h : h + 1, b]
            top = jnp.maximum(before, jnp.where(there, tops_of(scores), MASKED))
            less = jnp.exp2((before - top) * EXPONENT)
            weighed = [weights_of(s, jnp.where(there, top, -MASKED)) for s in scores]
            one = 1.0 / (sums[0, h : h + 1, b] * less + sums_of(weighed))
            shrink[0, h : h + 1, b] = less * one
            inverse[0, h : h + 1, b] = one
            for keys, p in zip(blocks, weighed):
                weights[h, keys, b] = p.astype(jnp.bfloat16)


def middle(place, query, key_mid, tops, sums):
    tok, columns = key_mid.shape
    kv_heads = columns // HEAD_WIDTH
    heads = query.shape[1] // HEAD_WIDTH
    group = heads // kv_heads
    by_column = lambda g, *_: (0, g)
    by_head = lambda g, *_: (g, 0, 0)
    stat_block = pl.BlockSpec((1, 8, tok), by_head)
    stat = jax.ShapeDtypeStruct(tops.shape, jnp.float32)
    return pl.pallas_call(
        functools.partial(middle_kernel, group),
        grid_spec=pltpu.PrefetchScalarGridSpec(
            num_scalar_prefetch=1,
            grid=(kv_heads,),
            in_specs=[
                pl.BlockSpec((tok, group * HEAD_WIDTH), by_column),
                pl.BlockSpec((tok, HEAD_WIDTH), by_column),
                stat_block,
                stat_block,
            ],
            out_specs=[pl.BlockSpec((group, tok, tok), by_head), stat_block, stat_block],
        ),
        out_shape=[jax.ShapeDtypeStruct((heads, tok, tok), jnp.bfloat16), stat, stat],
        compiler_params=params(1, 14),
        name="middle",
    )(place, query, key_mid, tops, sums)


def far_values_kernel(group, own, weights, v, out):
    tok = weights.shape[1]
    v_t = v[...].T
    for h in range(group):
        columns = slice(h * HEAD_WIDTH, (h + 1) * HEAD_WIDTH)
        for first in range(0, tok, QROWS):
            b = slice(first, first + QROWS)
            out[columns, b] = own[columns, b] + dot(v_t[:, first:], weights[h, first:, b], 1, 0)


def finish_kernel(group, rest, weights, v, shrink, inverse, out):
    tok = out.shape[0]
    v_t = v[...].T
    for h in range(group):
        columns = slice(h * HEAD_WIDTH, (h + 1) * HEAD_WIDTH)
        for first in range(0, tok, QROWS):
            b = slice(first, first + QROWS)
            mid = dot(v_t, weights[h, :, b], 1, 0)
            total = rest[columns, b] * shrink[0, h : h + 1, b] + mid * inverse[0, h : h + 1, b]
            out[b, columns] = total.T.astype(jnp.bfloat16)


def value_blocks(weights, value):
    tok, columns = value.shape
    kv_heads = columns // HEAD_WIDTH
    group = weights.shape[0] // kv_heads
    by_head = lambda g: (g, 0, 0)
    rest_block = pl.BlockSpec((group * HEAD_WIDTH, tok), lambda g: (g, 0))
    weight_block = pl.BlockSpec((group, tok, tok), by_head)
    kv_block = pl.BlockSpec((tok, HEAD_WIDTH), lambda g: (0, g))
    stat_block = pl.BlockSpec((1, 8, tok), by_head)
    return kv_heads, group, [rest_block, weight_block, kv_block, stat_block, stat_block]


def far_values(own, weights, value):
    kv_heads, group, blocks = value_blocks(weights, value)
    return pl.pallas_call(
        functools.partial(far_values_kernel, group),
        grid=(kv_heads,),
        in_specs=blocks[:3],
        out_specs=blocks[0],
        out_shape=jax.ShapeDtypeStruct(own.shape, own.dtype),
        compiler_params=params(1, 14),
        name="far_values",
    )(own, weights, value)


def finish(rest, weights, value, shrink, inverse):
    kv_heads, group, blocks = value_blocks(weights, value)
    tok = value.shape[0]
    return pl.pallas_call(
        functools.partial(finish_kernel, group),
        grid=(kv_heads,),
        in_specs=blocks,
        out_specs=pl.BlockSpec((tok, group * HEAD_WIDTH), lambda g: (0, g)),
        out_shape=jax.ShapeDtypeStruct((tok, rest.shape[0]), jnp.bfloat16),
        compiler_params=params(1, 14),
        name="finish",
    )(rest, weights, value, shrink, inverse)


def shifted(array, steps):
    count = lax.axis_size("seq")
    return lax.ppermute(array, "seq", [(source, source + steps) for source in range(count - steps)])


def exchanged(array, axis, bit):
    count = lax.axis_size(axis)
    return lax.ppermute(array, axis, [(source, source ^ bit) for source in range(count)])


def on_device(
    normed_input, query, key, value, adapter_down_maps, adapter_up_maps, block_adapter_choice
):
    tok = query.shape[0]
    assert 2 * tok == WINDOW and SEG_LEN % tok == 0
    where = lax.axis_index("seq")
    place = where.reshape(1)
    choice = block_adapter_choice

    key_far = shifted(key, 2)
    latent = latent_share(place, choice, normed_input.T, adapter_down_maps)
    bit = 1
    while 2 * bit < lax.axis_size("tp"):
        latent = latent + exchanged(latent, "tp", bit)
        bit *= 2
    theirs = exchanged(latent, "tp", bit)
    value_full = adapt(place, choice, latent, theirs, adapter_up_maps, value)
    value_far = shifted(value_full, 2)
    value_mid = shifted(value_full, 1)
    key_own, _ = lax.optimization_barrier((key, value_full))
    key_mid = exchanged(jnp.where(where % 2 == 0, key_own, key_far), "seq", 1)

    own, weights_far, tops, sums = near_far(place, query, key, value_full, key_far)
    rest = far_values(own, weights_far, value_far)
    tops, rest = lax.optimization_barrier((tops, rest))
    weights_mid, shrink, inverse = middle(place, query, key_mid, tops, sums)
    return finish(rest, weights_mid, value_mid, shrink, inverse)


def solution(mesh):
    placed = (
        P("seq", "tp"),
        P("seq", "tp"),
        P("seq", "tp"),
        P("seq", "tp"),
        P(None, None, "tp"),
        P(None, None, "tp"),
        P(),
    )
    return jax.shard_map(
        on_device, mesh=mesh, in_specs=placed, out_specs=P("seq", "tp"), check_vma=False
    )
```

```python
import functools

import jax
import jax.numpy as jnp
from jax import lax
from jax.experimental import pallas as pl
from jax.experimental.pallas import tpu as pltpu
from jax.sharding import PartitionSpec as P

HEAD_WIDTH = 128
WINDOW = 1024
SEG_LEN = 2048
SCALE = 168.0 ** (-0.5)
LOG2_E = 1.4426950408889634
EXPONENT = SCALE * LOG2_E
MASKED = -1e30
TILE = 256
HALF = 128
ONES = 16


def params(steps, mib):
    return pltpu.CompilerParams(
        vmem_limit_bytes=mib * 1024 * 1024, dimension_semantics=("arbitrary",) * steps
    )


def dot(left, right, left_dim, right_dim):
    return lax.dot_general(
        left, right, (((left_dim,), (right_dim,)), ((), ())), preferred_element_type=jnp.float32
    )


def in_hbm(array):
    return pltpu.with_memory_space_constraint(array, pltpu.HBM)


def adapter_of(place, choice, tok):
    return choice[lax.div(place[0] * tok, SEG_LEN)]


def latent_kernel(pieces, place, choice, input_t, down, out, rows, map_rows, sems):
    tok = out.shape[1]
    copies = [
        pltpu.make_async_copy(
            down.at[adapter_of(place, choice, tok)], map_rows, sems.at[len(pieces)]
        )
    ]
    for n, (first, last) in enumerate(pieces):
        part = pl.ds(first, last - first)
        copies.append(pltpu.make_async_copy(input_t.at[part], rows.at[part], sems.at[n]))
    for copy in copies:
        copy.start()
    copies[0].wait()
    total = None
    for (first, last), copy in zip(pieces, copies[1:]):
        copy.wait()
        product = dot(map_rows[:, first:last], rows[first:last, :], 1, 0)
        total = product if total is None else total + product
    out[...] = total


def latent_share(place, choice, input_t, down_maps):
    features, tok = input_t.shape
    rank = down_maps.shape[1]
    pieces = [(first, min(first + 512, features)) for first in range(0, features, 512)]
    return pl.pallas_call(
        functools.partial(latent_kernel, pieces),
        grid_spec=pltpu.PrefetchScalarGridSpec(
            num_scalar_prefetch=2,
            grid=(1,),
            in_specs=[
                pl.BlockSpec(memory_space=pltpu.HBM),
                pl.BlockSpec(memory_space=pltpu.HBM),
            ],
            out_specs=pl.BlockSpec((rank, tok), lambda i, *_: (0, 0)),
            scratch_shapes=[
                pltpu.VMEM((features, tok), input_t.dtype),
                pltpu.VMEM((rank, features), down_maps.dtype),
                pltpu.SemaphoreType.DMA((len(pieces) + 1,)),
            ],
        ),
        out_shape=jax.ShapeDtypeStruct((rank, tok), jnp.float32),
        compiler_params=params(1, 8),
        name="latent_share",
    )(place, in_hbm(choice), in_hbm(input_t), in_hbm(down_maps))


def adapt_kernel(place, choice, mine, theirs, up, value, out):
    latent = (mine[...] + theirs[...]).astype(jnp.bfloat16)
    update = dot(latent, up[0], 0, 0)
    out[...] = (value[...].astype(jnp.float32) + update).astype(jnp.bfloat16)


def adapt(place, choice, mine, theirs, up_maps, value):
    rank, tok = mine.shape
    columns = value.shape[1]
    whole = lambda i, *_: (0, 0)
    chosen = lambda i, place, choice: (adapter_of(place, choice, tok), 0, 0)
    return pl.pallas_call(
        adapt_kernel,
        grid_spec=pltpu.PrefetchScalarGridSpec(
            num_scalar_prefetch=2,
            grid=(1,),
            in_specs=[
                pl.BlockSpec((rank, tok), whole),
                pl.BlockSpec((rank, tok), whole),
                pl.BlockSpec((1, rank, columns), chosen),
                pl.BlockSpec((tok, columns), whole),
            ],
            out_specs=pl.BlockSpec((tok, columns), whole),
        ),
        out_shape=jax.ShapeDtypeStruct((tok, columns), jnp.bfloat16),
        compiler_params=params(1, 8),
        name="adapt_values",
    )(place, choice, mine, theirs, up_maps, value)


def weights_of(scores, top):
    return jnp.exp2(((scores - top) * EXPONENT).astype(jnp.bfloat16))


def top_of(scores):
    return functools.reduce(jnp.maximum, [jnp.max(s, axis=0, keepdims=True) for s in scores])


def values_and_ones(v):
    tok = v.shape[0]
    return jnp.concatenate([v[...].T, jnp.ones((ONES, tok), jnp.bfloat16)], axis=0)


def head_rows(h):
    return slice(h * (HEAD_WIDTH + ONES), (h + 1) * (HEAD_WIDTH + ONES))


def near_far_kernel(group, place, q, k, v, k_far, out, weights_far, tops):
    far_there = place[0] >= 2
    tok = q.shape[0]
    causal = lax.broadcasted_iota(jnp.int32, (HALF, HALF), 0) <= lax.broadcasted_iota(
        jnp.int32, (HALF, HALF), 1
    )
    v_t = values_and_ones(v)
    nothing = jnp.zeros((HALF, HALF), jnp.bfloat16)
    parts = tok // TILE
    blocks = [slice(i * TILE, (i + 1) * TILE) for i in range(parts)]
    for i in range(parts):
        for h in range(group):
            qh = q[blocks[i], h * HEAD_WIDTH : (h + 1) * HEAD_WIDTH]
            near = [dot(k[blocks[j], :], qh, 1, 1) for j in range(i + 1)]
            far = [dot(k_far[blocks[j], :], qh, 1, 1) for j in range(i, parts)]
            near_columns, far_columns = [], []
            for half in range(2):
                a = slice(half * HALF, (half + 1) * HALF)
                near_edge = near[i][: (half + 1) * HALF, a]
                far_edge = far[0][half * HALF :, a]
                near_pieces = [s[:, a] for s in near[:i]]
                if half == 1:
                    near_pieces.append(near_edge[:HALF])
                near_pieces.append(jnp.where(causal, near_edge[half * HALF :], MASKED))
                far_pieces = [jnp.where(causal, MASKED, far_edge[:HALF])]
                if half == 0:
                    far_pieces.append(far_edge[HALF:])
                far_pieces += [s[:, a] for s in far[1:]]
                top = jnp.maximum(
                    top_of(near_pieces), jnp.where(far_there, top_of(far_pieces), MASKED)
                )
                far_top = jnp.where(far_there, top, -MASKED)
                near_weights = [weights_of(s, top) for s in near_pieces]
                far_weights = [weights_of(s, far_top) for s in far_pieces]
                if half == 0:
                    near_weights.append(nothing)
                else:
                    far_weights.insert(0, nothing)
                near_columns.append(jnp.concatenate(near_weights, axis=0))
                far_columns.append(jnp.concatenate(far_weights, axis=0))
                queries = slice(i * TILE + half * HALF, i * TILE + (half + 1) * HALF)
                tops[0, h : h + 1, queries] = top
            out[head_rows(h), blocks[i]] = dot(
                v_t[:, : (i + 1) * TILE], jnp.concatenate(near_columns, axis=1), 1, 0
            )
            weights_far[h, i * TILE :, blocks[i]] = jnp.concatenate(far_columns, axis=1)


def head_specs(tok, kv_heads, group):
    return dict(
        queries=pl.BlockSpec((tok, group * HEAD_WIDTH), lambda g, *_: (0, g)),
        one=pl.BlockSpec((tok, HEAD_WIDTH), lambda g, *_: (0, g)),
        rest=pl.BlockSpec((group * (HEAD_WIDTH + ONES), tok), lambda g, *_: (g, 0)),
        weights=pl.BlockSpec((group, tok, tok), lambda g, *_: (g, 0, 0)),
        stat=pl.BlockSpec((1, 8, tok), lambda g, *_: (g, 0, 0)),
    )


def near_far(place, query, key, value, key_far):
    tok, columns = key.shape
    kv_heads = columns // HEAD_WIDTH
    heads = query.shape[1] // HEAD_WIDTH
    group = heads // kv_heads
    spec = head_specs(tok, kv_heads, group)
    return pl.pallas_call(
        functools.partial(near_far_kernel, group),
        grid_spec=pltpu.PrefetchScalarGridSpec(
            num_scalar_prefetch=1,
            grid=(kv_heads,),
            in_specs=[spec["queries"], spec["one"], spec["one"], spec["one"]],
            out_specs=[spec["rest"], spec["weights"], spec["stat"]],
        ),
        out_shape=[
            jax.ShapeDtypeStruct((heads * (HEAD_WIDTH + ONES), tok), jnp.float32),
            jax.ShapeDtypeStruct((heads, tok, tok), jnp.bfloat16),
            jax.ShapeDtypeStruct((kv_heads, 8, tok), jnp.float32),
        ],
        compiler_params=params(1, 14),
        name="near_far",
    )(place, query, key, value, key_far)


def middle_kernel(group, place, q, k, v, own, tops, rest, shrink):
    there = place[0] >= 1
    tok = q.shape[0]
    v_t = values_and_ones(v)
    blocks = [slice(first, first + TILE) for first in range(0, tok, TILE)]
    for b in blocks:
        for h in range(group):
            qh = q[b, h * HEAD_WIDTH : (h + 1) * HEAD_WIDTH]
            scores = [dot(k[keys, :], qh, 1, 1) for keys in blocks]
            before = tops[0, h : h + 1, b]
            top = jnp.maximum(before, jnp.where(there, top_of(scores), MASKED))
            less = jnp.exp2((before - top) * EXPONENT)
            top = jnp.where(there, top, -MASKED)
            weights = jnp.concatenate([weights_of(s, top) for s in scores], axis=0)
            shrink[0, h : h + 1, b] = less
            rest[head_rows(h), b] = own[head_rows(h), b] * less + dot(v_t, weights, 1, 0)


def middle(place, query, key, value, own, tops):
    tok, columns = key.shape
    kv_heads = columns // HEAD_WIDTH
    group = query.shape[1] // columns
    spec = head_specs(tok, kv_heads, group)
    return pl.pallas_call(
        functools.partial(middle_kernel, group),
        grid_spec=pltpu.PrefetchScalarGridSpec(
            num_scalar_prefetch=1,
            grid=(kv_heads,),
            in_specs=[spec["queries"], spec["one"], spec["one"], spec["rest"], spec["stat"]],
            out_specs=[spec["rest"], spec["stat"]],
        ),
        out_shape=[
            jax.ShapeDtypeStruct(own.shape, own.dtype),
            jax.ShapeDtypeStruct(tops.shape, tops.dtype),
        ],
        compiler_params=params(1, 14),
        name="middle",
    )(place, query, key, value, own, tops)


def finish_kernel(group, rest, shrink, weights, v, out):
    tok = out.shape[0]
    v_t = values_and_ones(v)
    for first in range(0, tok, TILE):
        b = slice(first, first + TILE)
        for h in range(group):
            far = dot(v_t[:, first:], weights[h, first:, b], 1, 0)
            total = rest[head_rows(h), b] + far * shrink[0, h : h + 1, b]
            normal = total[:HEAD_WIDTH] * (1.0 / total[HEAD_WIDTH : HEAD_WIDTH + 1])
            out[b, h * HEAD_WIDTH : (h + 1) * HEAD_WIDTH] = normal.astype(jnp.bfloat16).T


def finish(rest, shrink, weights, value):
    tok, columns = value.shape
    kv_heads = columns // HEAD_WIDTH
    group = weights.shape[0] // kv_heads
    spec = head_specs(tok, kv_heads, group)
    return pl.pallas_call(
        functools.partial(finish_kernel, group),
        grid=(kv_heads,),
        in_specs=[spec["rest"], spec["stat"], spec["weights"], spec["one"]],
        out_specs=spec["queries"],
        out_shape=jax.ShapeDtypeStruct((tok, group * columns), jnp.bfloat16),
        compiler_params=params(1, 14),
        name="finish",
    )(rest, shrink, weights, value)


def shifted(array, steps):
    count = lax.axis_size("seq")
    return lax.ppermute(array, "seq", [(source, source + steps) for source in range(count - steps)])


def exchanged(array, axis, bit):
    count = lax.axis_size(axis)
    return lax.ppermute(array, axis, [(source, source ^ bit) for source in range(count)])


def on_device(
    normed_input, query, key, value, adapter_down_maps, adapter_up_maps, block_adapter_choice
):
    tok = query.shape[0]
    assert 2 * tok == WINDOW and SEG_LEN % tok == 0
    where = lax.axis_index("seq")
    place = where.reshape(1)
    choice = block_adapter_choice

    key_far = shifted(key, 2)
    latent = latent_share(place, choice, normed_input.T, adapter_down_maps)
    bit = 1
    while 2 * bit < lax.axis_size("tp"):
        latent = latent + exchanged(latent, "tp", bit)
        bit *= 2
    theirs = exchanged(latent, "tp", bit)
    value_full = adapt(place, choice, latent, theirs, adapter_up_maps, value)
    value_mid = shifted(value_full, 1)
    key_own, _ = lax.optimization_barrier((key, value_full))
    key_mid = exchanged(jnp.where(where % 2 == 0, key_own, key_far), "seq", 1)
    value_far = shifted(value_full, 2)

    own, weights_far, tops = near_far(place, query, key, value_full, key_far)
    rest, shrink = middle(place, query, key_mid, value_mid, own, tops)
    return finish(rest, shrink, weights_far, value_far)


def solution(mesh):
    placed = (
        P("seq", "tp"),
        P("seq", "tp"),
        P("seq", "tp"),
        P("seq", "tp"),
        P(None, None, "tp"),
        P(None, None, "tp"),
        P(),
    )
    return jax.shard_map(
        on_device, mesh=mesh, in_specs=placed, out_specs=P("seq", "tp"), check_vma=False
    )
```

```python
import functools

import jax
import jax.numpy as jnp
from jax import lax
from jax.experimental import pallas as pl
from jax.experimental.pallas import tpu as pltpu
from jax.sharding import PartitionSpec as P

HEAD_WIDTH = 128
WINDOW = 1024
SEG_LEN = 2048
SCALE = 168.0 ** (-0.5)
LOG2_E = 1.4426950408889634
EXPONENT = SCALE * LOG2_E
MASKED = -1e30
TILE = 256
HALF = 128
ONES = 16
PAIR = 2
PARTS = 1


def params(steps, mib):
    return pltpu.CompilerParams(
        vmem_limit_bytes=mib * 1024 * 1024, dimension_semantics=("arbitrary",) * steps
    )


def dot(left, right, left_dim, right_dim):
    return lax.dot_general(
        left, right, (((left_dim,), (right_dim,)), ((), ())), preferred_element_type=jnp.float32
    )


def in_hbm(array):
    return pltpu.with_memory_space_constraint(array, pltpu.HBM)


def adapter_of(place, choice, tok):
    return choice[lax.div(place[0] * tok, SEG_LEN)]


def latent_kernel(pieces, place, choice, input_t, down, out, rows, map_rows, sems):
    tok = out.shape[1]
    copies = [
        pltpu.make_async_copy(
            down.at[adapter_of(place, choice, tok)], map_rows, sems.at[len(pieces)]
        )
    ]
    for n, (first, last) in enumerate(pieces):
        part = pl.ds(first, last - first)
        copies.append(pltpu.make_async_copy(input_t.at[part], rows.at[part], sems.at[n]))
    for copy in copies:
        copy.start()
    copies[0].wait()
    total = None
    for (first, last), copy in zip(pieces, copies[1:]):
        copy.wait()
        product = dot(map_rows[:, first:last], rows[first:last, :], 1, 0)
        total = product if total is None else total + product
    out[...] = total


def latent_share(place, choice, input_t, down_maps):
    features, tok = input_t.shape
    rank = down_maps.shape[1]
    pieces = [(first, min(first + 512, features)) for first in range(0, features, 512)]
    return pl.pallas_call(
        functools.partial(latent_kernel, pieces),
        grid_spec=pltpu.PrefetchScalarGridSpec(
            num_scalar_prefetch=2,
            grid=(1,),
            in_specs=[
                pl.BlockSpec(memory_space=pltpu.HBM),
                pl.BlockSpec(memory_space=pltpu.HBM),
            ],
            out_specs=pl.BlockSpec((rank, tok), lambda i, *_: (0, 0)),
            scratch_shapes=[
                pltpu.VMEM((features, tok), input_t.dtype),
                pltpu.VMEM((rank, features), down_maps.dtype),
                pltpu.SemaphoreType.DMA((len(pieces) + 1,)),
            ],
        ),
        out_shape=jax.ShapeDtypeStruct((rank, tok), jnp.float32),
        compiler_params=params(1, 8),
        name="latent_share",
    )(place, in_hbm(choice), in_hbm(input_t), in_hbm(down_maps))


def adapt_kernel(place, choice, mine, theirs, up, value, *outs):
    latent = (mine[...] + theirs[...]).astype(jnp.bfloat16)
    update = dot(latent, up[0], 0, 0)
    total = (value[...].astype(jnp.float32) + update).astype(jnp.bfloat16)
    for n, out in enumerate(outs):
        rows = out.shape[0]
        out[...] = total[n * rows : (n + 1) * rows]


def adapt(place, choice, mine, theirs, up_maps, value):
    rank, tok = mine.shape
    columns = value.shape[1]
    whole = lambda i, *_: (0, 0)
    chosen = lambda i, place, choice: (adapter_of(place, choice, tok), 0, 0)
    rows = tok // PARTS
    return pl.pallas_call(
        adapt_kernel,
        grid_spec=pltpu.PrefetchScalarGridSpec(
            num_scalar_prefetch=2,
            grid=(1,),
            in_specs=[
                pl.BlockSpec((rank, tok), whole),
                pl.BlockSpec((rank, tok), whole),
                pl.BlockSpec((1, rank, columns), chosen),
                pl.BlockSpec((tok, columns), whole),
            ],
            out_specs=[pl.BlockSpec((rows, columns), whole)] * PARTS,
        ),
        out_shape=[jax.ShapeDtypeStruct((rows, columns), jnp.bfloat16)] * PARTS,
        compiler_params=params(1, 8),
        name="adapt_values",
    )(place, choice, mine, theirs, up_maps, value)


def weights_of(scores, top):
    return jnp.exp2(((scores - top) * EXPONENT).astype(jnp.bfloat16))


def tree(operation, items):
    items = list(items)
    while len(items) > 1:
        items = [
            operation(items[n], items[n + 1]) if n + 1 < len(items) else items[n]
            for n in range(0, len(items), 2)
        ]
    return items[0]


def top_of(scores):
    pieces = [s[n : n + 32] for s in scores for n in range(0, s.shape[0], 32)]
    pieces = tree(jnp.maximum, pieces)
    pieces = tree(jnp.maximum, [pieces[n : n + 8] for n in range(0, 32, 8)])
    return jnp.max(pieces, axis=0, keepdims=True)


def tile(parts, j, columns):
    rows = parts[0].shape[0]
    first = j * TILE % rows
    return parts[j * TILE // rows][first : first + TILE, columns]


def values_and_ones(parts, columns):
    turned = [p[:, columns].T for p in parts]
    tok = sum(p.shape[0] for p in parts)
    turned = turned[0] if len(turned) == 1 else jnp.concatenate(turned, axis=1)
    return jnp.concatenate([turned, jnp.ones((ONES, tok), jnp.bfloat16)], axis=0)


def head_rows(h):
    return slice(h * (HEAD_WIDTH + ONES), (h + 1) * (HEAD_WIDTH + ONES))


def head_columns(h):
    return slice(h * HEAD_WIDTH, (h + 1) * HEAD_WIDTH)


def in_steps(units, stages):
    held = [None] * len(units)
    for step in range(len(units) + len(stages) - 1):
        for n, stage in enumerate(stages):
            if 0 <= step - n < len(units):
                held[step - n] = stage(units[step - n], held[step - n])


def units_of(group, tok):
    return [(h, i) for g in range(PAIR) for i in range(tok // TILE) for h in range(g * group, (g + 1) * group)]


def near_far_kernel(group, place, q, k, *refs):
    v, k_far, (out, weights_far, tops) = refs[:PARTS], refs[PARTS : 2 * PARTS], refs[2 * PARTS :]
    far_there = place[0] >= 2
    tok = q.shape[0]
    causal = lax.broadcasted_iota(jnp.int32, (HALF, HALF), 0) <= lax.broadcasted_iota(
        jnp.int32, (HALF, HALF), 1
    )
    v_t = [values_and_ones(v, head_columns(g)) for g in range(PAIR)]
    nothing = jnp.zeros((HALF, HALF), jnp.bfloat16)
    tiles = tok // TILE
    blocks = [slice(i * TILE, (i + 1) * TILE) for i in range(tiles)]

    def score(unit, _):
        h, i = unit
        qh = q[blocks[i], head_columns(h)]
        columns = head_columns(h // group)
        near = [dot(k[blocks[j], columns], qh, 1, 1) for j in range(i + 1)]
        far = [dot(tile(k_far, j, columns), qh, 1, 1) for j in range(i, tiles)]
        return near, far

    def weigh(unit, scores):
        h, i = unit
        near, far = scores
        near_columns, far_columns = [], []
        for half in range(2):
            a = slice(half * HALF, (half + 1) * HALF)
            near_edge = near[i][: (half + 1) * HALF, a]
            far_edge = far[0][half * HALF :, a]
            near_pieces = [s[:, a] for s in near[:i]]
            if half == 1:
                near_pieces.append(near_edge[:HALF])
            near_pieces.append(jnp.where(causal, near_edge[half * HALF :], MASKED))
            far_pieces = [jnp.where(causal, MASKED, far_edge[:HALF])]
            if half == 0:
                far_pieces.append(far_edge[HALF:])
            far_pieces += [s[:, a] for s in far[1:]]
            top = jnp.maximum(
                top_of(near_pieces), jnp.where(far_there, top_of(far_pieces), MASKED)
            )
            far_top = jnp.where(far_there, top, -MASKED)
            near_weights = [weights_of(s, top) for s in near_pieces]
            far_weights = [weights_of(s, far_top) for s in far_pieces]
            if half == 0:
                near_weights.append(nothing)
            else:
                far_weights.insert(0, nothing)
            near_columns.append(jnp.concatenate(near_weights, axis=0))
            far_columns.append(jnp.concatenate(far_weights, axis=0))
            queries = slice(i * TILE + half * HALF, i * TILE + (half + 1) * HALF)
            tops[0, h : h + 1, queries] = top
        weights_far[h, i * TILE :, blocks[i]] = jnp.concatenate(far_columns, axis=1)
        return jnp.concatenate(near_columns, axis=1)

    def multiply(unit, weights):
        h, i = unit
        out[head_rows(h), blocks[i]] = dot(v_t[h // group][:, : (i + 1) * TILE], weights, 1, 0)

    in_steps(units_of(group, tok), [score, weigh, multiply])


def middle_kernel(group, place, q, own, weights_far, tops, *refs):
    k, v_far, (rest, weights, shrink) = refs[:PARTS], refs[PARTS : 2 * PARTS], refs[2 * PARTS :]
    there = place[0] >= 1
    tok = q.shape[0]
    v_t = [values_and_ones(v_far, head_columns(g)) for g in range(PAIR)]
    tiles = tok // TILE
    blocks = [slice(i * TILE, (i + 1) * TILE) for i in range(tiles)]

    def score(unit, _):
        h, i = unit
        qh = q[blocks[i], head_columns(h)]
        return [dot(tile(k, j, head_columns(h // group)), qh, 1, 1) for j in range(tiles)]

    def weigh(unit, scores):
        h, i = unit
        before = tops[0, h : h + 1, blocks[i]]
        top = jnp.maximum(before, jnp.where(there, top_of(scores), MASKED))
        less = jnp.exp2((before - top) * EXPONENT)
        top = jnp.where(there, top, -MASKED)
        for j, s in enumerate(scores):
            weights[h, blocks[j], blocks[i]] = weights_of(s, top)
        shrink[0, h : h + 1, blocks[i]] = less
        return less

    def multiply(unit, less):
        h, i = unit
        far = dot(v_t[h // group][:, i * TILE :], weights_far[h, i * TILE :, blocks[i]], 1, 0)
        rest[head_rows(h), blocks[i]] = (own[head_rows(h), blocks[i]] + far) * less

    in_steps(units_of(group, tok), [score, weigh, multiply])


def finish_kernel(group, rest, weights, *refs):
    v, (out,) = refs[:PARTS], refs[PARTS:]
    tok = out.shape[0]
    v_t = [values_and_ones(v, head_columns(g)) for g in range(PAIR)]
    blocks = [slice(first, first + TILE) for first in range(0, tok, TILE)]

    def multiply(unit, _):
        h, i = unit
        return dot(v_t[h // group], weights[h, :, blocks[i]], 1, 0)

    def normalise(unit, middle):
        h, i = unit
        total = rest[head_rows(h), blocks[i]] + middle
        normal = total[:HEAD_WIDTH] * (1.0 / total[HEAD_WIDTH : HEAD_WIDTH + 1])
        out[blocks[i], head_columns(h)] = normal.astype(jnp.bfloat16).T

    in_steps(units_of(group, tok), [multiply, normalise])


def by_heads(kernel, name, query_shape, columns, place, arrays, kinds, out_kinds):
    tok, width = query_shape
    kv_heads = columns // HEAD_WIDTH
    group = width // columns
    grid = kv_heads // PAIR
    rows = tok // PARTS
    depth = HEAD_WIDTH + ONES
    heads = width // HEAD_WIDTH
    step = heads // grid
    specs = dict(
        queries=((tok, width), (tok, width // grid), lambda g, *_: (0, g), jnp.bfloat16),
        one=((tok, columns), (tok, columns // grid), lambda g, *_: (0, g), jnp.bfloat16),
        part=((rows, columns), (rows, columns // grid), lambda g, *_: (0, g), jnp.bfloat16),
        rest=((heads * depth, tok), (step * depth, tok), lambda g, *_: (g, 0), jnp.float32),
        weights=((heads, tok, tok), (step, tok, tok), lambda g, *_: (g, 0, 0), jnp.bfloat16),
        stat=((grid, 8, tok), (1, 8, tok), lambda g, *_: (g, 0, 0), jnp.float32),
    )
    block = lambda kind: pl.BlockSpec(specs[kind][1], specs[kind][2])
    return pl.pallas_call(
        functools.partial(kernel, group),
        grid_spec=pltpu.PrefetchScalarGridSpec(
            num_scalar_prefetch=len(place),
            grid=(grid,),
            in_specs=[block(kind) for kind in kinds],
            out_specs=[block(kind) for kind in out_kinds],
        ),
        out_shape=[jax.ShapeDtypeStruct(specs[kind][0], specs[kind][3]) for kind in out_kinds],
        compiler_params=params(1, 24),
        name=name,
    )(*place, *arrays)


def shifted(array, steps):
    count = lax.axis_size("seq")
    return lax.ppermute(array, "seq", [(source, source + steps) for source in range(count - steps)])


def exchanged(array, axis, bit):
    count = lax.axis_size(axis)
    return lax.ppermute(array, axis, [(source, source ^ bit) for source in range(count)])


def on_device(
    normed_input, query, key, value, adapter_down_maps, adapter_up_maps, block_adapter_choice
):
    tok = query.shape[0]
    assert 2 * tok == WINDOW and SEG_LEN % tok == 0
    where = lax.axis_index("seq")
    place = where.reshape(1)
    choice = block_adapter_choice

    rows = tok // PARTS
    key_parts = [key[n * rows : (n + 1) * rows] for n in range(PARTS)] if PARTS > 1 else [key]
    key_far = [shifted(part, 2) for part in key_parts]
    latent = latent_share(place, choice, normed_input.T, adapter_down_maps)
    bit = 1
    while 2 * bit < lax.axis_size("tp"):
        latent = latent + exchanged(latent, "tp", bit)
        bit *= 2
    theirs = exchanged(latent, "tp", bit)
    values = adapt(place, choice, latent, theirs, adapter_up_maps, value)
    value_far = [shifted(part, 2) for part in values]

    def from_one_back(own, far):
        return [
            exchanged(jnp.where(where % 2 == 0, mine, theirs), "seq", 1)
            for mine, theirs in zip(own, far)
        ]

    call = functools.partial(by_heads, query_shape=query.shape, columns=key.shape[1])
    key_own, _ = lax.optimization_barrier((key_parts, values))
    key_mid = from_one_back(key_own, key_far)
    own, weights_far, tops = call(
        near_far_kernel,
        "near_far",
        place=[place],
        arrays=[query, key, *values, *key_far],
        kinds=["queries", "one"] + ["part"] * (2 * PARTS),
        out_kinds=["rest", "weights", "stat"],
    )
    values, own = lax.optimization_barrier((values, own))
    value_mid = from_one_back(values, value_far)
    rest, weights_mid, _ = call(
        middle_kernel,
        "middle",
        place=[place],
        arrays=[query, own, weights_far, tops, *key_mid, *value_far],
        kinds=["queries", "rest", "weights", "stat"] + ["part"] * (2 * PARTS),
        out_kinds=["rest", "weights", "stat"],
    )
    return call(
        finish_kernel,
        "finish",
        place=[],
        arrays=[rest, weights_mid, *value_mid],
        kinds=["rest", "weights"] + ["part"] * PARTS,
        out_kinds=["queries"],
    )[0]


def solution(mesh):
    placed = (
        P("seq", "tp"),
        P("seq", "tp"),
        P("seq", "tp"),
        P("seq", "tp"),
        P(None, None, "tp"),
        P(None, None, "tp"),
        P(),
    )
    return jax.shard_map(
        on_device, mesh=mesh, in_specs=placed, out_specs=P("seq", "tp"), check_vma=False
    )
```

```python
import functools

import jax
import jax.numpy as jnp
from jax import lax
from jax.experimental import pallas as pl
from jax.experimental.pallas import tpu as pltpu
from jax.sharding import PartitionSpec as P

HEAD_WIDTH = 128
WINDOW = 1024
SEG_LEN = 2048
SCALE = 168.0 ** (-0.5)
LOG2_E = 1.4426950408889634
EXPONENT = SCALE * LOG2_E
MASKED = -1e30
TILE = 256
HALF = 128
ONES = 16
PAIR = 2
PARTS = 2


def params(steps, mib):
    return pltpu.CompilerParams(
        vmem_limit_bytes=mib * 1024 * 1024, dimension_semantics=("arbitrary",) * steps
    )


def dot(left, right, left_dim, right_dim):
    return lax.dot_general(
        left, right, (((left_dim,), (right_dim,)), ((), ())), preferred_element_type=jnp.float32
    )


def in_hbm(array):
    return pltpu.with_memory_space_constraint(array, pltpu.HBM)


def adapter_of(place, choice, tok):
    return choice[lax.div(place[0] * tok, SEG_LEN)]


def latent_kernel(place, choice, input_t, down, out):
    out[...] = dot(down[0], input_t[...], 1, 0)


def latent_share(place, choice, input_t, down_maps):
    features, tok = input_t.shape
    rank = down_maps.shape[1]
    whole = lambda i, *_: (0, 0)
    chosen = lambda i, place, choice: (adapter_of(place, choice, tok), 0, 0)
    return pl.pallas_call(
        latent_kernel,
        grid_spec=pltpu.PrefetchScalarGridSpec(
            num_scalar_prefetch=2,
            grid=(1,),
            in_specs=[
                pl.BlockSpec((features, tok), whole),
                pl.BlockSpec((1, rank, features), chosen),
            ],
            out_specs=pl.BlockSpec((rank, tok), whole),
        ),
        out_shape=jax.ShapeDtypeStruct((rank, tok), jnp.float32),
        compiler_params=params(1, 8),
        name="latent_share",
    )(place, in_hbm(choice), input_t, in_hbm(down_maps))


def adapt_kernel(place, choice, mine, theirs, up, value, *outs):
    latent = (mine[...] + theirs[...]).astype(jnp.bfloat16)
    update = dot(latent, up[0], 0, 0)
    total = (value[...].astype(jnp.float32) + update).astype(jnp.bfloat16)
    for n, out in enumerate(outs):
        rows = out.shape[0]
        out[...] = total[n * rows : (n + 1) * rows]


def adapt(place, choice, mine, theirs, up_maps, value):
    rank, tok = mine.shape
    columns = value.shape[1]
    whole = lambda i, *_: (0, 0)
    chosen = lambda i, place, choice: (adapter_of(place, choice, tok), 0, 0)
    rows = tok // PARTS
    return pl.pallas_call(
        adapt_kernel,
        grid_spec=pltpu.PrefetchScalarGridSpec(
            num_scalar_prefetch=2,
            grid=(1,),
            in_specs=[
                pl.BlockSpec((rank, tok), whole),
                pl.BlockSpec((rank, tok), whole),
                pl.BlockSpec((1, rank, columns), chosen),
                pl.BlockSpec((tok, columns), whole),
            ],
            out_specs=[pl.BlockSpec((rows, columns), whole)] * PARTS,
        ),
        out_shape=[jax.ShapeDtypeStruct((rows, columns), jnp.bfloat16)] * PARTS,
        compiler_params=params(1, 8),
        name="adapt_values",
    )(place, choice, mine, theirs, up_maps, value)


def weights_of(scores, top):
    return jnp.exp2(((scores - top) * EXPONENT).astype(jnp.bfloat16))


def tree(operation, items):
    items = list(items)
    while len(items) > 1:
        items = [
            operation(items[n], items[n + 1]) if n + 1 < len(items) else items[n]
            for n in range(0, len(items), 2)
        ]
    return items[0]


def top_of(scores):
    pieces = [s[n : n + 32] for s in scores for n in range(0, s.shape[0], 32)]
    pieces = tree(jnp.maximum, pieces)
    pieces = tree(jnp.maximum, [pieces[n : n + 8] for n in range(0, 32, 8)])
    return jnp.max(pieces, axis=0, keepdims=True)


def tile(parts, j, columns):
    rows = parts[0].shape[0]
    first = j * TILE % rows
    return parts[j * TILE // rows][first : first + TILE, columns]


def values_and_ones(parts, columns):
    turned = [p[:, columns].T for p in parts]
    tok = sum(p.shape[0] for p in parts)
    turned = turned[0] if len(turned) == 1 else jnp.concatenate(turned, axis=1)
    return jnp.concatenate([turned, jnp.ones((ONES, tok), jnp.bfloat16)], axis=0)


def head_rows(h):
    return slice(h * (HEAD_WIDTH + ONES), (h + 1) * (HEAD_WIDTH + ONES))


def head_columns(h):
    return slice(h * HEAD_WIDTH, (h + 1) * HEAD_WIDTH)


def in_steps(units, stages):
    held = [None] * len(units)
    for step in range(len(units) + len(stages) - 1):
        for n, stage in enumerate(stages):
            if 0 <= step - n < len(units):
                held[step - n] = stage(units[step - n], held[step - n])


def units_of(group, tok):
    return [(h, i) for g in range(PAIR) for i in range(tok // TILE) for h in range(g * group, (g + 1) * group)]


def near_far_kernel(group, place, q, k, *refs):
    v, k_far, (out, weights_far, tops) = refs[:PARTS], refs[PARTS : 2 * PARTS], refs[2 * PARTS :]
    far_there = place[0] >= 2
    tok = q.shape[0]
    causal = lax.broadcasted_iota(jnp.int32, (HALF, HALF), 0) <= lax.broadcasted_iota(
        jnp.int32, (HALF, HALF), 1
    )
    v_t = [values_and_ones(v, head_columns(g)) for g in range(PAIR)]
    nothing = jnp.zeros((HALF, HALF), jnp.bfloat16)
    tiles = tok // TILE
    blocks = [slice(i * TILE, (i + 1) * TILE) for i in range(tiles)]

    def score(unit, _):
        h, i = unit
        qh = q[blocks[i], head_columns(h)]
        columns = head_columns(h // group)
        near = [dot(k[blocks[j], columns], qh, 1, 1) for j in range(i + 1)]
        far = [dot(tile(k_far, j, columns), qh, 1, 1) for j in range(i, tiles)]
        return near, far

    def weigh(unit, scores):
        h, i = unit
        near, far = scores
        near_columns, far_columns = [], []
        for half in range(2):
            a = slice(half * HALF, (half + 1) * HALF)
            near_edge = near[i][: (half + 1) * HALF, a]
            far_edge = far[0][half * HALF :, a]
            near_pieces = [s[:, a] for s in near[:i]]
            if half == 1:
                near_pieces.append(near_edge[:HALF])
            near_pieces.append(jnp.where(causal, near_edge[half * HALF :], MASKED))
            far_pieces = [jnp.where(causal, MASKED, far_edge[:HALF])]
            if half == 0:
                far_pieces.append(far_edge[HALF:])
            far_pieces += [s[:, a] for s in far[1:]]
            top = jnp.maximum(
                top_of(near_pieces), jnp.where(far_there, top_of(far_pieces), MASKED)
            )
            far_top = jnp.where(far_there, top, -MASKED)
            near_weights = [weights_of(s, top) for s in near_pieces]
            far_weights = [weights_of(s, far_top) for s in far_pieces]
            if half == 0:
                near_weights.append(nothing)
            else:
                far_weights.insert(0, nothing)
            near_columns.append(jnp.concatenate(near_weights, axis=0))
            far_columns.append(jnp.concatenate(far_weights, axis=0))
            queries = slice(i * TILE + half * HALF, i * TILE + (half + 1) * HALF)
            tops[0, h : h + 1, queries] = top
        weights_far[h, i * TILE :, blocks[i]] = jnp.concatenate(far_columns, axis=1)
        return jnp.concatenate(near_columns, axis=1)

    def multiply(unit, weights):
        h, i = unit
        out[head_rows(h), blocks[i]] = dot(v_t[h // group][:, : (i + 1) * TILE], weights, 1, 0)

    in_steps(units_of(group, tok), [score, weigh, multiply])


def middle_kernel(group, place, q, own, weights_far, tops, *refs):
    k, v_far, (rest, weights, shrink) = refs[:PARTS], refs[PARTS : 2 * PARTS], refs[2 * PARTS :]
    there = place[0] >= 1
    tok = q.shape[0]
    v_t = [values_and_ones(v_far, head_columns(g)) for g in range(PAIR)]
    tiles = tok // TILE
    blocks = [slice(i * TILE, (i + 1) * TILE) for i in range(tiles)]

    def score(unit, _):
        h, i = unit
        qh = q[blocks[i], head_columns(h)]
        return [dot(tile(k, j, head_columns(h // group)), qh, 1, 1) for j in range(tiles)]

    def weigh(unit, scores):
        h, i = unit
        before = tops[0, h : h + 1, blocks[i]]
        top = jnp.maximum(before, jnp.where(there, top_of(scores), MASKED))
        less = jnp.exp2((before - top) * EXPONENT)
        top = jnp.where(there, top, -MASKED)
        for j, s in enumerate(scores):
            weights[h, blocks[j], blocks[i]] = weights_of(s, top)
        shrink[0, h : h + 1, blocks[i]] = less
        return less

    def multiply(unit, less):
        h, i = unit
        far = dot(v_t[h // group][:, i * TILE :], weights_far[h, i * TILE :, blocks[i]], 1, 0)
        rest[head_rows(h), blocks[i]] = (own[head_rows(h), blocks[i]] + far) * less

    in_steps(units_of(group, tok), [score, weigh, multiply])


def finish_kernel(group, rest, weights, *refs):
    v, (out,) = refs[:PARTS], refs[PARTS:]
    tok = out.shape[0]
    v_t = [values_and_ones(v, head_columns(g)) for g in range(PAIR)]
    blocks = [slice(first, first + TILE) for first in range(0, tok, TILE)]

    def multiply(unit, _):
        h, i = unit
        return dot(v_t[h // group], weights[h, :, blocks[i]], 1, 0)

    def normalise(unit, middle):
        h, i = unit
        total = rest[head_rows(h), blocks[i]] + middle
        normal = total[:HEAD_WIDTH] * (1.0 / total[HEAD_WIDTH : HEAD_WIDTH + 1])
        out[blocks[i], head_columns(h)] = normal.astype(jnp.bfloat16).T

    in_steps(units_of(group, tok), [multiply, normalise])


def by_heads(kernel, name, query_shape, columns, place, arrays, kinds, out_kinds):
    tok, width = query_shape
    kv_heads = columns // HEAD_WIDTH
    group = width // columns
    grid = kv_heads // PAIR
    rows = tok // PARTS
    depth = HEAD_WIDTH + ONES
    heads = width // HEAD_WIDTH
    step = heads // grid
    specs = dict(
        queries=((tok, width), (tok, width // grid), lambda g, *_: (0, g), jnp.bfloat16),
        one=((tok, columns), (tok, columns // grid), lambda g, *_: (0, g), jnp.bfloat16),
        part=((rows, columns), (rows, columns // grid), lambda g, *_: (0, g), jnp.bfloat16),
        rest=((heads * depth, tok), (step * depth, tok), lambda g, *_: (g, 0), jnp.float32),
        weights=((heads, tok, tok), (step, tok, tok), lambda g, *_: (g, 0, 0), jnp.bfloat16),
        stat=((grid, 8, tok), (1, 8, tok), lambda g, *_: (g, 0, 0), jnp.float32),
    )
    block = lambda kind: pl.BlockSpec(specs[kind][1], specs[kind][2])
    return pl.pallas_call(
        functools.partial(kernel, group),
        grid_spec=pltpu.PrefetchScalarGridSpec(
            num_scalar_prefetch=len(place),
            grid=(grid,),
            in_specs=[block(kind) for kind in kinds],
            out_specs=[block(kind) for kind in out_kinds],
        ),
        out_shape=[jax.ShapeDtypeStruct(specs[kind][0], specs[kind][3]) for kind in out_kinds],
        compiler_params=params(1, 24),
        name=name,
    )(*place, *arrays)


def shifted(array, steps):
    count = lax.axis_size("seq")
    return lax.ppermute(array, "seq", [(source, source + steps) for source in range(count - steps)])


def exchanged(array, axis, bit):
    count = lax.axis_size(axis)
    return lax.ppermute(array, axis, [(source, source ^ bit) for source in range(count)])


def on_device(
    normed_input, query, key, value, adapter_down_maps, adapter_up_maps, block_adapter_choice
):
    tok = query.shape[0]
    assert 2 * tok == WINDOW and SEG_LEN % tok == 0
    where = lax.axis_index("seq")
    place = where.reshape(1)
    choice = block_adapter_choice

    rows = tok // PARTS
    key_parts = [key[n * rows : (n + 1) * rows] for n in range(PARTS)] if PARTS > 1 else [key]
    key_far = [shifted(key_parts[0], 2)]
    latent = latent_share(place, choice, normed_input.T, adapter_down_maps)
    bit = 1
    while 2 * bit < lax.axis_size("tp"):
        latent = latent + exchanged(latent, "tp", bit)
        bit *= 2
    key_parts, latent = lax.optimization_barrier((key_parts, latent))
    key_far += [shifted(part, 2) for part in key_parts[1:]]
    theirs = exchanged(latent, "tp", bit)
    values = adapt(place, choice, latent, theirs, adapter_up_maps, value)
    value_far = [shifted(part, 2) for part in values]

    def from_one_back(own, far):
        return [
            exchanged(jnp.where(where % 2 == 0, mine, theirs), "seq", 1)
            for mine, theirs in zip(own, far)
        ]

    call = functools.partial(by_heads, query_shape=query.shape, columns=key.shape[1])
    key_late, _ = lax.optimization_barrier((key_parts[1:], values))
    key_mid = from_one_back(key_parts[:1] + key_late, key_far)
    values, key_mid[0] = lax.optimization_barrier((values, key_mid[0]))
    own, weights_far, tops = call(
        near_far_kernel,
        "near_far",
        place=[place],
        arrays=[query, key, *values, *key_far],
        kinds=["queries", "one"] + ["part"] * (2 * PARTS),
        out_kinds=["rest", "weights", "stat"],
    )
    values, own = lax.optimization_barrier((values, own))
    value_mid = from_one_back(values, value_far)
    rest, weights_mid, _ = call(
        middle_kernel,
        "middle",
        place=[place],
        arrays=[query, own, weights_far, tops, *key_mid, *value_far],
        kinds=["queries", "rest", "weights", "stat"] + ["part"] * (2 * PARTS),
        out_kinds=["rest", "weights", "stat"],
    )
    return call(
        finish_kernel,
        "finish",
        place=[],
        arrays=[rest, weights_mid, *value_mid],
        kinds=["rest", "weights"] + ["part"] * PARTS,
        out_kinds=["queries"],
    )[0]


def solution(mesh):
    placed = (
        P("seq", "tp"),
        P("seq", "tp"),
        P("seq", "tp"),
        P("seq", "tp"),
        P(None, None, "tp"),
        P(None, None, "tp"),
        P(),
    )
    return jax.shard_map(
        on_device, mesh=mesh, in_specs=placed, out_specs=P("seq", "tp"), check_vma=False
    )
```

```python
import functools

import jax
import jax.numpy as jnp
from jax import lax
from jax.experimental import pallas as pl
from jax.experimental.pallas import tpu as pltpu
from jax.sharding import PartitionSpec as P

HEAD_WIDTH = 128
WINDOW = 1024
SEG_LEN = 2048
SCALE = 168.0 ** (-0.5)
LOG2_E = 1.4426950408889634
EXPONENT = SCALE * LOG2_E
MASKED = -1e30
TILE = 256
HALF = 128
ONES = 16
PAIR = 2
PARTS = 1


def params(steps, mib):
    return pltpu.CompilerParams(
        vmem_limit_bytes=mib * 1024 * 1024, dimension_semantics=("arbitrary",) * steps
    )


def dot(left, right, left_dim, right_dim):
    return lax.dot_general(
        left, right, (((left_dim,), (right_dim,)), ((), ())), preferred_element_type=jnp.float32
    )


def in_hbm(array):
    return pltpu.with_memory_space_constraint(array, pltpu.HBM)


def adapter_of(place, choice, tok):
    return choice[lax.div(place[0] * tok, SEG_LEN)]


def latent_kernel(pieces, place, choice, input_t, down, out, rows, map_rows, sems):
    tok = out.shape[1]
    copies = [
        pltpu.make_async_copy(
            down.at[adapter_of(place, choice, tok)], map_rows, sems.at[len(pieces)]
        )
    ]
    for n, (first, last) in enumerate(pieces):
        part = pl.ds(first, last - first)
        copies.append(pltpu.make_async_copy(input_t.at[part], rows.at[part], sems.at[n]))
    for copy in copies:
        copy.start()
    copies[0].wait()
    total = None
    for (first, last), copy in zip(pieces, copies[1:]):
        copy.wait()
        product = dot(map_rows[:, first:last], rows[first:last, :], 1, 0)
        total = product if total is None else total + product
    out[...] = total


def latent_share(place, choice, input_t, down_maps):
    features, tok = input_t.shape
    rank = down_maps.shape[1]
    pieces = [(first, min(first + 512, features)) for first in range(0, features, 512)]
    return pl.pallas_call(
        functools.partial(latent_kernel, pieces),
        grid_spec=pltpu.PrefetchScalarGridSpec(
            num_scalar_prefetch=2,
            grid=(1,),
            in_specs=[
                pl.BlockSpec(memory_space=pltpu.HBM),
                pl.BlockSpec(memory_space=pltpu.HBM),
            ],
            out_specs=pl.BlockSpec((rank, tok), lambda i, *_: (0, 0)),
            scratch_shapes=[
                pltpu.VMEM((features, tok), input_t.dtype),
                pltpu.VMEM((rank, features), down_maps.dtype),
                pltpu.SemaphoreType.DMA((len(pieces) + 1,)),
            ],
        ),
        out_shape=jax.ShapeDtypeStruct((rank, tok), jnp.float32),
        compiler_params=params(1, 8),
        name="latent_share",
    )(place, in_hbm(choice), in_hbm(input_t), in_hbm(down_maps))


def adapt_kernel(place, choice, mine, theirs, up, value, *outs):
    latent = (mine[...] + theirs[...]).astype(jnp.bfloat16)
    update = dot(latent, up[0], 0, 0)
    total = (value[...].astype(jnp.float32) + update).astype(jnp.bfloat16)
    for n, out in enumerate(outs):
        rows = out.shape[0]
        out[...] = total[n * rows : (n + 1) * rows]


def adapt(place, choice, mine, theirs, up_maps, value):
    rank, tok = mine.shape
    columns = value.shape[1]
    whole = lambda i, *_: (0, 0)
    chosen = lambda i, place, choice: (adapter_of(place, choice, tok), 0, 0)
    rows = tok // PARTS
    return pl.pallas_call(
        adapt_kernel,
        grid_spec=pltpu.PrefetchScalarGridSpec(
            num_scalar_prefetch=2,
            grid=(1,),
            in_specs=[
                pl.BlockSpec((rank, tok), whole),
                pl.BlockSpec((rank, tok), whole),
                pl.BlockSpec((1, rank, columns), chosen),
                pl.BlockSpec((tok, columns), whole),
            ],
            out_specs=[pl.BlockSpec((rows, columns), whole)] * PARTS,
        ),
        out_shape=[jax.ShapeDtypeStruct((rows, columns), jnp.bfloat16)] * PARTS,
        compiler_params=params(1, 8),
        name="adapt_values",
    )(place, choice, mine, theirs, up_maps, value)


def weights_of(scores, top):
    return jnp.exp2(((scores - top) * EXPONENT).astype(jnp.bfloat16))


def tree(operation, items):
    items = list(items)
    while len(items) > 1:
        items = [
            operation(items[n], items[n + 1]) if n + 1 < len(items) else items[n]
            for n in range(0, len(items), 2)
        ]
    return items[0]


def top_of(scores):
    pieces = [s[n : n + 32] for s in scores for n in range(0, s.shape[0], 32)]
    pieces = tree(jnp.maximum, pieces)
    pieces = tree(jnp.maximum, [pieces[n : n + 8] for n in range(0, 32, 8)])
    return jnp.max(pieces, axis=0, keepdims=True)


def tile(parts, j, columns):
    rows = parts[0].shape[0]
    first = j * TILE % rows
    return parts[j * TILE // rows][first : first + TILE, columns]


def values_and_ones(parts, columns):
    turned = [p[:, columns].T for p in parts]
    tok = sum(p.shape[0] for p in parts)
    turned = turned[0] if len(turned) == 1 else jnp.concatenate(turned, axis=1)
    return jnp.concatenate([turned, jnp.ones((ONES, tok), jnp.bfloat16)], axis=0)


def head_rows(h):
    return slice(h * (HEAD_WIDTH + ONES), (h + 1) * (HEAD_WIDTH + ONES))


def head_columns(h):
    return slice(h * HEAD_WIDTH, (h + 1) * HEAD_WIDTH)


def in_steps(units, stages):
    held = [None] * len(units)
    for step in range(len(units) + len(stages) - 1):
        for n, stage in enumerate(stages):
            if 0 <= step - n < len(units):
                held[step - n] = stage(units[step - n], held[step - n])


def units_of(group, tok):
    return [(h, i) for g in range(PAIR) for i in range(tok // TILE) for h in range(g * group, (g + 1) * group)]


def near_far_kernel(group, place, q, k, *refs):
    v, k_far, (out, weights_far, tops) = refs[:PARTS], refs[PARTS : 2 * PARTS], refs[2 * PARTS :]
    far_there = place[0] >= 2
    tok = q.shape[0]
    causal = lax.broadcasted_iota(jnp.int32, (HALF, HALF), 0) <= lax.broadcasted_iota(
        jnp.int32, (HALF, HALF), 1
    )
    v_t = [values_and_ones(v, head_columns(g)) for g in range(PAIR)]
    nothing = jnp.zeros((HALF, HALF), jnp.bfloat16)
    tiles = tok // TILE
    blocks = [slice(i * TILE, (i + 1) * TILE) for i in range(tiles)]

    def score(unit, _):
        h, i = unit
        qh = q[blocks[i], head_columns(h)]
        columns = head_columns(h // group)
        near = [dot(k[blocks[j], columns], qh, 1, 1) for j in range(i + 1)]
        far = [dot(tile(k_far, j, columns), qh, 1, 1) for j in range(i, tiles)]
        return near, far

    def weigh(unit, scores):
        h, i = unit
        near, far = scores
        near_columns, far_columns = [], []
        for half in range(2):
            a = slice(half * HALF, (half + 1) * HALF)
            near_edge = near[i][: (half + 1) * HALF, a]
            far_edge = far[0][half * HALF :, a]
            near_pieces = [s[:, a] for s in near[:i]]
            if half == 1:
                near_pieces.append(near_edge[:HALF])
            near_pieces.append(jnp.where(causal, near_edge[half * HALF :], MASKED))
            far_pieces = [jnp.where(causal, MASKED, far_edge[:HALF])]
            if half == 0:
                far_pieces.append(far_edge[HALF:])
            far_pieces += [s[:, a] for s in far[1:]]
            top = jnp.maximum(
                top_of(near_pieces), jnp.where(far_there, top_of(far_pieces), MASKED)
            )
            far_top = jnp.where(far_there, top, -MASKED)
            near_weights = [weights_of(s, top) for s in near_pieces]
            far_weights = [weights_of(s, far_top) for s in far_pieces]
            if half == 0:
                near_weights.append(nothing)
            else:
                far_weights.insert(0, nothing)
            near_columns.append(jnp.concatenate(near_weights, axis=0))
            far_columns.append(jnp.concatenate(far_weights, axis=0))
            queries = slice(i * TILE + half * HALF, i * TILE + (half + 1) * HALF)
            tops[0, h : h + 1, queries] = top
        weights_far[h, i * TILE :, blocks[i]] = jnp.concatenate(far_columns, axis=1)
        return jnp.concatenate(near_columns, axis=1)

    def multiply(unit, weights):
        h, i = unit
        out[head_rows(h), blocks[i]] = dot(v_t[h // group][:, : (i + 1) * TILE], weights, 1, 0)

    in_steps(units_of(group, tok), [score, weigh, multiply])


def middle_kernel(group, place, q, own, weights_far, tops, *refs):
    k, v_far, (rest, weights, shrink) = refs[:PARTS], refs[PARTS : 2 * PARTS], refs[2 * PARTS :]
    there = place[0] >= 1
    tok = q.shape[0]
    v_t = [values_and_ones(v_far, head_columns(g)) for g in range(PAIR)]
    tiles = tok // TILE
    blocks = [slice(i * TILE, (i + 1) * TILE) for i in range(tiles)]

    def score(unit, _):
        h, i = unit
        qh = q[blocks[i], head_columns(h)]
        return [dot(tile(k, j, head_columns(h // group)), qh, 1, 1) for j in range(tiles)]

    def weigh(unit, scores):
        h, i = unit
        before = tops[0, h : h + 1, blocks[i]]
        top = jnp.maximum(before, jnp.where(there, top_of(scores), MASKED))
        less = jnp.exp2((before - top) * EXPONENT)
        top = jnp.where(there, top, -MASKED)
        for j, s in enumerate(scores):
            weights[h, blocks[j], blocks[i]] = weights_of(s, top)
        shrink[0, h : h + 1, blocks[i]] = less
        return less

    def multiply(unit, less):
        h, i = unit
        far = dot(v_t[h // group][:, i * TILE :], weights_far[h, i * TILE :, blocks[i]], 1, 0)
        rest[head_rows(h), blocks[i]] = (own[head_rows(h), blocks[i]] + far) * less

    in_steps(units_of(group, tok), [score, weigh, multiply])


def finish_kernel(group, place, rest, weights, *refs):
    v, (out,) = refs[:PARTS], refs[PARTS:]
    tok = out.shape[0]
    v_t = [values_and_ones(v, head_columns(g)) for g in range(PAIR)]
    blocks = [slice(first, first + TILE) for first in range(0, tok, TILE)]

    def multiply(unit, _):
        h, i = unit
        return dot(v_t[h // group], weights[h, :, blocks[i]], 1, 0)

    def normalise(unit, middle):
        h, i = unit
        total = rest[head_rows(h), blocks[i]] + middle
        normal = total[:HEAD_WIDTH] * (1.0 / total[HEAD_WIDTH : HEAD_WIDTH + 1])
        out[blocks[i], head_columns(h)] = normal.astype(jnp.bfloat16).T

    in_steps(units_of(group, tok), [multiply, normalise])


def by_heads(kernel, name, query_shape, columns, place, arrays, kinds, out_kinds):
    tok, width = query_shape
    kv_heads = columns // HEAD_WIDTH
    group = width // columns
    grid = kv_heads // PAIR
    rows = tok // PARTS
    depth = HEAD_WIDTH + ONES
    heads = width // HEAD_WIDTH
    step = heads // grid
    specs = dict(
        queries=((tok, width), (tok, width // grid), lambda g, *_: (0, g), jnp.bfloat16),
        one=((tok, columns), (tok, columns // grid), lambda g, *_: (0, g), jnp.bfloat16),
        part=((rows, columns), (rows, columns // grid), lambda g, *_: (0, g), jnp.bfloat16),
        pair=(
            (2, rows, columns),
            (None, rows, columns // grid),
            lambda g, place: (1 - lax.rem(place[0], 2), 0, g),
            jnp.bfloat16,
        ),
        rest=((heads * depth, tok), (step * depth, tok), lambda g, *_: (g, 0), jnp.float32),
        weights=((heads, tok, tok), (step, tok, tok), lambda g, *_: (g, 0, 0), jnp.bfloat16),
        stat=((grid, 8, tok), (1, 8, tok), lambda g, *_: (g, 0, 0), jnp.float32),
    )
    block = lambda kind: pl.BlockSpec(specs[kind][1], specs[kind][2])
    return pl.pallas_call(
        functools.partial(kernel, group),
        grid_spec=pltpu.PrefetchScalarGridSpec(
            num_scalar_prefetch=len(place),
            grid=(grid,),
            in_specs=[block(kind) for kind in kinds],
            out_specs=[block(kind) for kind in out_kinds],
        ),
        out_shape=[jax.ShapeDtypeStruct(specs[kind][0], specs[kind][3]) for kind in out_kinds],
        compiler_params=params(1, 24),
        name=name,
    )(*place, *arrays)


def shifted(array, steps):
    count = lax.axis_size("seq")
    return lax.ppermute(array, "seq", [(source, source + steps) for source in range(count - steps)])


def exchanged(array, axis, bit):
    count = lax.axis_size(axis)
    return lax.ppermute(array, axis, [(source, source ^ bit) for source in range(count)])


def on_device(
    normed_input, query, key, value, adapter_down_maps, adapter_up_maps, block_adapter_choice
):
    tok = query.shape[0]
    assert 2 * tok == WINDOW and SEG_LEN % tok == 0
    where = lax.axis_index("seq")
    place = where.reshape(1)
    choice = block_adapter_choice

    rows = tok // PARTS
    key_parts = [key[n * rows : (n + 1) * rows] for n in range(PARTS)] if PARTS > 1 else [key]
    key_far = [shifted(part, 2) for part in key_parts]
    latent = latent_share(place, choice, normed_input.T, adapter_down_maps)
    bit = 1
    while 2 * bit < lax.axis_size("tp"):
        latent = latent + exchanged(latent, "tp", bit)
        bit *= 2
    theirs = exchanged(latent, "tp", bit)
    values = adapt(place, choice, latent, theirs, adapter_up_maps, value)
    value_far = [shifted(part, 2) for part in values]

    pairs = [[n, n + 1] for n in range(0, lax.axis_size("seq"), 2)]

    def from_one_back(own, far):
        return [
            in_hbm(
                lax.all_gather(
                    jnp.where(where % 2 == 0, mine, theirs), "seq", axis_index_groups=pairs
                )
            )
            for mine, theirs in zip(own, far)
        ]

    call = functools.partial(by_heads, query_shape=query.shape, columns=key.shape[1])
    key_own, _ = lax.optimization_barrier((key_parts, values))
    key_mid = from_one_back(key_own, key_far)
    own, weights_far, tops = call(
        near_far_kernel,
        "near_far",
        place=[place],
        arrays=[query, key, *values, *key_far],
        kinds=["queries", "one"] + ["part"] * (2 * PARTS),
        out_kinds=["rest", "weights", "stat"],
    )
    values, own = lax.optimization_barrier((values, own))
    value_mid = from_one_back(values, value_far)
    rest, weights_mid, _ = call(
        middle_kernel,
        "middle",
        place=[place],
        arrays=[query, own, weights_far, tops, *key_mid, *value_far],
        kinds=["queries", "rest", "weights", "stat"] + ["pair"] * PARTS + ["part"] * PARTS,
        out_kinds=["rest", "weights", "stat"],
    )
    return call(
        finish_kernel,
        "finish",
        place=[place],
        arrays=[rest, weights_mid, *value_mid],
        kinds=["rest", "weights"] + ["pair"] * PARTS,
        out_kinds=["queries"],
    )[0]


def solution(mesh):
    placed = (
        P("seq", "tp"),
        P("seq", "tp"),
        P("seq", "tp"),
        P("seq", "tp"),
        P(None, None, "tp"),
        P(None, None, "tp"),
        P(),
    )
    return jax.shard_map(
        on_device, mesh=mesh, in_specs=placed, out_specs=P("seq", "tp"), check_vma=False
    )
```

```python
import functools

import jax
import jax.numpy as jnp
from jax import lax
from jax.experimental import pallas as pl
from jax.experimental.pallas import tpu as pltpu
from jax.sharding import PartitionSpec as P

HEAD_WIDTH = 128
WINDOW = 1024
SEG_LEN = 2048
SCALE = 168.0 ** (-0.5)
LOG2_E = 1.4426950408889634
EXPONENT = SCALE * LOG2_E
MASKED = -1e30
TILE = 256
HALF = 128
ONES = 16
PAIR = 2


def params(steps, mib):
    return pltpu.CompilerParams(
        vmem_limit_bytes=mib * 1024 * 1024, dimension_semantics=("arbitrary",) * steps
    )


def dot(left, right, left_dim, right_dim):
    return lax.dot_general(
        left, right, (((left_dim,), (right_dim,)), ((), ())), preferred_element_type=jnp.float32
    )


def in_hbm(array):
    return pltpu.with_memory_space_constraint(array, pltpu.HBM)


def adapter_of(place, choice, tok):
    return choice[lax.div(place[0] * tok, SEG_LEN)]


def latent_kernel(pieces, place, choice, input_t, down, out, rows, map_rows, sems):
    tok = out.shape[1]
    copies = [
        pltpu.make_async_copy(
            down.at[adapter_of(place, choice, tok)], map_rows, sems.at[len(pieces)]
        )
    ]
    for n, (first, last) in enumerate(pieces):
        part = pl.ds(first, last - first)
        copies.append(pltpu.make_async_copy(input_t.at[part], rows.at[part], sems.at[n]))
    for copy in copies:
        copy.start()
    copies[0].wait()
    total = None
    for (first, last), copy in zip(pieces, copies[1:]):
        copy.wait()
        product = dot(map_rows[:, first:last], rows[first:last, :], 1, 0)
        total = product if total is None else total + product
    out[...] = total


def latent_share(place, choice, input_t, down_maps):
    features, tok = input_t.shape
    rank = down_maps.shape[1]
    pieces = [(first, min(first + 512, features)) for first in range(0, features, 512)]
    return pl.pallas_call(
        functools.partial(latent_kernel, pieces),
        grid_spec=pltpu.PrefetchScalarGridSpec(
            num_scalar_prefetch=2,
            grid=(1,),
            in_specs=[
                pl.BlockSpec(memory_space=pltpu.HBM),
                pl.BlockSpec(memory_space=pltpu.HBM),
            ],
            out_specs=pl.BlockSpec((rank, tok), lambda i, *_: (0, 0)),
            scratch_shapes=[
                pltpu.VMEM((features, tok), input_t.dtype),
                pltpu.VMEM((rank, features), down_maps.dtype),
                pltpu.SemaphoreType.DMA((len(pieces) + 1,)),
            ],
        ),
        out_shape=jax.ShapeDtypeStruct((rank, tok), jnp.float32),
        compiler_params=params(1, 8),
        name="latent_share",
    )(place, in_hbm(choice), in_hbm(input_t), in_hbm(down_maps))


def adapt_kernel(place, choice, mine, theirs, up, value, out):
    latent = (mine[...] + theirs[...]).astype(jnp.bfloat16)
    update = dot(latent, up[0], 0, 0)
    total = (value[...].astype(jnp.float32) + update).astype(jnp.bfloat16)
    parts, _, width = out.shape
    for n in range(parts):
        out[n] = total[:, n * width : (n + 1) * width]


def adapt(place, choice, mine, theirs, up_maps, value):
    rank, tok = mine.shape
    columns = value.shape[1]
    whole = lambda i, *_: (0, 0)
    chosen = lambda i, place, choice: (adapter_of(place, choice, tok), 0, 0)
    shape = (columns // (PAIR * HEAD_WIDTH), tok, PAIR * HEAD_WIDTH)
    return pl.pallas_call(
        adapt_kernel,
        grid_spec=pltpu.PrefetchScalarGridSpec(
            num_scalar_prefetch=2,
            grid=(1,),
            in_specs=[
                pl.BlockSpec((rank, tok), whole),
                pl.BlockSpec((rank, tok), whole),
                pl.BlockSpec((1, rank, columns), chosen),
                pl.BlockSpec((tok, columns), whole),
            ],
            out_specs=pl.BlockSpec(shape, lambda i, *_: (0, 0, 0)),
        ),
        out_shape=jax.ShapeDtypeStruct(shape, jnp.bfloat16),
        compiler_params=params(1, 8),
        name="adapt_values",
    )(place, choice, mine, theirs, up_maps, value)


def weights_of(scores, top):
    return jnp.exp2(((scores - top) * EXPONENT).astype(jnp.bfloat16))


def tree(operation, items):
    items = list(items)
    while len(items) > 1:
        items = [
            operation(items[n], items[n + 1]) if n + 1 < len(items) else items[n]
            for n in range(0, len(items), 2)
        ]
    return items[0]


def top_of(scores):
    pieces = [s[n : n + 32] for s in scores for n in range(0, s.shape[0], 32)]
    pieces = tree(jnp.maximum, pieces)
    pieces = tree(jnp.maximum, [pieces[n : n + 8] for n in range(0, 32, 8)])
    return jnp.max(pieces, axis=0, keepdims=True)


def values_and_ones(v, columns):
    turned = v[:, columns].T
    return jnp.concatenate([turned, jnp.ones((ONES, v.shape[0]), jnp.bfloat16)], axis=0)


def head_rows(h):
    return slice(h * (HEAD_WIDTH + ONES), (h + 1) * (HEAD_WIDTH + ONES))


def head_columns(h):
    return slice(h * HEAD_WIDTH, (h + 1) * HEAD_WIDTH)


def in_steps(units, stages):
    held = [None] * len(units)
    for step in range(len(units) + len(stages) - 1):
        for n, stage in enumerate(stages):
            if 0 <= step - n < len(units):
                held[step - n] = stage(units[step - n], held[step - n])


def units_of(group, tok):
    return [(h, i) for g in range(PAIR) for i in range(tok // TILE) for h in range(g * group, (g + 1) * group)]


def near_far_kernel(group, place, q, k, v, k_far, out, weights_far, tops):
    far_there = place[0] >= 2
    tok = q.shape[0]
    causal = lax.broadcasted_iota(jnp.int32, (HALF, HALF), 0) <= lax.broadcasted_iota(
        jnp.int32, (HALF, HALF), 1
    )
    v_t = [values_and_ones(v, head_columns(g)) for g in range(PAIR)]
    nothing = jnp.zeros((HALF, HALF), jnp.bfloat16)
    tiles = tok // TILE
    blocks = [slice(i * TILE, (i + 1) * TILE) for i in range(tiles)]

    def score(unit, _):
        h, i = unit
        qh = q[blocks[i], head_columns(h)]
        columns = head_columns(h // group)
        near = [dot(k[blocks[j], columns], qh, 1, 1) for j in range(i + 1)]
        far = [dot(k_far[blocks[j], columns], qh, 1, 1) for j in range(i, tiles)]
        return near, far

    def weigh(unit, scores):
        h, i = unit
        near, far = scores
        near_columns, far_columns = [], []
        for half in range(2):
            a = slice(half * HALF, (half + 1) * HALF)
            near_edge = near[i][: (half + 1) * HALF, a]
            far_edge = far[0][half * HALF :, a]
            near_pieces = [s[:, a] for s in near[:i]]
            if half == 1:
                near_pieces.append(near_edge[:HALF])
            near_pieces.append(jnp.where(causal, near_edge[half * HALF :], MASKED))
            far_pieces = [jnp.where(causal, MASKED, far_edge[:HALF])]
            if half == 0:
                far_pieces.append(far_edge[HALF:])
            far_pieces += [s[:, a] for s in far[1:]]
            top = jnp.maximum(
                top_of(near_pieces), jnp.where(far_there, top_of(far_pieces), MASKED)
            )
            far_top = jnp.where(far_there, top, -MASKED)
            near_weights = [weights_of(s, top) for s in near_pieces]
            far_weights = [weights_of(s, far_top) for s in far_pieces]
            if half == 0:
                near_weights.append(nothing)
            else:
                far_weights.insert(0, nothing)
            near_columns.append(jnp.concatenate(near_weights, axis=0))
            far_columns.append(jnp.concatenate(far_weights, axis=0))
            queries = slice(i * TILE + half * HALF, i * TILE + (half + 1) * HALF)
            tops[0, h : h + 1, queries] = top
        weights_far[h, i * TILE :, blocks[i]] = jnp.concatenate(far_columns, axis=1)
        return jnp.concatenate(near_columns, axis=1)

    def multiply(unit, weights):
        h, i = unit
        out[head_rows(h), blocks[i]] = dot(v_t[h // group][:, : (i + 1) * TILE], weights, 1, 0)

    in_steps(units_of(group, tok), [score, weigh, multiply])


def middle_kernel(group, place, q, own, weights_far, tops, k, v_far, rest, weights, shrink):
    there = place[0] >= 1
    tok = q.shape[0]
    v_t = [values_and_ones(v_far, head_columns(g)) for g in range(PAIR)]
    tiles = tok // TILE
    blocks = [slice(i * TILE, (i + 1) * TILE) for i in range(tiles)]

    def score(unit, _):
        h, i = unit
        qh = q[blocks[i], head_columns(h)]
        return [dot(k[blocks[j], head_columns(h // group)], qh, 1, 1) for j in range(tiles)]

    def weigh(unit, scores):
        h, i = unit
        before = tops[0, h : h + 1, blocks[i]]
        top = jnp.maximum(before, jnp.where(there, top_of(scores), MASKED))
        less = jnp.exp2((before - top) * EXPONENT)
        top = jnp.where(there, top, -MASKED)
        for j, s in enumerate(scores):
            weights[h, blocks[j], blocks[i]] = weights_of(s, top)
        shrink[0, h : h + 1, blocks[i]] = less
        return less

    def multiply(unit, less):
        h, i = unit
        far = dot(v_t[h // group][:, i * TILE :], weights_far[h, i * TILE :, blocks[i]], 1, 0)
        rest[head_rows(h), blocks[i]] = (own[head_rows(h), blocks[i]] + far) * less

    in_steps(units_of(group, tok), [score, weigh, multiply])


def finish_kernel(group, rest, weights, v, *refs):
    out = refs[-1]
    tok = out.shape[0]
    v_t = [values_and_ones(v, head_columns(g)) for g in range(PAIR)]
    blocks = [slice(first, first + TILE) for first in range(0, tok, TILE)]

    def multiply(unit, _):
        h, i = unit
        return dot(v_t[h // group], weights[h, :, blocks[i]], 1, 0)

    def normalise(unit, middle):
        h, i = unit
        total = rest[head_rows(h), blocks[i]] + middle
        normal = total[:HEAD_WIDTH] * (1.0 / total[HEAD_WIDTH : HEAD_WIDTH + 1])
        out[blocks[i], head_columns(h)] = normal.astype(jnp.bfloat16).T

    in_steps(units_of(group, tok), [multiply, normalise])


def by_heads(kernel, name, query_shape, columns, place, arrays, kinds, out_kinds, only=None, into=None):
    tok, width = query_shape
    kv_heads = columns // HEAD_WIDTH
    group = width // columns
    grid = kv_heads // PAIR
    depth = HEAD_WIDTH + ONES
    heads = width // HEAD_WIDTH
    step = heads // grid
    at = (lambda g: g) if only is None else (lambda g: only)
    one_group = (tok, columns // grid)
    specs = dict(
        queries=((tok, width), (tok, width // grid), lambda g, *_: (0, at(g)), jnp.bfloat16),
        one=((tok, columns), one_group, lambda g, *_: (0, at(g)), jnp.bfloat16),
        values=((grid, *one_group), (None, *one_group), lambda g, *_: (at(g), 0, 0), jnp.bfloat16),
        alone=(one_group, one_group, lambda g, *_: (0, 0), jnp.bfloat16),
        rest=((heads * depth, tok), (step * depth, tok), lambda g, *_: (at(g), 0), jnp.float32),
        weights=((heads, tok, tok), (step, tok, tok), lambda g, *_: (at(g), 0, 0), jnp.bfloat16),
        stat=((grid, 8, tok), (1, 8, tok), lambda g, *_: (at(g), 0, 0), jnp.float32),
    )
    block = lambda kind: pl.BlockSpec(specs[kind][1], specs[kind][2])
    in_specs = [block(kind) for kind in kinds]
    aliases = {}
    if into is not None:
        aliases = {len(place) + len(arrays): 0}
        arrays = [*arrays, into]
        in_specs.append(pl.BlockSpec(memory_space=pl.ANY))
    return pl.pallas_call(
        functools.partial(kernel, group),
        grid_spec=pltpu.PrefetchScalarGridSpec(
            num_scalar_prefetch=len(place),
            grid=(grid if only is None else 1,),
            in_specs=in_specs,
            out_specs=[block(kind) for kind in out_kinds],
        ),
        out_shape=[jax.ShapeDtypeStruct(specs[kind][0], specs[kind][3]) for kind in out_kinds],
        input_output_aliases=aliases,
        compiler_params=params(1, 24),
        name=name,
    )(*place, *arrays)


def shifted(array, steps):
    count = lax.axis_size("seq")
    return lax.ppermute(array, "seq", [(source, source + steps) for source in range(count - steps)])


def exchanged(array, axis, bit):
    count = lax.axis_size(axis)
    return lax.ppermute(array, axis, [(source, source ^ bit) for source in range(count)])


def on_device(
    normed_input, query, key, value, adapter_down_maps, adapter_up_maps, block_adapter_choice
):
    tok = query.shape[0]
    assert 2 * tok == WINDOW and SEG_LEN % tok == 0
    where = lax.axis_index("seq")
    place = where.reshape(1)
    choice = block_adapter_choice

    key_far = shifted(key, 2)
    latent = latent_share(place, choice, normed_input.T, adapter_down_maps)
    bit = 1
    while 2 * bit < lax.axis_size("tp"):
        latent = latent + exchanged(latent, "tp", bit)
        bit *= 2
    theirs = exchanged(latent, "tp", bit)
    values = adapt(place, choice, latent, theirs, adapter_up_maps, value)
    value_far = shifted(values, 2)

    def from_one_back(own, far):
        return exchanged(jnp.where(where % 2 == 0, own, far), "seq", 1)

    call = functools.partial(by_heads, query_shape=query.shape, columns=key.shape[1])
    key_own, _ = lax.optimization_barrier((key, values))
    key_mid = from_one_back(key_own, key_far)
    own, weights_far, tops = call(
        near_far_kernel,
        "near_far",
        place=[place],
        arrays=[query, key, values, key_far],
        kinds=["queries", "one", "values", "one"],
        out_kinds=["rest", "weights", "stat"],
    )
    values, own = lax.optimization_barrier((values, own))
    value_mid = from_one_back(values[0], value_far[0])
    rest, weights_mid, _ = call(
        middle_kernel,
        "middle",
        place=[place],
        arrays=[query, own, weights_far, tops, key_mid, value_far],
        kinds=["queries", "rest", "weights", "stat", "one", "values"],
        out_kinds=["rest", "weights", "stat"],
    )
    values, value_far, rest = lax.optimization_barrier((values, value_far, rest))
    done = None
    for n in range(values.shape[0]):
        if n > 0:
            value_mid = from_one_back(values[n], value_far[n])
        [done] = call(
            finish_kernel,
            "finish",
            place=[],
            arrays=[rest, weights_mid, value_mid],
            kinds=["rest", "weights", "alone"],
            out_kinds=["queries"],
            only=n,
            into=done,
        )
    return done


def solution(mesh):
    placed = (
        P("seq", "tp"),
        P("seq", "tp"),
        P("seq", "tp"),
        P("seq", "tp"),
        P(None, None, "tp"),
        P(None, None, "tp"),
        P(),
    )
    return jax.shard_map(
        on_device, mesh=mesh, in_specs=placed, out_specs=P("seq", "tp"), check_vma=False
    )
```

```python
import functools

import jax
import jax.numpy as jnp
from jax import lax
from jax.experimental import pallas as pl
from jax.experimental.pallas import tpu as pltpu
from jax.sharding import PartitionSpec as P

HEAD_WIDTH = 128
WINDOW = 1024
SEG_LEN = 2048
SCALE = 168.0 ** (-0.5)
LOG2_E = 1.4426950408889634
EXPONENT = SCALE * LOG2_E
MASKED = -1e30
TILE = 256
HALF = 128
ONES = 16
PAIR = 2


def params(steps, mib):
    return pltpu.CompilerParams(
        vmem_limit_bytes=mib * 1024 * 1024, dimension_semantics=("arbitrary",) * steps
    )


def dot(left, right, left_dim, right_dim):
    return lax.dot_general(
        left, right, (((left_dim,), (right_dim,)), ((), ())), preferred_element_type=jnp.float32
    )


def in_hbm(array):
    return pltpu.with_memory_space_constraint(array, pltpu.HBM)


def adapter_of(place, choice, tok):
    return choice[lax.div(place[0] * tok, SEG_LEN)]


def latent_kernel(pieces, place, choice, input_t, down, out, rows, map_rows, sems):
    tok = out.shape[1]
    copies = [
        pltpu.make_async_copy(
            down.at[adapter_of(place, choice, tok)], map_rows, sems.at[len(pieces)]
        )
    ]
    for n, (first, last) in enumerate(pieces):
        part = pl.ds(first, last - first)
        copies.append(pltpu.make_async_copy(input_t.at[part], rows.at[part], sems.at[n]))
    for copy in copies:
        copy.start()
    copies[0].wait()
    total = None
    for (first, last), copy in zip(pieces, copies[1:]):
        copy.wait()
        product = dot(map_rows[:, first:last], rows[first:last, :], 1, 0)
        total = product if total is None else total + product
    out[...] = total


def latent_share(place, choice, input_t, down_maps):
    features, tok = input_t.shape
    rank = down_maps.shape[1]
    pieces = [(first, min(first + 512, features)) for first in range(0, features, 512)]
    return pl.pallas_call(
        functools.partial(latent_kernel, pieces),
        grid_spec=pltpu.PrefetchScalarGridSpec(
            num_scalar_prefetch=2,
            grid=(1,),
            in_specs=[
                pl.BlockSpec(memory_space=pltpu.HBM),
                pl.BlockSpec(memory_space=pltpu.HBM),
            ],
            out_specs=pl.BlockSpec((rank, tok), lambda i, *_: (0, 0)),
            scratch_shapes=[
                pltpu.VMEM((features, tok), input_t.dtype),
                pltpu.VMEM((rank, features), down_maps.dtype),
                pltpu.SemaphoreType.DMA((len(pieces) + 1,)),
            ],
        ),
        out_shape=jax.ShapeDtypeStruct((rank, tok), jnp.float32),
        compiler_params=params(1, 8),
        name="latent_share",
    )(place, in_hbm(choice), in_hbm(input_t), in_hbm(down_maps))


def adapt_kernel(place, choice, mine, theirs, up, value, out):
    latent = (mine[...] + theirs[...]).astype(jnp.bfloat16)
    update = dot(latent, up[0], 0, 0)
    total = (value[...].astype(jnp.float32) + update).astype(jnp.bfloat16)
    parts, _, width = out.shape
    for n in range(parts):
        out[n] = total[:, n * width : (n + 1) * width]


def adapt(place, choice, mine, theirs, up_maps, value):
    rank, tok = mine.shape
    columns = value.shape[1]
    whole = lambda i, *_: (0, 0)
    chosen = lambda i, place, choice: (adapter_of(place, choice, tok), 0, 0)
    shape = (columns // (PAIR * HEAD_WIDTH), tok, PAIR * HEAD_WIDTH)
    return pl.pallas_call(
        adapt_kernel,
        grid_spec=pltpu.PrefetchScalarGridSpec(
            num_scalar_prefetch=2,
            grid=(1,),
            in_specs=[
                pl.BlockSpec((rank, tok), whole),
                pl.BlockSpec((rank, tok), whole),
                pl.BlockSpec((1, rank, columns), chosen),
                pl.BlockSpec((tok, columns), whole),
            ],
            out_specs=pl.BlockSpec(shape, lambda i, *_: (0, 0, 0)),
        ),
        out_shape=jax.ShapeDtypeStruct(shape, jnp.bfloat16),
        compiler_params=params(1, 8),
        name="adapt_values",
    )(place, choice, mine, theirs, in_hbm(up_maps), value)


def weights_of(scores, top):
    return jnp.exp2(((scores - top) * EXPONENT).astype(jnp.bfloat16))


def tree(operation, items):
    items = list(items)
    while len(items) > 1:
        items = [
            operation(items[n], items[n + 1]) if n + 1 < len(items) else items[n]
            for n in range(0, len(items), 2)
        ]
    return items[0]


def top_of(scores):
    pieces = [s[n : n + 32] for s in scores for n in range(0, s.shape[0], 32)]
    pieces = tree(jnp.maximum, pieces)
    pieces = tree(jnp.maximum, [pieces[n : n + 8] for n in range(0, 32, 8)])
    return jnp.max(pieces, axis=0, keepdims=True)


def values_and_ones(v, columns):
    turned = v[:, columns].T
    return jnp.concatenate([turned, jnp.ones((ONES, v.shape[0]), jnp.bfloat16)], axis=0)


def head_rows(h):
    return slice(h * (HEAD_WIDTH + ONES), (h + 1) * (HEAD_WIDTH + ONES))


def head_columns(h):
    return slice(h * HEAD_WIDTH, (h + 1) * HEAD_WIDTH)


def in_steps(units, stages):
    held = [None] * len(units)
    for step in range(len(units) + len(stages) - 1):
        for n, stage in enumerate(stages):
            if 0 <= step - n < len(units):
                held[step - n] = stage(units[step - n], held[step - n])


def units_of(group, tok):
    return [(h, i) for g in range(PAIR) for i in range(tok // TILE) for h in range(g * group, (g + 1) * group)]


def near_far_kernel(group, place, *refs):
    @pl.when(place[0] >= 2)
    def _():
        near_far_steps(group, True, *refs)

    @pl.when(place[0] < 2)
    def _():
        near_far_steps(group, False, *refs)


def near_far_steps(group, far_there, q, k, v, k_far, out, weights_far, tops):
    tok = q.shape[0]
    causal = lax.broadcasted_iota(jnp.int32, (HALF, HALF), 0) <= lax.broadcasted_iota(
        jnp.int32, (HALF, HALF), 1
    )
    v_t = [values_and_ones(v, head_columns(g)) for g in range(PAIR)]
    nothing = jnp.zeros((HALF, HALF), jnp.bfloat16)
    tiles = tok // TILE
    blocks = [slice(i * TILE, (i + 1) * TILE) for i in range(tiles)]

    def score(unit, _):
        h, i = unit
        qh = q[blocks[i], head_columns(h)]
        columns = head_columns(h // group)
        near = [dot(k[blocks[j], columns], qh, 1, 1) for j in range(i + 1)]
        far = []
        if far_there:
            far = [dot(k_far[blocks[j], columns], qh, 1, 1) for j in range(i, tiles)]
        return near, far

    def weigh(unit, scores):
        h, i = unit
        near, far = scores
        near_columns, far_columns = [], []
        for half in range(2):
            a = slice(half * HALF, (half + 1) * HALF)
            near_edge = near[i][: (half + 1) * HALF, a]
            near_pieces = [s[:, a] for s in near[:i]]
            if half == 1:
                near_pieces.append(near_edge[:HALF])
            near_pieces.append(jnp.where(causal, near_edge[half * HALF :], MASKED))
            far_pieces = []
            if far_there:
                far_edge = far[0][half * HALF :, a]
                far_pieces.append(jnp.where(causal, MASKED, far_edge[:HALF]))
                if half == 0:
                    far_pieces.append(far_edge[HALF:])
                far_pieces += [s[:, a] for s in far[1:]]
            top = top_of(near_pieces + far_pieces)
            near_weights = [weights_of(s, top) for s in near_pieces]
            if half == 0:
                near_weights.append(nothing)
            near_columns.append(jnp.concatenate(near_weights, axis=0))
            if far_there:
                far_weights = [weights_of(s, top) for s in far_pieces]
                if half == 1:
                    far_weights.insert(0, nothing)
                far_columns.append(jnp.concatenate(far_weights, axis=0))
            queries = slice(i * TILE + half * HALF, i * TILE + (half + 1) * HALF)
            tops[0, h : h + 1, queries] = top
        if far_there:
            weights_far[h, i * TILE :, blocks[i]] = jnp.concatenate(far_columns, axis=1)
        return jnp.concatenate(near_columns, axis=1)

    def multiply(unit, weights):
        h, i = unit
        out[head_rows(h), blocks[i]] = dot(v_t[h // group][:, : (i + 1) * TILE], weights, 1, 0)

    in_steps(units_of(group, tok), [score, weigh, multiply])


def middle_kernel(group, place, *refs):
    @pl.when(place[0] >= 2)
    def _():
        middle_steps(group, True, *refs)

    @pl.when(place[0] == 1)
    def _():
        middle_steps(group, False, *refs)

    @pl.when(place[0] == 0)
    def _():
        own, rest = refs[1], refs[6]
        rest[...] = own[...]


def middle_steps(group, far_there, q, own, weights_far, tops, k, v_far, rest, weights):
    tok = q.shape[0]
    v_t = [values_and_ones(v_far, head_columns(g)) for g in range(PAIR)] if far_there else []
    tiles = tok // TILE
    blocks = [slice(i * TILE, (i + 1) * TILE) for i in range(tiles)]

    def score(unit, _):
        h, i = unit
        qh = q[blocks[i], head_columns(h)]
        return [dot(k[blocks[j], head_columns(h // group)], qh, 1, 1) for j in range(tiles)]

    def weigh(unit, scores):
        h, i = unit
        before = tops[0, h : h + 1, blocks[i]]
        top = jnp.maximum(before, top_of(scores))
        for j, s in enumerate(scores):
            weights[h, blocks[j], blocks[i]] = weights_of(s, top)
        return jnp.exp2((before - top) * EXPONENT)

    def multiply(unit, less):
        h, i = unit
        total = own[head_rows(h), blocks[i]]
        if far_there:
            total += dot(v_t[h // group][:, i * TILE :], weights_far[h, i * TILE :, blocks[i]], 1, 0)
        rest[head_rows(h), blocks[i]] = total * less

    in_steps(units_of(group, tok), [score, weigh, multiply])


def finish_kernel(group, place, *refs):
    @pl.when(place[0] >= 1)
    def _():
        finish_steps(group, True, *refs)

    @pl.when(place[0] == 0)
    def _():
        finish_steps(group, False, *refs)


def finish_steps(group, there, rest, weights, v, *refs):
    out = refs[-1]
    tok = out.shape[0]
    v_t = [values_and_ones(v, head_columns(g)) for g in range(PAIR)] if there else []
    blocks = [slice(first, first + TILE) for first in range(0, tok, TILE)]

    def multiply(unit, _):
        h, i = unit
        return dot(v_t[h // group], weights[h, :, blocks[i]], 1, 0) if there else None

    def normalise(unit, middle):
        h, i = unit
        total = rest[head_rows(h), blocks[i]]
        if there:
            total += middle
        normal = total[:HEAD_WIDTH] * (1.0 / total[HEAD_WIDTH : HEAD_WIDTH + 1])
        out[blocks[i], head_columns(h)] = normal.astype(jnp.bfloat16).T

    in_steps(units_of(group, tok), [multiply, normalise])


def by_heads(kernel, name, query_shape, columns, place, arrays, kinds, out_kinds, only=None, into=None):
    tok, width = query_shape
    kv_heads = columns // HEAD_WIDTH
    group = width // columns
    grid = kv_heads // PAIR
    depth = HEAD_WIDTH + ONES
    heads = width // HEAD_WIDTH
    step = heads // grid
    at = (lambda g: g) if only is None else (lambda g: only)
    one_group = (tok, columns // grid)
    specs = dict(
        queries=((tok, width), (tok, width // grid), lambda g, *_: (0, at(g)), jnp.bfloat16),
        one=((tok, columns), one_group, lambda g, *_: (0, at(g)), jnp.bfloat16),
        values=((grid, *one_group), (None, *one_group), lambda g, *_: (at(g), 0, 0), jnp.bfloat16),
        alone=(one_group, one_group, lambda g, *_: (0, 0), jnp.bfloat16),
        rest=((heads * depth, tok), (step * depth, tok), lambda g, *_: (at(g), 0), jnp.float32),
        weights=((heads, tok, tok), (step, tok, tok), lambda g, *_: (at(g), 0, 0), jnp.bfloat16),
        stat=((grid, 8, tok), (1, 8, tok), lambda g, *_: (at(g), 0, 0), jnp.float32),
    )
    block = lambda kind: pl.BlockSpec(specs[kind][1], specs[kind][2])
    in_specs = [block(kind) for kind in kinds]
    aliases = {}
    if into is not None:
        aliases = {len(place) + len(arrays): 0}
        arrays = [*arrays, into]
        in_specs.append(pl.BlockSpec(memory_space=pl.ANY))
    return pl.pallas_call(
        functools.partial(kernel, group),
        grid_spec=pltpu.PrefetchScalarGridSpec(
            num_scalar_prefetch=len(place),
            grid=(grid if only is None else 1,),
            in_specs=in_specs,
            out_specs=[block(kind) for kind in out_kinds],
        ),
        out_shape=[jax.ShapeDtypeStruct(specs[kind][0], specs[kind][3]) for kind in out_kinds],
        input_output_aliases=aliases,
        compiler_params=params(1, 24),
        name=name,
    )(*place, *arrays)


def shifted(array, steps):
    count = lax.axis_size("seq")
    return lax.ppermute(array, "seq", [(source, source + steps) for source in range(count - steps)])


def exchanged(array, axis, bit):
    count = lax.axis_size(axis)
    return lax.ppermute(array, axis, [(source, source ^ bit) for source in range(count)])


def on_device(
    normed_input, query, key, value, adapter_down_maps, adapter_up_maps, block_adapter_choice
):
    tok = query.shape[0]
    assert 2 * tok == WINDOW and SEG_LEN % tok == 0
    where = lax.axis_index("seq")
    place = where.reshape(1)
    choice = block_adapter_choice

    key_far = shifted(key, 2)
    latent = latent_share(place, choice, normed_input.T, adapter_down_maps)
    bit = 1
    while 2 * bit < lax.axis_size("tp"):
        latent = latent + exchanged(latent, "tp", bit)
        bit *= 2
    theirs = exchanged(latent, "tp", bit)
    values = adapt(place, choice, latent, theirs, adapter_up_maps, value)
    value_far = shifted(values, 2)

    def from_one_back(own, far):
        return exchanged(jnp.where(where % 2 == 0, own, far), "seq", 1)

    call = functools.partial(by_heads, query_shape=query.shape, columns=key.shape[1])
    key_own, _ = lax.optimization_barrier((key, values))
    key_mid = from_one_back(key_own, key_far)
    own, weights_far, tops = call(
        near_far_kernel,
        "near_far",
        place=[place],
        arrays=[query, key, values, key_far],
        kinds=["queries", "one", "values", "one"],
        out_kinds=["rest", "weights", "stat"],
    )
    values, own = lax.optimization_barrier((values, own))
    value_mid = from_one_back(values[0], value_far[0])
    rest, weights_mid = call(
        middle_kernel,
        "middle",
        place=[place],
        arrays=[query, own, weights_far, tops, key_mid, value_far],
        kinds=["queries", "rest", "weights", "stat", "one", "values"],
        out_kinds=["rest", "weights"],
    )
    values, value_far, rest = lax.optimization_barrier((values, value_far, rest))
    done = None
    for n in range(values.shape[0]):
        if n > 0:
            value_mid = from_one_back(values[n], value_far[n])
        [done] = call(
            finish_kernel,
            "finish",
            place=[place],
            arrays=[rest, weights_mid, value_mid],
            kinds=["rest", "weights", "alone"],
            out_kinds=["queries"],
            only=n,
            into=done,
        )
    return done


def solution(mesh):
    placed = (
        P("seq", "tp"),
        P("seq", "tp"),
        P("seq", "tp"),
        P("seq", "tp"),
        P(None, None, "tp"),
        P(None, None, "tp"),
        P(),
    )
    return jax.shard_map(
        on_device, mesh=mesh, in_specs=placed, out_specs=P("seq", "tp"), check_vma=False
    )
```

```python
import functools

import jax
import jax.numpy as jnp
from jax import lax
from jax.experimental import pallas as pl
from jax.experimental.pallas import tpu as pltpu
from jax.sharding import PartitionSpec as P

HEAD_WIDTH = 128
WINDOW = 1024
SEG_LEN = 2048
SCALE = 168.0 ** (-0.5)
LOG2_E = 1.4426950408889634
EXPONENT = SCALE * LOG2_E
MASKED = -1e30
TILE = 256
HALF = 128
ONES = 16
PAIR = 2


def params(steps, mib):
    return pltpu.CompilerParams(
        vmem_limit_bytes=mib * 1024 * 1024, dimension_semantics=("arbitrary",) * steps
    )


def dot(left, right, left_dim, right_dim):
    return lax.dot_general(
        left, right, (((left_dim,), (right_dim,)), ((), ())), preferred_element_type=jnp.float32
    )


def in_hbm(array):
    return pltpu.with_memory_space_constraint(array, pltpu.HBM)


def adapter_of(place, choice, tok):
    return choice[lax.div(place[0] * tok, SEG_LEN)]


def latent_kernel(pieces, place, choice, input_t, down, out, rows, map_rows, sems):
    tok = out.shape[1]
    copies = [
        pltpu.make_async_copy(
            down.at[adapter_of(place, choice, tok)], map_rows, sems.at[len(pieces)]
        )
    ]
    for n, (first, last) in enumerate(pieces):
        part = pl.ds(first, last - first)
        copies.append(pltpu.make_async_copy(input_t.at[part], rows.at[part], sems.at[n]))
    for copy in copies:
        copy.start()
    copies[0].wait()
    total = None
    for (first, last), copy in zip(pieces, copies[1:]):
        copy.wait()
        product = dot(map_rows[:, first:last], rows[first:last, :], 1, 0)
        total = product if total is None else total + product
    out[...] = total


def latent_share(place, choice, input_t, down_maps):
    features, tok = input_t.shape
    rank = down_maps.shape[1]
    pieces = [(first, min(first + 512, features)) for first in range(0, features, 512)]
    return pl.pallas_call(
        functools.partial(latent_kernel, pieces),
        grid_spec=pltpu.PrefetchScalarGridSpec(
            num_scalar_prefetch=2,
            grid=(1,),
            in_specs=[
                pl.BlockSpec(memory_space=pltpu.HBM),
                pl.BlockSpec(memory_space=pltpu.HBM),
            ],
            out_specs=pl.BlockSpec((rank, tok), lambda i, *_: (0, 0)),
            scratch_shapes=[
                pltpu.VMEM((features, tok), input_t.dtype),
                pltpu.VMEM((rank, features), down_maps.dtype),
                pltpu.SemaphoreType.DMA((len(pieces) + 1,)),
            ],
        ),
        out_shape=jax.ShapeDtypeStruct((rank, tok), jnp.float32),
        compiler_params=params(1, 8),
        name="latent_share",
    )(place, in_hbm(choice), in_hbm(input_t), in_hbm(down_maps))


def adapt_kernel(place, choice, mine, theirs, up, value, out):
    latent = (mine[...] + theirs[...]).astype(jnp.bfloat16)
    update = dot(latent, up[0], 0, 0)
    total = (value[...].astype(jnp.float32) + update).astype(jnp.bfloat16)
    parts, _, width = out.shape
    for n in range(parts):
        out[n] = total[:, n * width : (n + 1) * width]


def adapt(place, choice, mine, theirs, up_maps, value):
    rank, tok = mine.shape
    columns = value.shape[1]
    whole = lambda i, *_: (0, 0)
    chosen = lambda i, place, choice: (adapter_of(place, choice, tok), 0, 0)
    shape = (columns // (PAIR * HEAD_WIDTH), tok, PAIR * HEAD_WIDTH)
    return pl.pallas_call(
        adapt_kernel,
        grid_spec=pltpu.PrefetchScalarGridSpec(
            num_scalar_prefetch=2,
            grid=(1,),
            in_specs=[
                pl.BlockSpec((rank, tok), whole),
                pl.BlockSpec((rank, tok), whole),
                pl.BlockSpec((1, rank, columns), chosen),
                pl.BlockSpec((tok, columns), whole),
            ],
            out_specs=pl.BlockSpec(shape, lambda i, *_: (0, 0, 0)),
        ),
        out_shape=jax.ShapeDtypeStruct(shape, jnp.bfloat16),
        compiler_params=params(1, 8),
        name="adapt_values",
    )(place, choice, mine, theirs, up_maps, value)


def weights_of(scores, top):
    return jnp.exp2(((scores - top) * EXPONENT).astype(jnp.bfloat16))


def tree(operation, items):
    items = list(items)
    while len(items) > 1:
        items = [
            operation(items[n], items[n + 1]) if n + 1 < len(items) else items[n]
            for n in range(0, len(items), 2)
        ]
    return items[0]


def top_of(scores):
    pieces = [s[n : n + 32] for s in scores for n in range(0, s.shape[0], 32)]
    pieces = tree(jnp.maximum, pieces)
    pieces = tree(jnp.maximum, [pieces[n : n + 8] for n in range(0, 32, 8)])
    return jnp.max(pieces, axis=0, keepdims=True)


def values_and_ones(v, columns):
    turned = v[:, columns].T
    return jnp.concatenate([turned, jnp.ones((ONES, v.shape[0]), jnp.bfloat16)], axis=0)


def picked(core, first, second):
    return jnp.where(core[0] == 1, first[...], second[...])


def head_rows(h):
    return slice(h * (HEAD_WIDTH + ONES), (h + 1) * (HEAD_WIDTH + ONES))


def head_columns(h):
    return slice(h * HEAD_WIDTH, (h + 1) * HEAD_WIDTH)


def in_steps(units, stages):
    held = [None] * len(units)
    for step in range(len(units) + len(stages) - 1):
        for n, stage in enumerate(stages):
            if 0 <= step - n < len(units):
                held[step - n] = stage(units[step - n], held[step - n])


def units_of(group, tok):
    return [(h, i) for g in range(PAIR) for i in range(tok // TILE) for h in range(g * group, (g + 1) * group)]


def near_far_kernel(group, place, core, *refs):
    @pl.when(place[0] >= 2)
    def _():
        near_far_steps(group, True, core, *refs)

    @pl.when(place[0] < 2)
    def _():
        near_far_steps(group, False, core, *refs)


def near_far_steps(group, far_there, core, q, k, v, k_far_1, k_far_0, out, weights_far, tops):
    k_far = picked(core, k_far_1, k_far_0) if far_there else None
    tok = q.shape[0]
    causal = lax.broadcasted_iota(jnp.int32, (HALF, HALF), 0) <= lax.broadcasted_iota(
        jnp.int32, (HALF, HALF), 1
    )
    v_t = [values_and_ones(v, head_columns(g)) for g in range(PAIR)]
    nothing = jnp.zeros((HALF, HALF), jnp.bfloat16)
    tiles = tok // TILE
    blocks = [slice(i * TILE, (i + 1) * TILE) for i in range(tiles)]

    def score(unit, _):
        h, i = unit
        qh = q[blocks[i], head_columns(h)]
        columns = head_columns(h // group)
        near = [dot(k[blocks[j], columns], qh, 1, 1) for j in range(i + 1)]
        far = []
        if far_there:
            far = [dot(k_far[blocks[j], columns], qh, 1, 1) for j in range(i, tiles)]
        return near, far

    def weigh(unit, scores):
        h, i = unit
        near, far = scores
        near_columns, far_columns = [], []
        for half in range(2):
            a = slice(half * HALF, (half + 1) * HALF)
            near_edge = near[i][: (half + 1) * HALF, a]
            near_pieces = [s[:, a] for s in near[:i]]
            if half == 1:
                near_pieces.append(near_edge[:HALF])
            near_pieces.append(jnp.where(causal, near_edge[half * HALF :], MASKED))
            far_pieces = []
            if far_there:
                far_edge = far[0][half * HALF :, a]
                far_pieces.append(jnp.where(causal, MASKED, far_edge[:HALF]))
                if half == 0:
                    far_pieces.append(far_edge[HALF:])
                far_pieces += [s[:, a] for s in far[1:]]
            top = top_of(near_pieces + far_pieces)
            near_weights = [weights_of(s, top) for s in near_pieces]
            if half == 0:
                near_weights.append(nothing)
            near_columns.append(jnp.concatenate(near_weights, axis=0))
            if far_there:
                far_weights = [weights_of(s, top) for s in far_pieces]
                if half == 1:
                    far_weights.insert(0, nothing)
                far_columns.append(jnp.concatenate(far_weights, axis=0))
            queries = slice(i * TILE + half * HALF, i * TILE + (half + 1) * HALF)
            tops[0, h : h + 1, queries] = top
        if far_there:
            weights_far[h, i * TILE :, blocks[i]] = jnp.concatenate(far_columns, axis=1)
        return jnp.concatenate(near_columns, axis=1)

    def multiply(unit, weights):
        h, i = unit
        out[head_rows(h), blocks[i]] = dot(v_t[h // group][:, : (i + 1) * TILE], weights, 1, 0)

    in_steps(units_of(group, tok), [score, weigh, multiply])


def middle_kernel(group, place, core, *refs):
    @pl.when(place[0] >= 2)
    def _():
        middle_steps(group, True, core, *refs)

    @pl.when(place[0] == 1)
    def _():
        middle_steps(group, False, core, *refs)

    @pl.when(place[0] == 0)
    def _():
        own, rest = refs[1], refs[8]
        rest[...] = own[...]


def middle_steps(
    group, far_there, core, q, own, weights_far, tops, k_1, k_0, v_far_1, v_far_0, rest, weights
):
    k = picked(core, k_1, k_0)
    v_far = picked(core, v_far_1, v_far_0) if far_there else None
    tok = q.shape[0]
    v_t = [values_and_ones(v_far, head_columns(g)) for g in range(PAIR)] if far_there else []
    tiles = tok // TILE
    blocks = [slice(i * TILE, (i + 1) * TILE) for i in range(tiles)]

    def score(unit, _):
        h, i = unit
        qh = q[blocks[i], head_columns(h)]
        return [dot(k[blocks[j], head_columns(h // group)], qh, 1, 1) for j in range(tiles)]

    def weigh(unit, scores):
        h, i = unit
        before = tops[0, h : h + 1, blocks[i]]
        top = jnp.maximum(before, top_of(scores))
        for j, s in enumerate(scores):
            weights[h, blocks[j], blocks[i]] = weights_of(s, top)
        return jnp.exp2((before - top) * EXPONENT)

    def multiply(unit, less):
        h, i = unit
        total = own[head_rows(h), blocks[i]]
        if far_there:
            total += dot(v_t[h // group][:, i * TILE :], weights_far[h, i * TILE :, blocks[i]], 1, 0)
        rest[head_rows(h), blocks[i]] = total * less

    in_steps(units_of(group, tok), [score, weigh, multiply])


def finish_kernel(group, place, core, *refs):
    @pl.when(place[0] >= 1)
    def _():
        finish_steps(group, True, core, *refs)

    @pl.when(place[0] == 0)
    def _():
        finish_steps(group, False, core, *refs)


def finish_steps(group, there, core, rest, weights, v_1, v_0, out):
    v = picked(core, v_1, v_0) if there else None
    tok = out.shape[0]
    v_t = [values_and_ones(v, head_columns(g)) for g in range(PAIR)] if there else []
    blocks = [slice(first, first + TILE) for first in range(0, tok, TILE)]

    def multiply(unit, _):
        h, i = unit
        return dot(v_t[h // group], weights[h, :, blocks[i]], 1, 0) if there else None

    def normalise(unit, middle):
        h, i = unit
        total = rest[head_rows(h), blocks[i]]
        if there:
            total += middle
        normal = total[:HEAD_WIDTH] * (1.0 / total[HEAD_WIDTH : HEAD_WIDTH + 1])
        out[blocks[i], head_columns(h)] = normal.astype(jnp.bfloat16).T

    in_steps(units_of(group, tok), [multiply, normalise])


def by_heads(kernel, name, query_shape, columns, place, arrays, kinds, out_kinds):
    tok, width = query_shape
    kv_heads = columns // HEAD_WIDTH
    group = width // columns
    grid = kv_heads // PAIR
    depth = HEAD_WIDTH + ONES
    heads = width // HEAD_WIDTH
    step = heads // grid
    one_group = (tok, columns // grid)
    specs = dict(
        queries=((tok, width), (tok, width // grid), lambda g, *_: (0, g), jnp.bfloat16),
        one=((tok, columns), one_group, lambda g, *_: (0, g), jnp.bfloat16),
        values=((grid, *one_group), (None, *one_group), lambda g, *_: (g, 0, 0), jnp.bfloat16),
        rest=((heads * depth, tok), (step * depth, tok), lambda g, *_: (g, 0), jnp.float32),
        weights=((heads, tok, tok), (step, tok, tok), lambda g, *_: (g, 0, 0), jnp.bfloat16),
        stat=((grid, 8, tok), (1, 8, tok), lambda g, *_: (g, 0, 0), jnp.float32),
    )
    block = lambda kind: pl.BlockSpec(specs[kind][1], specs[kind][2])
    return pl.pallas_call(
        functools.partial(kernel, group),
        grid_spec=pltpu.PrefetchScalarGridSpec(
            num_scalar_prefetch=len(place),
            grid=(grid,),
            in_specs=[block(kind) for kind in kinds],
            out_specs=[block(kind) for kind in out_kinds],
        ),
        out_shape=[jax.ShapeDtypeStruct(specs[kind][0], specs[kind][3]) for kind in out_kinds],
        compiler_params=params(1, 24),
        name=name,
    )(*place, *arrays)


def moved(array, pairs, core):
    count = lax.axis_size("tp")
    return lax.ppermute(
        array,
        ("seq", "tp"),
        [(a * count + t, b * count + t) for a, b in pairs for t in range(core, count, 2)],
    )


def exchanged(array, axis, bit):
    count = lax.axis_size(axis)
    return lax.ppermute(array, axis, [(source, source ^ bit) for source in range(count)])


def on_device(
    normed_input, query, key, value, adapter_down_maps, adapter_up_maps, block_adapter_choice
):
    tok = query.shape[0]
    assert 2 * tok == WINDOW and SEG_LEN % tok == 0
    where = lax.axis_index("seq")
    place = where.reshape(1)
    core = (lax.axis_index("tp") % 2).reshape(1)
    choice = block_adapter_choice

    count = lax.axis_size("seq")
    two_on = [(n, n + 2) for n in range(count - 2)]
    swap = [(n, n ^ 1) for n in range(count)]
    even = where % 2 == 0
    barrier = lax.optimization_barrier
    call = functools.partial(by_heads, query_shape=query.shape, columns=key.shape[1])

    key_far_1 = moved(key, two_on, 1)
    latent = latent_share(place, choice, normed_input.T, adapter_down_maps)
    bit = 1
    while 2 * bit < lax.axis_size("tp"):
        latent = latent + exchanged(latent, "tp", bit)
        bit *= 2
    key_0, latent = barrier((key, latent))
    key_far_0 = moved(key_0, two_on, 0)
    theirs = exchanged(latent, "tp", bit)
    key_mid_1 = moved(jnp.where(even, key_0, key_far_1), swap, 1)
    values = adapt(place, choice, latent, theirs, adapter_up_maps, value)
    value_far_1 = moved(values, two_on, 1)
    value_far_0 = moved(values, two_on, 0)
    key_0, values = barrier((key_0, values))
    key_mid_0 = moved(jnp.where(even, key_0, key_far_0), swap, 0)
    values, key_mid_1 = barrier((values, key_mid_1))
    own, weights_far, tops = call(
        near_far_kernel,
        "near_far",
        place=[place, core],
        arrays=[query, key, values, key_far_1, key_far_0],
        kinds=["queries", "one", "values", "one", "one"],
        out_kinds=["rest", "weights", "stat"],
    )
    values_1, own = barrier((values, own))
    values_0, own = barrier((values, own))
    value_mid_1 = moved(jnp.where(even, values_1, value_far_1), swap, 1)
    value_mid_0 = moved(jnp.where(even, values_0, value_far_0), swap, 0)
    rest, weights_mid = call(
        middle_kernel,
        "middle",
        place=[place, core],
        arrays=[query, own, weights_far, tops, key_mid_1, key_mid_0, value_far_1, value_far_0],
        kinds=["queries", "rest", "weights", "stat", "one", "one", "values", "values"],
        out_kinds=["rest", "weights"],
    )
    return call(
        finish_kernel,
        "finish",
        place=[place, core],
        arrays=[rest, weights_mid, value_mid_1, value_mid_0],
        kinds=["rest", "weights", "values", "values"],
        out_kinds=["queries"],
    )[0]


def solution(mesh):
    placed = (
        P("seq", "tp"),
        P("seq", "tp"),
        P("seq", "tp"),
        P("seq", "tp"),
        P(None, None, "tp"),
        P(None, None, "tp"),
        P(),
    )
    return jax.shard_map(
        on_device, mesh=mesh, in_specs=placed, out_specs=P("seq", "tp"), check_vma=False
    )
```

```python
import functools

import jax
import jax.numpy as jnp
from jax import lax
from jax.experimental import pallas as pl
from jax.experimental.pallas import tpu as pltpu
from jax.sharding import PartitionSpec as P

HEAD_WIDTH = 128
WINDOW = 1024
SEG_LEN = 2048
SCALE = 168.0 ** (-0.5)
LOG2_E = 1.4426950408889634
EXPONENT = SCALE * LOG2_E
MASKED = -1e30
TILE = 256
HALF = 128
ONES = 16
PAIR = 2
PIECE = 256


def params(steps, mib):
    return pltpu.CompilerParams(
        vmem_limit_bytes=mib * 1024 * 1024, dimension_semantics=("arbitrary",) * steps
    )


def dot(left, right, left_dim, right_dim):
    return lax.dot_general(
        left, right, (((left_dim,), (right_dim,)), ((), ())), preferred_element_type=jnp.float32
    )


def in_hbm(array):
    return pltpu.with_memory_space_constraint(array, pltpu.HBM)


def adapter_of(place, choice, tok):
    return choice[lax.div(place[0] * tok, SEG_LEN)]


def latent_kernel(pieces, place, choice, input_t, down, up, out, up_out, rows, map_rows, up_rows, sems):
    chosen = adapter_of(place, choice, out.shape[1])
    copies = [
        pltpu.make_async_copy(down.at[chosen], map_rows, sems.at[0]),
        pltpu.make_async_copy(up.at[chosen], up_rows, sems.at[1]),
    ]
    for n, (first, last) in enumerate(pieces):
        part = pl.ds(first, last - first)
        copies.append(pltpu.make_async_copy(input_t.at[part], rows.at[part], sems.at[n + 2]))
    for copy in copies:
        copy.start()
    copies[0].wait()
    total = None
    for (first, last), copy in zip(pieces, copies[2:]):
        copy.wait()
        product = dot(map_rows[:, first:last], rows[first:last, :], 1, 0)
        total = product if total is None else total + product
    out[...] = total
    copies[1].wait()
    up_out[...] = up_rows[...]


def latent_share(place, choice, input_t, down_maps, up_maps):
    features, tok = input_t.shape
    rank, columns = up_maps.shape[1:]
    pieces = [(first, min(first + PIECE, features)) for first in range(0, features, PIECE)]
    whole = lambda i, *_: (0, 0)
    return pl.pallas_call(
        functools.partial(latent_kernel, pieces),
        grid_spec=pltpu.PrefetchScalarGridSpec(
            num_scalar_prefetch=2,
            grid=(1,),
            in_specs=[pl.BlockSpec(memory_space=pltpu.HBM)] * 3,
            out_specs=[pl.BlockSpec((rank, tok), whole), pl.BlockSpec((rank, columns), whole)],
            scratch_shapes=[
                pltpu.VMEM((features, tok), input_t.dtype),
                pltpu.VMEM((rank, features), down_maps.dtype),
                pltpu.VMEM((rank, columns), up_maps.dtype),
                pltpu.SemaphoreType.DMA((len(pieces) + 2,)),
            ],
        ),
        out_shape=[
            jax.ShapeDtypeStruct((rank, tok), jnp.float32),
            jax.ShapeDtypeStruct((rank, columns), up_maps.dtype),
        ],
        compiler_params=params(1, 8),
        name="latent_share",
    )(place, in_hbm(choice), in_hbm(input_t), in_hbm(down_maps), in_hbm(up_maps))


def adapt_kernel(mine, theirs, up, value, out):
    latent = (mine[...] + theirs[...]).astype(jnp.bfloat16)
    update = dot(latent, up[...], 0, 0)
    total = (value[...].astype(jnp.float32) + update).astype(jnp.bfloat16)
    parts, _, width = out.shape
    for n in range(parts):
        out[n] = total[:, n * width : (n + 1) * width]


def adapt(mine, theirs, up, value):
    tok, columns = value.shape
    shape = (columns // (PAIR * HEAD_WIDTH), tok, PAIR * HEAD_WIDTH)
    return pl.pallas_call(
        adapt_kernel,
        out_shape=jax.ShapeDtypeStruct(shape, jnp.bfloat16),
        compiler_params=pltpu.CompilerParams(vmem_limit_bytes=8 * 1024 * 1024),
        name="adapt_values",
    )(mine, theirs, up, value)


def weights_of(scores, top):
    return jnp.exp2(((scores - top) * EXPONENT).astype(jnp.bfloat16))


def tree(operation, items):
    items = list(items)
    while len(items) > 1:
        items = [
            operation(items[n], items[n + 1]) if n + 1 < len(items) else items[n]
            for n in range(0, len(items), 2)
        ]
    return items[0]


def top_of(scores):
    pieces = [s[n : n + 32] for s in scores for n in range(0, s.shape[0], 32)]
    pieces = tree(jnp.maximum, pieces)
    pieces = tree(jnp.maximum, [pieces[n : n + 8] for n in range(0, 32, 8)])
    return jnp.max(pieces, axis=0, keepdims=True)


def values_and_ones(v, columns):
    turned = v[:, columns].T
    return jnp.concatenate([turned, jnp.ones((ONES, v.shape[0]), jnp.bfloat16)], axis=0)


def head_rows(h):
    return slice(h * (HEAD_WIDTH + ONES), (h + 1) * (HEAD_WIDTH + ONES))


def head_columns(h):
    return slice(h * HEAD_WIDTH, (h + 1) * HEAD_WIDTH)


def in_steps(units, stages):
    held = [None] * len(units)
    for step in range(len(units) + len(stages) - 1):
        for n, stage in enumerate(stages):
            if 0 <= step - n < len(units):
                held[step - n] = stage(units[step - n], held[step - n])


def units_of(group, tok):
    return [(h, i) for g in range(PAIR) for i in range(tok // TILE) for h in range(g * group, (g + 1) * group)]


def near_far_kernel(group, place, *refs):
    @pl.when(place[0] >= 2)
    def _():
        near_far_steps(group, True, *refs)

    @pl.when(place[0] < 2)
    def _():
        near_far_steps(group, False, *refs)


def near_far_steps(group, far_there, q, k, v, k_far, out, weights_far, tops):
    tok = q.shape[0]
    causal = lax.broadcasted_iota(jnp.int32, (HALF, HALF), 0) <= lax.broadcasted_iota(
        jnp.int32, (HALF, HALF), 1
    )
    v_t = [values_and_ones(v, head_columns(g)) for g in range(PAIR)]
    nothing = jnp.zeros((HALF, HALF), jnp.bfloat16)
    tiles = tok // TILE
    blocks = [slice(i * TILE, (i + 1) * TILE) for i in range(tiles)]

    def score(unit, _):
        h, i = unit
        qh = q[blocks[i], head_columns(h)]
        columns = head_columns(h // group)
        near = [dot(k[blocks[j], columns], qh, 1, 1) for j in range(i + 1)]
        far = []
        if far_there:
            far = [dot(k_far[blocks[j], columns], qh, 1, 1) for j in range(i, tiles)]
        return near, far

    def weigh(unit, scores):
        h, i = unit
        near, far = scores
        near_columns, far_columns = [], []
        for half in range(2):
            a = slice(half * HALF, (half + 1) * HALF)
            near_edge = near[i][: (half + 1) * HALF, a]
            near_pieces = [s[:, a] for s in near[:i]]
            if half == 1:
                near_pieces.append(near_edge[:HALF])
            near_pieces.append(jnp.where(causal, near_edge[half * HALF :], MASKED))
            far_pieces = []
            if far_there:
                far_edge = far[0][half * HALF :, a]
                far_pieces.append(jnp.where(causal, MASKED, far_edge[:HALF]))
                if half == 0:
                    far_pieces.append(far_edge[HALF:])
                far_pieces += [s[:, a] for s in far[1:]]
            top = top_of(near_pieces + far_pieces)
            near_weights = [weights_of(s, top) for s in near_pieces]
            if half == 0:
                near_weights.append(nothing)
            near_columns.append(jnp.concatenate(near_weights, axis=0))
            if far_there:
                far_weights = [weights_of(s, top) for s in far_pieces]
                if half == 1:
                    far_weights.insert(0, nothing)
                far_columns.append(jnp.concatenate(far_weights, axis=0))
            queries = slice(i * TILE + half * HALF, i * TILE + (half + 1) * HALF)
            tops[0, h : h + 1, queries] = top
        if far_there:
            weights_far[h, i * TILE :, blocks[i]] = jnp.concatenate(far_columns, axis=1)
        return jnp.concatenate(near_columns, axis=1)

    def multiply(unit, weights):
        h, i = unit
        out[head_rows(h), blocks[i]] = dot(v_t[h // group][:, : (i + 1) * TILE], weights, 1, 0)

    in_steps(units_of(group, tok), [score, weigh, multiply])


def middle_kernel(group, place, *refs):
    @pl.when(place[0] >= 2)
    def _():
        middle_steps(group, True, *refs)

    @pl.when(place[0] == 1)
    def _():
        middle_steps(group, False, *refs)

    @pl.when(place[0] == 0)
    def _():
        q, own, out, stage, sems = refs[0], refs[1], refs[8], refs[9], refs[10]
        write_steps(group, pl.program_id(0), q.shape[0], lambda h, b: own[head_rows(h), b], out, stage, sems)


def middle_steps(group, far_there, q, own, weights_far, tops, k, v_far, rest, weights, *_):
    tok = q.shape[0]
    v_t = [values_and_ones(v_far, head_columns(g)) for g in range(PAIR)] if far_there else []
    tiles = tok // TILE
    blocks = [slice(i * TILE, (i + 1) * TILE) for i in range(tiles)]

    def score(unit, _):
        h, i = unit
        qh = q[blocks[i], head_columns(h)]
        return [dot(k[blocks[j], head_columns(h // group)], qh, 1, 1) for j in range(tiles)]

    def weigh(unit, scores):
        h, i = unit
        before = tops[0, h : h + 1, blocks[i]]
        top = jnp.maximum(before, top_of(scores))
        for j, s in enumerate(scores):
            weights[h, blocks[j], blocks[i]] = weights_of(s, top)
        return jnp.exp2((before - top) * EXPONENT)

    def multiply(unit, less):
        h, i = unit
        total = own[head_rows(h), blocks[i]]
        if far_there:
            total += dot(v_t[h // group][:, i * TILE :], weights_far[h, i * TILE :, blocks[i]], 1, 0)
        rest[head_rows(h), blocks[i]] = total * less

    in_steps(units_of(group, tok), [score, weigh, multiply])


def write_steps(group, step, tok, total_of, out, stage, sems):
    units = units_of(group, tok)
    copies = []
    for n, (h, i) in enumerate(units):
        b = slice(i * TILE, (i + 1) * TILE)
        total = total_of(h, b)
        normal = total[:HEAD_WIDTH] * (1.0 / total[HEAD_WIDTH : HEAD_WIDTH + 1])
        stage[b, head_columns(h)] = normal.astype(jnp.bfloat16).T
        if h % group == group - 1:
            first = (h + 1 - group) * HEAD_WIDTH
            width = group * HEAD_WIDTH
            target = pl.ds(pl.multiple_of(step * stage.shape[1] + first, HEAD_WIDTH), width)
            copies.append(
                pltpu.make_async_copy(
                    stage.at[pl.ds(i * TILE, TILE), pl.ds(first, width)],
                    out.at[pl.ds(i * TILE, TILE), target],
                    sems.at[len(copies)],
                )
            )
            copies[-1].start()
    for copy in copies:
        copy.wait()


def finish_kernel(group, place, rest, weights, v, _, out, stage, sems, step):
    tok = weights.shape[1]

    @pl.when(place[0] >= 1)
    def _():
        v_t = [values_and_ones(v, head_columns(g)) for g in range(PAIR)]
        held = {}

        def total_of(h, b):
            units = [(m, i) for m, i in units_of(group, tok)]
            at = units.index((h, b.start // TILE))
            for m, i in units[len(held) : at + 2]:
                c = slice(i * TILE, (i + 1) * TILE)
                held[m, i] = dot(v_t[m // group], weights[m, :, c], 1, 0)
            return rest[head_rows(h), b] + held[h, b.start // TILE]

        write_steps(group, step, tok, total_of, out, stage, sems)


def by_heads(
    kernel, name, query_shape, columns, place, arrays, kinds, out_kinds, only=None, into=None
):
    tok, width = query_shape
    kv_heads = columns // HEAD_WIDTH
    group = width // columns
    grid = kv_heads // PAIR
    depth = HEAD_WIDTH + ONES
    heads = width // HEAD_WIDTH
    step = heads // grid
    at = (lambda g: g) if only is None else (lambda g: only)
    one_group = (tok, columns // grid)
    specs = dict(
        queries=((tok, width), (tok, width // grid), lambda g, *_: (0, at(g)), jnp.bfloat16),
        one=((tok, columns), one_group, lambda g, *_: (0, at(g)), jnp.bfloat16),
        values=((grid, *one_group), (None, *one_group), lambda g, *_: (at(g), 0, 0), jnp.bfloat16),
        alone=(one_group, one_group, lambda g, *_: (0, 0), jnp.bfloat16),
        rest=((heads * depth, tok), (step * depth, tok), lambda g, *_: (at(g), 0), jnp.float32),
        weights=((heads, tok, tok), (step, tok, tok), lambda g, *_: (at(g), 0, 0), jnp.bfloat16),
        stat=((grid, 8, tok), (1, 8, tok), lambda g, *_: (at(g), 0, 0), jnp.float32),
        output=((tok, width), None, None, jnp.bfloat16),
    )

    def block(kind):
        if kind == "output":
            return pl.BlockSpec(memory_space=pl.ANY)
        return pl.BlockSpec(specs[kind][1], specs[kind][2])

    aliases, scratch = {}, []
    if into is not None:
        aliases = {len(place) + len(arrays): out_kinds.index("output")}
        arrays, kinds = [*arrays, into], [*kinds, "output"]
    if "output" in out_kinds:
        copies = PAIR * tok // TILE
        scratch = [
            pltpu.VMEM((tok, width // grid), jnp.bfloat16),
            pltpu.SemaphoreType.DMA((copies,)),
        ]
    return pl.pallas_call(
        functools.partial(kernel, group),
        grid_spec=pltpu.PrefetchScalarGridSpec(
            num_scalar_prefetch=len(place),
            grid=(grid if only is None else 1,),
            in_specs=[block(kind) for kind in kinds],
            out_specs=[block(kind) for kind in out_kinds],
            scratch_shapes=scratch,
        ),
        out_shape=[jax.ShapeDtypeStruct(specs[kind][0], specs[kind][3]) for kind in out_kinds],
        input_output_aliases=aliases,
        compiler_params=params(1, 24),
        name=name,
    )(*place, *arrays)


def shifted(array, steps):
    count = lax.axis_size("seq")
    return lax.ppermute(array, "seq", [(source, source + steps) for source in range(count - steps)])


def exchanged(array, axis, bit):
    count = lax.axis_size(axis)
    return lax.ppermute(array, axis, [(source, source ^ bit) for source in range(count)])


def on_device(
    normed_input, query, key, value, adapter_down_maps, adapter_up_maps, block_adapter_choice
):
    tok = query.shape[0]
    assert 2 * tok == WINDOW and SEG_LEN % tok == 0
    where = lax.axis_index("seq")
    place = where.reshape(1)
    choice = block_adapter_choice

    key_far = shifted(key, 2)
    latent, up = latent_share(place, choice, normed_input.T, adapter_down_maps, adapter_up_maps)
    bit = 1
    while 2 * bit < lax.axis_size("tp"):
        latent = latent + exchanged(latent, "tp", bit)
        bit *= 2
    theirs = exchanged(latent, "tp", bit)
    values = adapt(latent, theirs, up, value)
    value_far = shifted(values, 2)

    def from_one_back(own, far):
        return exchanged(jnp.where(where % 2 == 0, own, far), "seq", 1)

    call = functools.partial(by_heads, query_shape=query.shape, columns=key.shape[1])
    key_own, _ = lax.optimization_barrier((key, values))
    key_mid = from_one_back(key_own, key_far)
    own, weights_far, tops = call(
        near_far_kernel,
        "near_far",
        place=[place],
        arrays=[query, key, values, key_far],
        kinds=["queries", "one", "values", "one"],
        out_kinds=["rest", "weights", "stat"],
    )
    values, own = lax.optimization_barrier((values, own))
    value_mid = from_one_back(values[0], value_far[0])
    rest, weights_mid, done = call(
        middle_kernel,
        "middle",
        place=[place],
        arrays=[query, own, weights_far, tops, key_mid, value_far],
        kinds=["queries", "rest", "weights", "stat", "one", "values"],
        out_kinds=["rest", "weights", "output"],
    )
    values, value_far, rest = lax.optimization_barrier((values, value_far, rest))
    for n in range(values.shape[0]):
        if n > 0:
            value_mid = from_one_back(values[n], value_far[n])
        [done] = call(
            functools.partial(finish_kernel, step=n),
            "finish",
            place=[place],
            arrays=[rest, weights_mid, value_mid],
            kinds=["rest", "weights", "alone"],
            out_kinds=["output"],
            only=n,
            into=done,
        )
    return done


def solution(mesh):
    placed = (
        P("seq", "tp"),
        P("seq", "tp"),
        P("seq", "tp"),
        P("seq", "tp"),
        P(None, None, "tp"),
        P(None, None, "tp"),
        P(),
    )
    return jax.shard_map(
        on_device, mesh=mesh, in_specs=placed, out_specs=P("seq", "tp"), check_vma=False
    )
```

```python
import functools

import jax
import jax.numpy as jnp
from jax import lax
from jax.experimental import pallas as pl
from jax.experimental.pallas import tpu as pltpu
from jax.sharding import PartitionSpec as P

HEAD_WIDTH = 128
WINDOW = 1024
SEG_LEN = 2048
SCALE = 168.0 ** (-0.5)
LOG2_E = 1.4426950408889634
EXPONENT = SCALE * LOG2_E
MASKED = -1e30
TILE = 256
HALF = 128
ONES = 16
PAIR = 2
PIECE = 256


def params(steps, mib):
    return pltpu.CompilerParams(
        vmem_limit_bytes=mib * 1024 * 1024, dimension_semantics=("arbitrary",) * steps
    )


def dot(left, right, left_dim, right_dim):
    return lax.dot_general(
        left, right, (((left_dim,), (right_dim,)), ((), ())), preferred_element_type=jnp.float32
    )


def in_hbm(array):
    return pltpu.with_memory_space_constraint(array, pltpu.HBM)


def adapter_of(place, choice, tok):
    return choice[lax.div(place[0] * tok, SEG_LEN)]


def latent_kernel(pieces, place, choice, input_t, down, up, out, up_out, rows, map_rows, up_rows, sems):
    chosen = adapter_of(place, choice, out.shape[1])
    copies = [
        pltpu.make_async_copy(down.at[chosen], map_rows, sems.at[0]),
        pltpu.make_async_copy(up.at[chosen], up_rows, sems.at[1]),
    ]
    for n, (first, last) in enumerate(pieces):
        part = pl.ds(first, last - first)
        copies.append(pltpu.make_async_copy(input_t.at[part], rows.at[part], sems.at[n + 2]))
    for copy in copies:
        copy.start()
    copies[0].wait()
    total = None
    for (first, last), copy in zip(pieces, copies[2:]):
        copy.wait()
        product = dot(map_rows[:, first:last], rows[first:last, :], 1, 0)
        total = product if total is None else total + product
    out[...] = total
    copies[1].wait()
    up_out[...] = up_rows[...]


def latent_share(place, choice, input_t, down_maps, up_maps):
    features, tok = input_t.shape
    rank, columns = up_maps.shape[1:]
    pieces = [(first, min(first + PIECE, features)) for first in range(0, features, PIECE)]
    whole = lambda i, *_: (0, 0)
    return pl.pallas_call(
        functools.partial(latent_kernel, pieces),
        grid_spec=pltpu.PrefetchScalarGridSpec(
            num_scalar_prefetch=2,
            grid=(1,),
            in_specs=[pl.BlockSpec(memory_space=pltpu.HBM)] * 3,
            out_specs=[pl.BlockSpec((rank, tok), whole), pl.BlockSpec((rank, columns), whole)],
            scratch_shapes=[
                pltpu.VMEM((features, tok), input_t.dtype),
                pltpu.VMEM((rank, features), down_maps.dtype),
                pltpu.VMEM((rank, columns), up_maps.dtype),
                pltpu.SemaphoreType.DMA((len(pieces) + 2,)),
            ],
        ),
        out_shape=[
            jax.ShapeDtypeStruct((rank, tok), jnp.float32),
            jax.ShapeDtypeStruct((rank, columns), up_maps.dtype),
        ],
        compiler_params=params(1, 8),
        name="latent_share",
    )(place, in_hbm(choice), in_hbm(input_t), in_hbm(down_maps), in_hbm(up_maps))


def adapt_kernel(mine, theirs, up, value, out):
    latent = (mine[...] + theirs[...]).astype(jnp.bfloat16)
    update = dot(latent, up[...], 0, 0)
    total = (value[...].astype(jnp.float32) + update).astype(jnp.bfloat16)
    parts, _, width = out.shape
    for n in range(parts):
        out[n] = total[:, n * width : (n + 1) * width]


def adapt(mine, theirs, up, value):
    tok, columns = value.shape
    shape = (columns // (PAIR * HEAD_WIDTH), tok, PAIR * HEAD_WIDTH)
    return pl.pallas_call(
        adapt_kernel,
        out_shape=jax.ShapeDtypeStruct(shape, jnp.bfloat16),
        compiler_params=pltpu.CompilerParams(vmem_limit_bytes=8 * 1024 * 1024),
        name="adapt_values",
    )(mine, theirs, up, value)


def weights_of(scores, top):
    return jnp.exp2(((scores - top) * EXPONENT).astype(jnp.bfloat16))


def tree(operation, items):
    items = list(items)
    while len(items) > 1:
        items = [
            operation(items[n], items[n + 1]) if n + 1 < len(items) else items[n]
            for n in range(0, len(items), 2)
        ]
    return items[0]


def top_of(scores):
    pieces = [s[n : n + 32] for s in scores for n in range(0, s.shape[0], 32)]
    pieces = tree(jnp.maximum, pieces)
    pieces = tree(jnp.maximum, [pieces[n : n + 8] for n in range(0, 32, 8)])
    return jnp.max(pieces, axis=0, keepdims=True)


def values_and_ones(v, columns):
    turned = v[:, columns].T
    return jnp.concatenate([turned, jnp.ones((ONES, v.shape[0]), jnp.bfloat16)], axis=0)


def head_rows(h):
    return slice(h * (HEAD_WIDTH + ONES), (h + 1) * (HEAD_WIDTH + ONES))


def head_columns(h):
    return slice(h * HEAD_WIDTH, (h + 1) * HEAD_WIDTH)


def in_steps(units, stages):
    held = [None] * len(units)
    for step in range(len(units) + len(stages) - 1):
        for n, stage in enumerate(stages):
            if 0 <= step - n < len(units):
                held[step - n] = stage(units[step - n], held[step - n])


def units_of(group, tok, kv_heads):
    return [
        (h, i)
        for g in kv_heads
        for i in range(tok // TILE)
        for h in range(g * group, (g + 1) * group)
    ]


def near_far_kernel(group, place, *refs):
    @pl.when(place[0] >= 2)
    def _():
        near_far_steps(group, True, *refs)

    @pl.when(place[0] < 2)
    def _():
        near_far_steps(group, False, *refs)


def near_far_steps(group, far_there, q, k, v, k_far, out, weights_far, tops):
    tok = q.shape[0]
    kv_heads = range(k.shape[1] // HEAD_WIDTH)
    causal = lax.broadcasted_iota(jnp.int32, (HALF, HALF), 0) <= lax.broadcasted_iota(
        jnp.int32, (HALF, HALF), 1
    )
    v_t = [values_and_ones(v[g // PAIR], head_columns(g % PAIR)) for g in kv_heads]
    nothing = jnp.zeros((HALF, HALF), jnp.bfloat16)
    tiles = tok // TILE
    blocks = [slice(i * TILE, (i + 1) * TILE) for i in range(tiles)]

    def score(unit, _):
        h, i = unit
        qh = q[blocks[i], head_columns(h)]
        columns = head_columns(h // group)
        near = [dot(k[blocks[j], columns], qh, 1, 1) for j in range(i + 1)]
        far = []
        if far_there:
            far = [dot(k_far[blocks[j], columns], qh, 1, 1) for j in range(i, tiles)]
        return near, far

    def weigh(unit, scores):
        h, i = unit
        near, far = scores
        near_columns, far_columns = [], []
        for half in range(2):
            a = slice(half * HALF, (half + 1) * HALF)
            near_edge = near[i][: (half + 1) * HALF, a]
            near_pieces = [s[:, a] for s in near[:i]]
            if half == 1:
                near_pieces.append(near_edge[:HALF])
            near_pieces.append(jnp.where(causal, near_edge[half * HALF :], MASKED))
            far_pieces = []
            if far_there:
                far_edge = far[0][half * HALF :, a]
                far_pieces.append(jnp.where(causal, MASKED, far_edge[:HALF]))
                if half == 0:
                    far_pieces.append(far_edge[HALF:])
                far_pieces += [s[:, a] for s in far[1:]]
            top = top_of(near_pieces + far_pieces)
            near_weights = [weights_of(s, top) for s in near_pieces]
            if half == 0:
                near_weights.append(nothing)
            near_columns.append(jnp.concatenate(near_weights, axis=0))
            if far_there:
                far_weights = [weights_of(s, top) for s in far_pieces]
                if half == 1:
                    far_weights.insert(0, nothing)
                far_columns.append(jnp.concatenate(far_weights, axis=0))
            queries = slice(i * TILE + half * HALF, i * TILE + (half + 1) * HALF)
            tops[h : h + 1, queries] = top
        if far_there:
            weights_far[h, i * TILE :, blocks[i]] = jnp.concatenate(far_columns, axis=1)
        return jnp.concatenate(near_columns, axis=1)

    def multiply(unit, weights):
        h, i = unit
        out[head_rows(h), blocks[i]] = dot(v_t[h // group][:, : (i + 1) * TILE], weights, 1, 0)

    in_steps(units_of(group, tok, kv_heads), [score, weigh, multiply])


def middle_kernel(group, place, *refs):
    @pl.when(place[0] >= 2)
    def _():
        middle_steps(group, True, *refs)

    @pl.when(place[0] == 1)
    def _():
        middle_steps(group, False, *refs)

    @pl.when(place[0] == 0)
    def _():
        q, own, k, out, stage, sems = refs[0], refs[1], refs[4], refs[8], refs[9], refs[10]
        kv_heads = range(k.shape[1] // HEAD_WIDTH)
        write_steps(
            group, kv_heads, q.shape[0], lambda h, b: own[head_rows(h), b], out, stage, sems
        )


def middle_steps(group, far_there, q, own, weights_far, tops, k, v_far, rest, weights, *_):
    tok = q.shape[0]
    kv_heads = range(k.shape[1] // HEAD_WIDTH)
    v_t = []
    if far_there:
        v_t = [values_and_ones(v_far[g // PAIR], head_columns(g % PAIR)) for g in kv_heads]
    tiles = tok // TILE
    blocks = [slice(i * TILE, (i + 1) * TILE) for i in range(tiles)]

    def score(unit, _):
        h, i = unit
        qh = q[blocks[i], head_columns(h)]
        return [dot(k[blocks[j], head_columns(h // group)], qh, 1, 1) for j in range(tiles)]

    def weigh(unit, scores):
        h, i = unit
        before = tops[h : h + 1, blocks[i]]
        top = jnp.maximum(before, top_of(scores))
        for j, s in enumerate(scores):
            weights[h, blocks[j], blocks[i]] = weights_of(s, top)
        return jnp.exp2((before - top) * EXPONENT)

    def multiply(unit, less):
        h, i = unit
        total = own[head_rows(h), blocks[i]]
        if far_there:
            total += dot(v_t[h // group][:, i * TILE :], weights_far[h, i * TILE :, blocks[i]], 1, 0)
        rest[head_rows(h), blocks[i]] = total * less

    in_steps(units_of(group, tok, kv_heads), [score, weigh, multiply])


def write_steps(group, kv_heads, tok, total_of, out, stage, sems):
    copies = []
    for h, i in units_of(group, tok, kv_heads):
        b = slice(i * TILE, (i + 1) * TILE)
        total = total_of(h, b)
        normal = total[:HEAD_WIDTH] * (1.0 / total[HEAD_WIDTH : HEAD_WIDTH + 1])
        stage[b, head_columns(h)] = normal.astype(jnp.bfloat16).T
        if h % group == group - 1:
            width = group * HEAD_WIDTH
            part = (pl.ds(i * TILE, TILE), pl.ds((h + 1) * HEAD_WIDTH - width, width))
            copies.append(
                pltpu.make_async_copy(stage.at[part], out.at[part], sems.at[len(copies)])
            )
            copies[-1].start()
    for copy in copies:
        copy.wait()


def finish_kernel(group, place, rest, weights, v, _, out, stage, sems, part):
    tok = weights.shape[1]
    kv_heads = range(part * PAIR, (part + 1) * PAIR)

    @pl.when(place[0] >= 1)
    def _():
        v_t = [values_and_ones(v, head_columns(g % PAIR)) for g in kv_heads]
        units = units_of(group, tok, kv_heads)
        held = []

        def total_of(h, b):
            at = units.index((h, b.start // TILE))
            for m, i in units[len(held) : at + 2]:
                c = slice(i * TILE, (i + 1) * TILE)
                held.append(dot(v_t[m // group - part * PAIR], weights[m, :, c], 1, 0))
            return rest[head_rows(h), b] + held[at]

        write_steps(group, kv_heads, tok, total_of, out, stage, sems)


def by_heads(kernel, name, query_shape, columns, place, arrays, out_kinds, into=None):
    tok, width = query_shape
    heads = width // HEAD_WIDTH
    shapes = dict(
        rest=((heads * (HEAD_WIDTH + ONES), tok), jnp.float32),
        weights=((heads, tok, tok), jnp.bfloat16),
        stat=((heads, tok), jnp.float32),
        output=((tok, width), jnp.bfloat16),
    )
    in_vmem, anywhere = pl.BlockSpec(memory_space=pltpu.VMEM), pl.BlockSpec(memory_space=pl.ANY)
    in_specs = [pl.BlockSpec(memory_space=pltpu.SMEM)] + [in_vmem] * len(arrays)
    arrays = [place, *arrays]
    aliases, scratch = {}, []
    if into is not None:
        aliases = {len(arrays): out_kinds.index("output")}
        arrays.append(into)
        in_specs.append(anywhere)
    if "output" in out_kinds:
        copies = columns // HEAD_WIDTH * (tok // TILE)
        scratch = [
            pltpu.VMEM((tok, width), jnp.bfloat16),
            pltpu.SemaphoreType.DMA((copies,)),
        ]
    return pl.pallas_call(
        functools.partial(kernel, width // columns),
        in_specs=in_specs,
        out_specs=[anywhere if kind == "output" else in_vmem for kind in out_kinds],
        scratch_shapes=scratch,
        out_shape=[jax.ShapeDtypeStruct(*shapes[kind]) for kind in out_kinds],
        input_output_aliases=aliases,
        compiler_params=pltpu.CompilerParams(vmem_limit_bytes=24 * 1024 * 1024),
        name=name,
    )(*arrays)


def shifted(array, steps):
    count = lax.axis_size("seq")
    return lax.ppermute(array, "seq", [(source, source + steps) for source in range(count - steps)])


def exchanged(array, axis, bit):
    count = lax.axis_size(axis)
    return lax.ppermute(array, axis, [(source, source ^ bit) for source in range(count)])


def on_device(
    normed_input, query, key, value, adapter_down_maps, adapter_up_maps, block_adapter_choice
):
    tok = query.shape[0]
    assert 2 * tok == WINDOW and SEG_LEN % tok == 0
    where = lax.axis_index("seq")
    place = where.reshape(1)
    choice = block_adapter_choice

    key_far = shifted(key, 2)
    latent, up = latent_share(place, choice, normed_input.T, adapter_down_maps, adapter_up_maps)
    bit = 1
    while 2 * bit < lax.axis_size("tp"):
        latent = latent + exchanged(latent, "tp", bit)
        bit *= 2
    theirs = exchanged(latent, "tp", bit)
    values = adapt(latent, theirs, up, value)
    value_far = shifted(values, 2)

    def from_one_back(own, far):
        return exchanged(jnp.where(where % 2 == 0, own, far), "seq", 1)

    call = functools.partial(by_heads, query_shape=query.shape, columns=key.shape[1])
    key_own, _ = lax.optimization_barrier((key, values))
    key_mid = from_one_back(key_own, key_far)
    own, weights_far, tops = call(
        near_far_kernel,
        "near_far",
        place=place,
        arrays=[query, key, values, key_far],
        out_kinds=["rest", "weights", "stat"],
    )
    values, own = lax.optimization_barrier((values, own))
    value_mid = from_one_back(values[0], value_far[0])
    rest, weights_mid, done = call(
        middle_kernel,
        "middle",
        place=place,
        arrays=[query, own, weights_far, tops, key_mid, value_far],
        out_kinds=["rest", "weights", "output"],
    )
    values, value_far, rest = lax.optimization_barrier((values, value_far, rest))
    for n in range(values.shape[0]):
        if n > 0:
            value_mid = from_one_back(values[n], value_far[n])
        [done] = call(
            functools.partial(finish_kernel, part=n),
            "finish",
            place=place,
            arrays=[rest, weights_mid, value_mid],
            out_kinds=["output"],
            into=done,
        )
    return done


def solution(mesh):
    placed = (
        P("seq", "tp"),
        P("seq", "tp"),
        P("seq", "tp"),
        P("seq", "tp"),
        P(None, None, "tp"),
        P(None, None, "tp"),
        P(),
    )
    return jax.shard_map(
        on_device, mesh=mesh, in_specs=placed, out_specs=P("seq", "tp"), check_vma=False
    )
```

```python
import functools

import jax
import jax.numpy as jnp
from jax import lax
from jax.experimental import pallas as pl
from jax.experimental.pallas import tpu as pltpu
from jax.sharding import PartitionSpec as P

HEAD_WIDTH = 128
WINDOW = 1024
SEG_LEN = 2048
SCALE = 168.0 ** (-0.5)
LOG2_E = 1.4426950408889634
EXPONENT = SCALE * LOG2_E
MASKED = -1e30
TILE = 256
HALF = 128
ONES = 16
PAIR = 2
PIECE = 256


def params(steps, mib):
    return pltpu.CompilerParams(
        vmem_limit_bytes=mib * 1024 * 1024, dimension_semantics=("arbitrary",) * steps
    )


def dot(left, right, left_dim, right_dim):
    return lax.dot_general(
        left, right, (((left_dim,), (right_dim,)), ((), ())), preferred_element_type=jnp.float32
    )


def in_hbm(array):
    return pltpu.with_memory_space_constraint(array, pltpu.HBM)


def adapter_of(place, choice, tok):
    return choice[lax.div(place[0] * tok, SEG_LEN)]


def first_half_kernel(key, out, sem):
    copy = pltpu.make_async_copy(key.at[pl.ds(0, out.shape[0])], out, sem)
    copy.start()
    copy.wait()


def first_half(key):
    rows, columns = key.shape
    return pl.pallas_call(
        first_half_kernel,
        in_specs=[pl.BlockSpec(memory_space=pltpu.HBM)],
        out_specs=pl.BlockSpec(memory_space=pltpu.VMEM),
        out_shape=jax.ShapeDtypeStruct((rows // 2, columns), key.dtype),
        scratch_shapes=[pltpu.SemaphoreType.DMA],
        compiler_params=pltpu.CompilerParams(vmem_limit_bytes=8 * 1024 * 1024),
        name="first_half",
    )(in_hbm(key))


def latent_kernel(
    pieces, place, choice, input_t, down, up, key, out, up_out, key_out, rows, map_rows, sems
):
    chosen = adapter_of(place, choice, out.shape[1])
    half = key_out.shape[0]
    copies = [
        pltpu.make_async_copy(down.at[chosen], map_rows, sems.at[0]),
        pltpu.make_async_copy(up.at[chosen], up_out, sems.at[1]),
        pltpu.make_async_copy(key.at[pl.ds(half, half)], key_out, sems.at[2]),
    ]
    for n, (first, last) in enumerate(pieces):
        part = pl.ds(first, last - first)
        copies.append(pltpu.make_async_copy(input_t.at[part], rows.at[part], sems.at[n + 3]))
    for copy in copies:
        copy.start()
    copies[0].wait()
    total = None
    for (first, last), copy in zip(pieces, copies[3:]):
        copy.wait()
        product = dot(map_rows[:, first:last], rows[first:last, :], 1, 0)
        total = product if total is None else total + product
    out[...] = total
    copies[1].wait()
    copies[2].wait()


def latent_share(place, choice, input_t, down_maps, up_maps, key):
    features, tok = input_t.shape
    rank, columns = up_maps.shape[1:]
    pieces = [(first, min(first + PIECE, features)) for first in range(0, features, PIECE)]
    in_smem, in_vmem = pl.BlockSpec(memory_space=pltpu.SMEM), pl.BlockSpec(memory_space=pltpu.VMEM)
    return pl.pallas_call(
        functools.partial(latent_kernel, pieces),
        in_specs=[in_smem] * 2 + [pl.BlockSpec(memory_space=pltpu.HBM)] * 4,
        out_specs=[in_vmem] * 3,
        out_shape=[
            jax.ShapeDtypeStruct((rank, tok), jnp.float32),
            jax.ShapeDtypeStruct((rank, columns), up_maps.dtype),
            jax.ShapeDtypeStruct((tok // 2, columns), key.dtype),
        ],
        scratch_shapes=[
            pltpu.VMEM((features, tok), input_t.dtype),
            pltpu.VMEM((rank, features), down_maps.dtype),
            pltpu.SemaphoreType.DMA((len(pieces) + 3,)),
        ],
        compiler_params=pltpu.CompilerParams(vmem_limit_bytes=8 * 1024 * 1024),
        name="latent_share",
    )(place, *(in_hbm(array) for array in (choice, input_t, down_maps, up_maps, key)))


def adapt_kernel(mine, theirs, up, value, *outs):
    latent = (mine[...] + theirs[...]).astype(jnp.bfloat16)
    update = dot(latent, up[...], 0, 0)
    total = (value[...].astype(jnp.float32) + update).astype(jnp.bfloat16)
    for n, out in enumerate(outs):
        width = out.shape[1]
        out[...] = total[:, n * width : (n + 1) * width]


def adapt(mine, theirs, up, value):
    tok, columns = value.shape
    width = PAIR * HEAD_WIDTH
    return pl.pallas_call(
        adapt_kernel,
        out_shape=[jax.ShapeDtypeStruct((tok, width), jnp.bfloat16)] * (columns // width),
        compiler_params=pltpu.CompilerParams(vmem_limit_bytes=8 * 1024 * 1024),
        name="adapt_values",
    )(mine, theirs, up, value)


def weights_of(scores, top):
    return jnp.exp2(((scores - top) * EXPONENT).astype(jnp.bfloat16))


def tree(operation, items):
    items = list(items)
    while len(items) > 1:
        items = [
            operation(items[n], items[n + 1]) if n + 1 < len(items) else items[n]
            for n in range(0, len(items), 2)
        ]
    return items[0]


def top_of(scores):
    pieces = [s[n : n + 32] for s in scores for n in range(0, s.shape[0], 32)]
    pieces = tree(jnp.maximum, pieces)
    pieces = tree(jnp.maximum, [pieces[n : n + 8] for n in range(0, 32, 8)])
    return jnp.max(pieces, axis=0, keepdims=True)


def values_and_ones(v, columns):
    turned = v[:, columns].T
    return jnp.concatenate([turned, jnp.ones((ONES, v.shape[0]), jnp.bfloat16)], axis=0)


def tile(halves, j, columns):
    rows = halves[0].shape[0]
    first = j * TILE % rows
    return halves[j * TILE // rows][first : first + TILE, columns]


def head_rows(h):
    return slice(h * (HEAD_WIDTH + ONES), (h + 1) * (HEAD_WIDTH + ONES))


def head_columns(h):
    return slice(h * HEAD_WIDTH, (h + 1) * HEAD_WIDTH)


def in_steps(units, stages):
    held = [None] * len(units)
    for step in range(len(units) + len(stages) - 1):
        for n, stage in enumerate(stages):
            if 0 <= step - n < len(units):
                held[step - n] = stage(units[step - n], held[step - n])


def units_of(group, tok, kv_heads):
    return [
        (h, i)
        for g in kv_heads
        for i in range(tok // TILE)
        for h in range(g * group, (g + 1) * group)
    ]


def near_far_kernel(group, place, *refs):
    @pl.when(place[0] >= 2)
    def _():
        near_far_steps(group, True, *refs)

    @pl.when(place[0] < 2)
    def _():
        near_far_steps(group, False, *refs)


def near_far_steps(group, far_there, q, k, v_a, v_b, k_far_1, k_far_2, out, weights_far, tops):
    v, k_far = (v_a, v_b), (k_far_1, k_far_2)
    tok = q.shape[0]
    kv_heads = range(k.shape[1] // HEAD_WIDTH)
    causal = lax.broadcasted_iota(jnp.int32, (HALF, HALF), 0) <= lax.broadcasted_iota(
        jnp.int32, (HALF, HALF), 1
    )
    v_t = [values_and_ones(v[g // PAIR], head_columns(g % PAIR)) for g in kv_heads]
    nothing = jnp.zeros((HALF, HALF), jnp.bfloat16)
    tiles = tok // TILE
    blocks = [slice(i * TILE, (i + 1) * TILE) for i in range(tiles)]

    def score(unit, _):
        h, i = unit
        qh = q[blocks[i], head_columns(h)]
        columns = head_columns(h // group)
        near = [dot(k[blocks[j], columns], qh, 1, 1) for j in range(i + 1)]
        far = []
        if far_there:
            far = [dot(tile(k_far, j, columns), qh, 1, 1) for j in range(i, tiles)]
        return near, far

    def weigh(unit, scores):
        h, i = unit
        near, far = scores
        near_columns, far_columns = [], []
        for half in range(2):
            a = slice(half * HALF, (half + 1) * HALF)
            near_edge = near[i][: (half + 1) * HALF, a]
            near_pieces = [s[:, a] for s in near[:i]]
            if half == 1:
                near_pieces.append(near_edge[:HALF])
            near_pieces.append(jnp.where(causal, near_edge[half * HALF :], MASKED))
            far_pieces = []
            if far_there:
                far_edge = far[0][half * HALF :, a]
                far_pieces.append(jnp.where(causal, MASKED, far_edge[:HALF]))
                if half == 0:
                    far_pieces.append(far_edge[HALF:])
                far_pieces += [s[:, a] for s in far[1:]]
            top = top_of(near_pieces + far_pieces)
            near_weights = [weights_of(s, top) for s in near_pieces]
            if half == 0:
                near_weights.append(nothing)
            near_columns.append(jnp.concatenate(near_weights, axis=0))
            if far_there:
                far_weights = [weights_of(s, top) for s in far_pieces]
                if half == 1:
                    far_weights.insert(0, nothing)
                far_columns.append(jnp.concatenate(far_weights, axis=0))
            queries = slice(i * TILE + half * HALF, i * TILE + (half + 1) * HALF)
            tops[h : h + 1, queries] = top
        if far_there:
            weights_far[h, i * TILE :, blocks[i]] = jnp.concatenate(far_columns, axis=1)
        return jnp.concatenate(near_columns, axis=1)

    def multiply(unit, weights):
        h, i = unit
        out[head_rows(h), blocks[i]] = dot(v_t[h // group][:, : (i + 1) * TILE], weights, 1, 0)

    in_steps(units_of(group, tok, kv_heads), [score, weigh, multiply])


def middle_kernel(group, place, *refs):
    @pl.when(place[0] >= 2)
    def _():
        middle_steps(group, True, *refs)

    @pl.when(place[0] == 1)
    def _():
        middle_steps(group, False, *refs)

    @pl.when(place[0] == 0)
    def _():
        q, own, k, out, stage, sems = refs[0], refs[1], refs[4], refs[10], refs[11], refs[12]
        kv_heads = range(k.shape[1] // HEAD_WIDTH)
        write_steps(
            group, kv_heads, q.shape[0], lambda h, b: own[head_rows(h), b], out, stage, sems
        )


def middle_steps(
    group, far_there, q, own, weights_far, tops, k_1, k_2, v_a, v_b, rest, weights, *_
):
    k, v_far = (k_1, k_2), (v_a, v_b)
    tok = q.shape[0]
    kv_heads = range(k_1.shape[1] // HEAD_WIDTH)
    v_t = []
    if far_there:
        v_t = [values_and_ones(v_far[g // PAIR], head_columns(g % PAIR)) for g in kv_heads]
    tiles = tok // TILE
    blocks = [slice(i * TILE, (i + 1) * TILE) for i in range(tiles)]

    def score(unit, _):
        h, i = unit
        qh = q[blocks[i], head_columns(h)]
        return [dot(tile(k, j, head_columns(h // group)), qh, 1, 1) for j in range(tiles)]

    def weigh(unit, scores):
        h, i = unit
        before = tops[h : h + 1, blocks[i]]
        top = jnp.maximum(before, top_of(scores))
        for j, s in enumerate(scores):
            weights[h, blocks[j], blocks[i]] = weights_of(s, top)
        return jnp.exp2((before - top) * EXPONENT)

    def multiply(unit, less):
        h, i = unit
        total = own[head_rows(h), blocks[i]]
        if far_there:
            total += dot(v_t[h // group][:, i * TILE :], weights_far[h, i * TILE :, blocks[i]], 1, 0)
        rest[head_rows(h), blocks[i]] = total * less

    in_steps(units_of(group, tok, kv_heads), [score, weigh, multiply])


def write_steps(group, kv_heads, tok, total_of, out, stage, sems):
    copies = []
    for h, i in units_of(group, tok, kv_heads):
        b = slice(i * TILE, (i + 1) * TILE)
        total = total_of(h, b)
        normal = total[:HEAD_WIDTH] * (1.0 / total[HEAD_WIDTH : HEAD_WIDTH + 1])
        stage[b, head_columns(h)] = normal.astype(jnp.bfloat16).T
        if h % group == group - 1:
            width = group * HEAD_WIDTH
            part = (pl.ds(i * TILE, TILE), pl.ds((h + 1) * HEAD_WIDTH - width, width))
            copies.append(
                pltpu.make_async_copy(stage.at[part], out.at[part], sems.at[len(copies)])
            )
            copies[-1].start()
    for copy in copies:
        copy.wait()


def finish_kernel(group, place, rest, weights, v, _, out, stage, sems, part):
    tok = weights.shape[1]
    kv_heads = range(part * PAIR, (part + 1) * PAIR)

    @pl.when(place[0] >= 1)
    def _():
        v_t = [values_and_ones(v, head_columns(g % PAIR)) for g in kv_heads]
        units = units_of(group, tok, kv_heads)
        held = []

        def total_of(h, b):
            at = units.index((h, b.start // TILE))
            for m, i in units[len(held) : at + 2]:
                c = slice(i * TILE, (i + 1) * TILE)
                held.append(dot(v_t[m // group - part * PAIR], weights[m, :, c], 1, 0))
            return rest[head_rows(h), b] + held[at]

        write_steps(group, kv_heads, tok, total_of, out, stage, sems)


def by_heads(kernel, name, query_shape, columns, place, arrays, out_kinds, into=None):
    tok, width = query_shape
    heads = width // HEAD_WIDTH
    shapes = dict(
        rest=((heads * (HEAD_WIDTH + ONES), tok), jnp.float32),
        weights=((heads, tok, tok), jnp.bfloat16),
        stat=((heads, tok), jnp.float32),
        output=((tok, width), jnp.bfloat16),
    )
    in_vmem, anywhere = pl.BlockSpec(memory_space=pltpu.VMEM), pl.BlockSpec(memory_space=pl.ANY)
    in_specs = [pl.BlockSpec(memory_space=pltpu.SMEM)] + [in_vmem] * len(arrays)
    arrays = [place, *arrays]
    aliases, scratch = {}, []
    if into is not None:
        aliases = {len(arrays): out_kinds.index("output")}
        arrays.append(into)
        in_specs.append(anywhere)
    if "output" in out_kinds:
        copies = columns // HEAD_WIDTH * (tok // TILE)
        scratch = [
            pltpu.VMEM((tok, width), jnp.bfloat16),
            pltpu.SemaphoreType.DMA((copies,)),
        ]
    return pl.pallas_call(
        functools.partial(kernel, width // columns),
        in_specs=in_specs,
        out_specs=[anywhere if kind == "output" else in_vmem for kind in out_kinds],
        scratch_shapes=scratch,
        out_shape=[jax.ShapeDtypeStruct(*shapes[kind]) for kind in out_kinds],
        input_output_aliases=aliases,
        compiler_params=pltpu.CompilerParams(vmem_limit_bytes=24 * 1024 * 1024),
        name=name,
    )(*arrays)


def shifted(array, steps):
    count = lax.axis_size("seq")
    return lax.ppermute(array, "seq", [(source, source + steps) for source in range(count - steps)])


def exchanged(array, axis, bit):
    count = lax.axis_size(axis)
    return lax.ppermute(array, axis, [(source, source ^ bit) for source in range(count)])


def on_device(
    normed_input, query, key, value, adapter_down_maps, adapter_up_maps, block_adapter_choice
):
    tok = query.shape[0]
    assert 2 * tok == WINDOW and SEG_LEN % tok == 0
    where = lax.axis_index("seq")
    place = where.reshape(1)
    choice = block_adapter_choice

    even = where % 2 == 0
    barrier = lax.optimization_barrier
    call = functools.partial(by_heads, query_shape=query.shape, columns=key.shape[1])

    def from_one_back(own, far):
        return exchanged(jnp.where(even, own, far), "seq", 1)

    key_1 = first_half(key)
    key_far_1 = shifted(key_1, 2)
    latent, up, key_2 = latent_share(
        place, choice, normed_input.T, adapter_down_maps, adapter_up_maps, key
    )
    key_far_2 = shifted(key_2, 2)
    bit = 1
    while 2 * bit < lax.axis_size("tp"):
        latent = latent + exchanged(latent, "tp", bit)
        bit *= 2
    key_1, latent = barrier((key_1, latent))
    theirs = exchanged(latent, "tp", bit)
    key_mid_1 = from_one_back(key_1, key_far_1)
    values = adapt(latent, theirs, up, value)
    value_far = [shifted(part, 2) for part in values]
    key_2, values = barrier((key_2, values))
    key_mid_2 = from_one_back(key_2, key_far_2)
    values, key_mid_1 = barrier((values, key_mid_1))
    own, weights_far, tops = call(
        near_far_kernel,
        "near_far",
        place=place,
        arrays=[query, key, *values, key_far_1, key_far_2],
        out_kinds=["rest", "weights", "stat"],
    )
    values, own = barrier((values, own))
    value_mid = [from_one_back(mine, theirs) for mine, theirs in zip(values, value_far)]
    rest, weights_mid, done = call(
        middle_kernel,
        "middle",
        place=place,
        arrays=[query, own, weights_far, tops, key_mid_1, key_mid_2, *value_far],
        out_kinds=["rest", "weights", "output"],
    )
    for n, part in enumerate(value_mid):
        [done] = call(
            functools.partial(finish_kernel, part=n),
            "finish",
            place=place,
            arrays=[rest, weights_mid, part],
            out_kinds=["output"],
            into=done,
        )
    return done


def solution(mesh):
    placed = (
        P("seq", "tp"),
        P("seq", "tp"),
        P("seq", "tp"),
        P("seq", "tp"),
        P(None, None, "tp"),
        P(None, None, "tp"),
        P(),
    )
    return jax.shard_map(
        on_device, mesh=mesh, in_specs=placed, out_specs=P("seq", "tp"), check_vma=False
    )
```

```python
import functools

import jax
import jax.numpy as jnp
from jax import lax
from jax.experimental import pallas as pl
from jax.experimental.pallas import tpu as pltpu
from jax.sharding import PartitionSpec as P

HEAD_WIDTH = 128
WINDOW = 1024
SEG_LEN = 2048
SCALE = 168.0 ** (-0.5)
LOG2_E = 1.4426950408889634
EXPONENT = SCALE * LOG2_E
MASKED = -1e30
TILE = 256
HALF = 128
ONES = 16
PAIR = 2
PIECE = 256


def params(steps, mib):
    return pltpu.CompilerParams(
        vmem_limit_bytes=mib * 1024 * 1024, dimension_semantics=("arbitrary",) * steps
    )


def dot(left, right, left_dim, right_dim):
    return lax.dot_general(
        left, right, (((left_dim,), (right_dim,)), ((), ())), preferred_element_type=jnp.float32
    )


def in_hbm(array):
    return pltpu.with_memory_space_constraint(array, pltpu.HBM)


def adapter_of(choice, tok):
    return choice[lax.div(lax.axis_index("seq") * tok, SEG_LEN)]


def first_half_kernel(key, out, sem):
    copy = pltpu.make_async_copy(key.at[pl.ds(0, out.shape[0])], out, sem)
    copy.start()
    copy.wait()


def first_half(key):
    rows, columns = key.shape
    return pl.pallas_call(
        first_half_kernel,
        in_specs=[pl.BlockSpec(memory_space=pltpu.HBM)],
        out_specs=pl.BlockSpec(memory_space=pltpu.VMEM),
        out_shape=jax.ShapeDtypeStruct((rows // 2, columns), key.dtype),
        scratch_shapes=[pltpu.SemaphoreType.DMA],
        compiler_params=pltpu.CompilerParams(vmem_limit_bytes=8 * 1024 * 1024),
        name="first_half",
    )(in_hbm(key))


def latent_kernel(
    pieces, choice, input_t, down, up, key, out, up_out, key_out, ids, rows, map_rows, sems
):
    half = key_out.shape[0]
    ids_copy = pltpu.make_async_copy(choice, ids, sems.at[0])
    ids_copy.start()
    copies = []
    for n, (first, last) in enumerate(pieces):
        part = pl.ds(first, last - first)
        copies.append(pltpu.make_async_copy(input_t.at[part], rows.at[part], sems.at[n + 4]))
        copies[-1].start()
    key_copy = pltpu.make_async_copy(key.at[pl.ds(half, half)], key_out, sems.at[1])
    key_copy.start()
    ids_copy.wait()
    chosen = adapter_of(ids, out.shape[1])
    down_copy = pltpu.make_async_copy(down.at[chosen], map_rows, sems.at[2])
    up_copy = pltpu.make_async_copy(up.at[chosen], up_out, sems.at[3])
    down_copy.start()
    up_copy.start()
    down_copy.wait()
    total = None
    for (first, last), copy in zip(pieces, copies):
        copy.wait()
        product = dot(map_rows[:, first:last], rows[first:last, :], 1, 0)
        total = product if total is None else total + product
    out[...] = total
    up_copy.wait()
    key_copy.wait()


def latent_share(choice, input_t, down_maps, up_maps, key):
    features, tok = input_t.shape
    rank, columns = up_maps.shape[1:]
    pieces = [(first, min(first + PIECE, features)) for first in range(0, features, PIECE)]
    return pl.pallas_call(
        functools.partial(latent_kernel, pieces),
        in_specs=[pl.BlockSpec(memory_space=pltpu.HBM)] * 5,
        out_specs=[pl.BlockSpec(memory_space=pltpu.VMEM)] * 3,
        out_shape=[
            jax.ShapeDtypeStruct((rank, tok), jnp.float32),
            jax.ShapeDtypeStruct((rank, columns), up_maps.dtype),
            jax.ShapeDtypeStruct((tok // 2, columns), key.dtype),
        ],
        scratch_shapes=[
            pltpu.SMEM(choice.shape, choice.dtype),
            pltpu.VMEM((features, tok), input_t.dtype),
            pltpu.VMEM((rank, features), down_maps.dtype),
            pltpu.SemaphoreType.DMA((len(pieces) + 4,)),
        ],
        compiler_params=pltpu.CompilerParams(vmem_limit_bytes=8 * 1024 * 1024),
        name="latent_share",
    )(*(in_hbm(array) for array in (choice, input_t, down_maps, up_maps, key)))


def adapt_kernel(mine, theirs, up, value, *outs):
    latent = (mine[...] + theirs[...]).astype(jnp.bfloat16)
    update = dot(latent, up[...], 0, 0)
    total = (value[...].astype(jnp.float32) + update).astype(jnp.bfloat16)
    for n, out in enumerate(outs):
        width = out.shape[1]
        out[...] = total[:, n * width : (n + 1) * width]


def adapt(mine, theirs, up, value):
    tok, columns = value.shape
    width = PAIR * HEAD_WIDTH
    return pl.pallas_call(
        adapt_kernel,
        out_shape=[jax.ShapeDtypeStruct((tok, width), jnp.bfloat16)] * (columns // width),
        compiler_params=pltpu.CompilerParams(vmem_limit_bytes=8 * 1024 * 1024),
        name="adapt_values",
    )(mine, theirs, up, value)


def weights_of(scores, top):
    return jnp.exp2(((scores - top) * EXPONENT).astype(jnp.bfloat16))


def tree(operation, items):
    items = list(items)
    while len(items) > 1:
        items = [
            operation(items[n], items[n + 1]) if n + 1 < len(items) else items[n]
            for n in range(0, len(items), 2)
        ]
    return items[0]


def top_of(scores):
    pieces = [s[n : n + 32] for s in scores for n in range(0, s.shape[0], 32)]
    pieces = tree(jnp.maximum, pieces)
    pieces = tree(jnp.maximum, [pieces[n : n + 8] for n in range(0, 32, 8)])
    return jnp.max(pieces, axis=0, keepdims=True)


def values_and_ones(v, columns):
    turned = v[:, columns].T
    return jnp.concatenate([turned, jnp.ones((ONES, v.shape[0]), jnp.bfloat16)], axis=0)


def tile(halves, j, columns):
    rows = halves[0].shape[0]
    first = j * TILE % rows
    return halves[j * TILE // rows][first : first + TILE, columns]


def head_rows(h):
    return slice(h * (HEAD_WIDTH + ONES), (h + 1) * (HEAD_WIDTH + ONES))


def head_columns(h):
    return slice(h * HEAD_WIDTH, (h + 1) * HEAD_WIDTH)


def in_steps(units, stages):
    held = [None] * len(units)
    for step in range(len(units) + len(stages) - 1):
        for n, stage in enumerate(stages):
            if 0 <= step - n < len(units):
                held[step - n] = stage(units[step - n], held[step - n])


def units_of(group, tok, kv_heads):
    return [
        (h, i)
        for g in kv_heads
        for i in range(tok // TILE)
        for h in range(g * group, (g + 1) * group)
    ]


def near_far_kernel(group, *refs):
    place = lax.axis_index("seq")

    @pl.when(place >= 2)
    def _():
        near_far_steps(group, True, *refs)

    @pl.when(place < 2)
    def _():
        near_far_steps(group, False, *refs)


def near_far_steps(group, far_there, q, k, v_a, v_b, k_far_1, k_far_2, out, weights_far, tops):
    v, k_far = (v_a, v_b), (k_far_1, k_far_2)
    tok = q.shape[0]
    kv_heads = range(k.shape[1] // HEAD_WIDTH)
    causal = lax.broadcasted_iota(jnp.int32, (HALF, HALF), 0) <= lax.broadcasted_iota(
        jnp.int32, (HALF, HALF), 1
    )
    v_t = [values_and_ones(v[g // PAIR], head_columns(g % PAIR)) for g in kv_heads]
    nothing = jnp.zeros((HALF, HALF), jnp.bfloat16)
    tiles = tok // TILE
    blocks = [slice(i * TILE, (i + 1) * TILE) for i in range(tiles)]

    def score(unit, _):
        h, i = unit
        qh = q[blocks[i], head_columns(h)]
        columns = head_columns(h // group)
        near = [dot(k[blocks[j], columns], qh, 1, 1) for j in range(i + 1)]
        far = []
        if far_there:
            far = [dot(tile(k_far, j, columns), qh, 1, 1) for j in range(i, tiles)]
        return near, far

    def weigh(unit, scores):
        h, i = unit
        near, far = scores
        near_columns, far_columns = [], []
        for half in range(2):
            a = slice(half * HALF, (half + 1) * HALF)
            near_edge = near[i][: (half + 1) * HALF, a]
            near_pieces = [s[:, a] for s in near[:i]]
            if half == 1:
                near_pieces.append(near_edge[:HALF])
            near_pieces.append(jnp.where(causal, near_edge[half * HALF :], MASKED))
            far_pieces = []
            if far_there:
                far_edge = far[0][half * HALF :, a]
                far_pieces.append(jnp.where(causal, MASKED, far_edge[:HALF]))
                if half == 0:
                    far_pieces.append(far_edge[HALF:])
                far_pieces += [s[:, a] for s in far[1:]]
            top = top_of(near_pieces + far_pieces)
            near_weights = [weights_of(s, top) for s in near_pieces]
            if half == 0:
                near_weights.append(nothing)
            near_columns.append(jnp.concatenate(near_weights, axis=0))
            if far_there:
                far_weights = [weights_of(s, top) for s in far_pieces]
                if half == 1:
                    far_weights.insert(0, nothing)
                far_columns.append(jnp.concatenate(far_weights, axis=0))
            queries = slice(i * TILE + half * HALF, i * TILE + (half + 1) * HALF)
            tops[h : h + 1, queries] = top
        if far_there:
            weights_far[h, i * TILE :, blocks[i]] = jnp.concatenate(far_columns, axis=1)
        return jnp.concatenate(near_columns, axis=1)

    def multiply(unit, weights):
        h, i = unit
        out[head_rows(h), blocks[i]] = dot(v_t[h // group][:, : (i + 1) * TILE], weights, 1, 0)

    in_steps(units_of(group, tok, kv_heads), [score, weigh, multiply])


def middle_kernel(group, *refs):
    place = lax.axis_index("seq")

    @pl.when(place >= 2)
    def _():
        middle_steps(group, True, *refs)

    @pl.when(place == 1)
    def _():
        middle_steps(group, False, *refs)

    @pl.when(place == 0)
    def _():
        q, own, k, out, stage, sems = refs[0], refs[1], refs[4], refs[10], refs[11], refs[12]
        kv_heads = range(k.shape[1] // HEAD_WIDTH)
        write_steps(
            group, kv_heads, q.shape[0], lambda h, b: own[head_rows(h), b], out, stage, sems
        )


def middle_steps(
    group, far_there, q, own, weights_far, tops, k_1, k_2, v_a, v_b, rest, weights, *_
):
    k, v_far = (k_1, k_2), (v_a, v_b)
    tok = q.shape[0]
    kv_heads = range(k_1.shape[1] // HEAD_WIDTH)
    v_t = []
    if far_there:
        v_t = [values_and_ones(v_far[g // PAIR], head_columns(g % PAIR)) for g in kv_heads]
    tiles = tok // TILE
    blocks = [slice(i * TILE, (i + 1) * TILE) for i in range(tiles)]

    def score(unit, _):
        h, i = unit
        qh = q[blocks[i], head_columns(h)]
        return [dot(tile(k, j, head_columns(h // group)), qh, 1, 1) for j in range(tiles)]

    def weigh(unit, scores):
        h, i = unit
        before = tops[h : h + 1, blocks[i]]
        top = jnp.maximum(before, top_of(scores))
        for j, s in enumerate(scores):
            weights[h, blocks[j], blocks[i]] = weights_of(s, top)
        return jnp.exp2((before - top) * EXPONENT)

    def multiply(unit, less):
        h, i = unit
        total = own[head_rows(h), blocks[i]]
        if far_there:
            total += dot(v_t[h // group][:, i * TILE :], weights_far[h, i * TILE :, blocks[i]], 1, 0)
        rest[head_rows(h), blocks[i]] = total * less

    in_steps(units_of(group, tok, kv_heads), [score, weigh, multiply])


def write_steps(group, kv_heads, tok, total_of, out, stage, sems):
    copies = []
    for h, i in units_of(group, tok, kv_heads):
        b = slice(i * TILE, (i + 1) * TILE)
        total = total_of(h, b)
        normal = total[:HEAD_WIDTH] * (1.0 / total[HEAD_WIDTH : HEAD_WIDTH + 1])
        stage[b, head_columns(h)] = normal.astype(jnp.bfloat16).T
        if h % group == group - 1:
            width = group * HEAD_WIDTH
            part = (pl.ds(i * TILE, TILE), pl.ds((h + 1) * HEAD_WIDTH - width, width))
            copies.append(
                pltpu.make_async_copy(stage.at[part], out.at[part], sems.at[len(copies)])
            )
            copies[-1].start()
    for copy in copies:
        copy.wait()


def finish_kernel(group, rest, weights, v, _, out, stage, sems, part):
    tok = weights.shape[1]
    kv_heads = range(part * PAIR, (part + 1) * PAIR)

    @pl.when(lax.axis_index("seq") >= 1)
    def _():
        v_t = [values_and_ones(v, head_columns(g % PAIR)) for g in kv_heads]
        units = units_of(group, tok, kv_heads)
        held = []

        def total_of(h, b):
            at = units.index((h, b.start // TILE))
            for m, i in units[len(held) : at + 2]:
                c = slice(i * TILE, (i + 1) * TILE)
                held.append(dot(v_t[m // group - part * PAIR], weights[m, :, c], 1, 0))
            return rest[head_rows(h), b] + held[at]

        write_steps(group, kv_heads, tok, total_of, out, stage, sems)


def by_heads(kernel, name, query_shape, columns, arrays, out_kinds, into=None):
    tok, width = query_shape
    heads = width // HEAD_WIDTH
    shapes = dict(
        rest=((heads * (HEAD_WIDTH + ONES), tok), jnp.float32),
        weights=((heads, tok, tok), jnp.bfloat16),
        stat=((heads, tok), jnp.float32),
        output=((tok, width), jnp.bfloat16),
    )
    in_vmem, anywhere = pl.BlockSpec(memory_space=pltpu.VMEM), pl.BlockSpec(memory_space=pl.ANY)
    in_specs = [in_vmem] * len(arrays)
    aliases, scratch = {}, []
    if into is not None:
        aliases = {len(arrays): out_kinds.index("output")}
        arrays.append(into)
        in_specs.append(anywhere)
    if "output" in out_kinds:
        copies = columns // HEAD_WIDTH * (tok // TILE)
        scratch = [
            pltpu.VMEM((tok, width), jnp.bfloat16),
            pltpu.SemaphoreType.DMA((copies,)),
        ]
    return pl.pallas_call(
        functools.partial(kernel, width // columns),
        in_specs=in_specs,
        out_specs=[anywhere if kind == "output" else in_vmem for kind in out_kinds],
        scratch_shapes=scratch,
        out_shape=[jax.ShapeDtypeStruct(*shapes[kind]) for kind in out_kinds],
        input_output_aliases=aliases,
        compiler_params=pltpu.CompilerParams(vmem_limit_bytes=24 * 1024 * 1024),
        name=name,
    )(*arrays)


def shifted(array, steps):
    count = lax.axis_size("seq")
    return lax.ppermute(array, "seq", [(source, source + steps) for source in range(count - steps)])


def exchanged(array, axis, bit):
    count = lax.axis_size(axis)
    return lax.ppermute(array, axis, [(source, source ^ bit) for source in range(count)])


def on_device(
    normed_input, query, key, value, adapter_down_maps, adapter_up_maps, block_adapter_choice
):
    tok = query.shape[0]
    assert 2 * tok == WINDOW and SEG_LEN % tok == 0
    where = lax.axis_index("seq")
    choice = block_adapter_choice

    even = where % 2 == 0
    barrier = lax.optimization_barrier
    call = functools.partial(by_heads, query_shape=query.shape, columns=key.shape[1])

    def from_one_back(own, far):
        return exchanged(jnp.where(even, own, far), "seq", 1)

    key_1 = first_half(key)
    key_far_1 = shifted(key_1, 2)
    latent, up, key_2 = latent_share(
        choice, normed_input.T, adapter_down_maps, adapter_up_maps, key
    )
    key_far_2 = shifted(key_2, 2)
    bit = 1
    while 2 * bit < lax.axis_size("tp"):
        latent = latent + exchanged(latent, "tp", bit)
        bit *= 2
    key_1, latent = barrier((key_1, latent))
    theirs = exchanged(latent, "tp", bit)
    key_mid_1 = from_one_back(key_1, key_far_1)
    values = adapt(latent, theirs, up, value)
    value_far = [shifted(part, 2) for part in values]
    key_2, values = barrier((key_2, values))
    key_mid_2 = from_one_back(key_2, key_far_2)
    values, key_mid_1 = barrier((values, key_mid_1))
    own, weights_far, tops = call(
        near_far_kernel,
        "near_far",
        arrays=[query, key, *values, key_far_1, key_far_2],
        out_kinds=["rest", "weights", "stat"],
    )
    values, own = barrier((values, own))
    value_mid = [from_one_back(mine, theirs) for mine, theirs in zip(values, value_far)]
    rest, weights_mid, done = call(
        middle_kernel,
        "middle",
        arrays=[query, own, weights_far, tops, key_mid_1, key_mid_2, *value_far],
        out_kinds=["rest", "weights", "output"],
    )
    for n, part in enumerate(value_mid):
        [done] = call(
            functools.partial(finish_kernel, part=n),
            "finish",
                arrays=[rest, weights_mid, part],
            out_kinds=["output"],
            into=done,
        )
    return done


def solution(mesh):
    placed = (
        P("seq", "tp"),
        P("seq", "tp"),
        P("seq", "tp"),
        P("seq", "tp"),
        P(None, None, "tp"),
        P(None, None, "tp"),
        P(),
    )
    return jax.shard_map(
        on_device, mesh=mesh, in_specs=placed, out_specs=P("seq", "tp"), check_vma=False
    )
```

```python
import functools

import jax
import jax.numpy as jnp
from jax import lax
from jax.experimental import pallas as pl
from jax.experimental.pallas import tpu as pltpu
from jax.sharding import PartitionSpec as P

HEAD_WIDTH = 128
WINDOW = 1024
SEG_LEN = 2048
SCALE = 168.0 ** (-0.5)
LOG2_E = 1.4426950408889634
EXPONENT = SCALE * LOG2_E
MASKED = -1e30
TILE = 256
HALF = 128
ONES = 16
PAIR = 2
PIECE = 256


def params(steps, mib):
    return pltpu.CompilerParams(
        vmem_limit_bytes=mib * 1024 * 1024, dimension_semantics=("arbitrary",) * steps
    )


def dot(left, right, left_dim, right_dim):
    return lax.dot_general(
        left, right, (((left_dim,), (right_dim,)), ((), ())), preferred_element_type=jnp.float32
    )


def in_hbm(array):
    return pltpu.with_memory_space_constraint(array, pltpu.HBM)


def adapter_of(choice, tok):
    return choice[lax.div(lax.axis_index("seq") * tok, SEG_LEN)]


def first_half_kernel(key, out, sem):
    copy = pltpu.make_async_copy(key.at[pl.ds(0, out.shape[0])], out, sem)
    copy.start()
    copy.wait()


def first_half(key):
    rows, columns = key.shape
    return pl.pallas_call(
        first_half_kernel,
        in_specs=[pl.BlockSpec(memory_space=pltpu.HBM)],
        out_specs=pl.BlockSpec(memory_space=pltpu.VMEM),
        out_shape=jax.ShapeDtypeStruct((rows // 2, columns), key.dtype),
        scratch_shapes=[pltpu.SemaphoreType.DMA],
        compiler_params=pltpu.CompilerParams(vmem_limit_bytes=8 * 1024 * 1024),
        name="first_half",
    )(in_hbm(key))


def latent_kernel(
    pieces, choice, input_t, down, up, key, out, up_out, key_out, ids, rows, map_rows, sems
):
    half = key_out.shape[0]
    ids_copy = pltpu.make_async_copy(choice, ids, sems.at[0])
    ids_copy.start()
    copies = []
    for n, (first, last) in enumerate(pieces):
        part = pl.ds(first, last - first)
        copies.append(pltpu.make_async_copy(input_t.at[part], rows.at[part], sems.at[n + 4]))
        copies[-1].start()
    key_copy = pltpu.make_async_copy(key.at[pl.ds(half, half)], key_out, sems.at[1])
    key_copy.start()
    ids_copy.wait()
    chosen = adapter_of(ids, out.shape[1])
    down_copy = pltpu.make_async_copy(down.at[chosen], map_rows, sems.at[2])
    up_copy = pltpu.make_async_copy(up.at[chosen], up_out, sems.at[3])
    down_copy.start()
    up_copy.start()
    down_copy.wait()
    total = None
    for (first, last), copy in zip(pieces, copies):
        copy.wait()
        product = dot(map_rows[:, first:last], rows[first:last, :], 1, 0)
        total = product if total is None else total + product
    out[...] = total
    up_copy.wait()
    key_copy.wait()


def latent_share(choice, input_t, down_maps, up_maps, key):
    features, tok = input_t.shape
    rank, columns = up_maps.shape[1:]
    pieces = [(first, min(first + PIECE, features)) for first in range(0, features, PIECE)]
    return pl.pallas_call(
        functools.partial(latent_kernel, pieces),
        in_specs=[pl.BlockSpec(memory_space=pltpu.HBM)] * 5,
        out_specs=[pl.BlockSpec(memory_space=pltpu.VMEM)] * 3,
        out_shape=[
            jax.ShapeDtypeStruct((rank, tok), jnp.float32),
            jax.ShapeDtypeStruct((rank, columns), up_maps.dtype),
            jax.ShapeDtypeStruct((tok // 2, columns), key.dtype),
        ],
        scratch_shapes=[
            pltpu.SMEM(choice.shape, choice.dtype),
            pltpu.VMEM((features, tok), input_t.dtype),
            pltpu.VMEM((rank, features), down_maps.dtype),
            pltpu.SemaphoreType.DMA((len(pieces) + 4,)),
        ],
        compiler_params=pltpu.CompilerParams(vmem_limit_bytes=8 * 1024 * 1024),
        name="latent_share",
    )(*(in_hbm(array) for array in (choice, input_t, down_maps, up_maps, key)))


def adapt_kernel(mine, theirs, up, value, *outs):
    latent = (mine[...] + theirs[...]).astype(jnp.bfloat16)
    update = dot(latent, up[...], 0, 0)
    total = (value[...].astype(jnp.float32) + update).astype(jnp.bfloat16)
    for n, out in enumerate(outs):
        width = out.shape[1]
        out[...] = total[:, n * width : (n + 1) * width]


def adapt(mine, theirs, up, value):
    tok, columns = value.shape
    width = PAIR * HEAD_WIDTH
    return pl.pallas_call(
        adapt_kernel,
        out_shape=[jax.ShapeDtypeStruct((tok, width), jnp.bfloat16)] * (columns // width),
        compiler_params=pltpu.CompilerParams(vmem_limit_bytes=8 * 1024 * 1024),
        name="adapt_values",
    )(mine, theirs, up, value)


def weights_of(scores, top):
    return jnp.exp2(((scores - top) * EXPONENT).astype(jnp.bfloat16))


def tree(operation, items):
    items = list(items)
    while len(items) > 1:
        items = [
            operation(items[n], items[n + 1]) if n + 1 < len(items) else items[n]
            for n in range(0, len(items), 2)
        ]
    return items[0]


def top_of(scores):
    pieces = [s[n : n + 32] for s in scores for n in range(0, s.shape[0], 32)]
    pieces = tree(jnp.maximum, pieces)
    pieces = tree(jnp.maximum, [pieces[n : n + 8] for n in range(0, 32, 8)])
    return jnp.max(pieces, axis=0, keepdims=True)


def values_and_ones(v, columns):
    turned = v[:, columns].T
    return jnp.concatenate([turned, jnp.ones((ONES, v.shape[0]), jnp.bfloat16)], axis=0)


def tile(halves, j, columns):
    rows = halves[0].shape[0]
    first = j * TILE % rows
    return halves[j * TILE // rows][first : first + TILE, columns]


def head_rows(h):
    return slice(h * (HEAD_WIDTH + ONES), (h + 1) * (HEAD_WIDTH + ONES))


def head_columns(h):
    return slice(h * HEAD_WIDTH, (h + 1) * HEAD_WIDTH)


def in_steps(units, stages):
    held = [None] * len(units)
    for step in range(len(units) + len(stages) - 1):
        for n, stage in enumerate(stages):
            if 0 <= step - n < len(units):
                held[step - n] = stage(units[step - n], held[step - n])


def units_of(group, tok, kv_heads):
    return [
        (h, i)
        for g in kv_heads
        for i in range(tok // TILE)
        for h in range(g * group, (g + 1) * group)
    ]


def near_far_kernel(group, *refs):
    place = lax.axis_index("seq")

    @pl.when(place >= 2)
    def _():
        near_far_steps(group, True, *refs)

    @pl.when(place < 2)
    def _():
        near_far_steps(group, False, *refs)


def near_far_steps(
    group, far_there, query, k_1, k_2, v_a, v_b, k_far_1, k_far_2, q, out, weights_far, tops, sems
):
    k, v, k_far = (k_1, k_2), (v_a, v_b), (k_far_1, k_far_2)
    copies = []
    for g in range(k_1.shape[1] // HEAD_WIDTH):
        part = (slice(None), pl.ds(g * group * HEAD_WIDTH, group * HEAD_WIDTH))
        copies.append(pltpu.make_async_copy(query.at[part], q.at[part], sems.at[g]))
        copies[-1].start()
    tok = q.shape[0]
    kv_heads = range(k_1.shape[1] // HEAD_WIDTH)
    causal = lax.broadcasted_iota(jnp.int32, (HALF, HALF), 0) <= lax.broadcasted_iota(
        jnp.int32, (HALF, HALF), 1
    )
    v_t = [values_and_ones(v[g // PAIR], head_columns(g % PAIR)) for g in kv_heads]
    nothing = jnp.zeros((HALF, HALF), jnp.bfloat16)
    tiles = tok // TILE
    blocks = [slice(i * TILE, (i + 1) * TILE) for i in range(tiles)]

    def score(unit, _):
        h, i = unit
        if h % group == 0 and i == 0:
            copies[h // group].wait()
        qh = q[blocks[i], head_columns(h)]
        columns = head_columns(h // group)
        near = [dot(tile(k, j, columns), qh, 1, 1) for j in range(i + 1)]
        far = []
        if far_there:
            far = [dot(tile(k_far, j, columns), qh, 1, 1) for j in range(i, tiles)]
        return near, far

    def weigh(unit, scores):
        h, i = unit
        near, far = scores
        near_columns, far_columns = [], []
        for half in range(2):
            a = slice(half * HALF, (half + 1) * HALF)
            near_edge = near[i][: (half + 1) * HALF, a]
            near_pieces = [s[:, a] for s in near[:i]]
            if half == 1:
                near_pieces.append(near_edge[:HALF])
            near_pieces.append(jnp.where(causal, near_edge[half * HALF :], MASKED))
            far_pieces = []
            if far_there:
                far_edge = far[0][half * HALF :, a]
                far_pieces.append(jnp.where(causal, MASKED, far_edge[:HALF]))
                if half == 0:
                    far_pieces.append(far_edge[HALF:])
                far_pieces += [s[:, a] for s in far[1:]]
            top = top_of(near_pieces + far_pieces)
            near_weights = [weights_of(s, top) for s in near_pieces]
            if half == 0:
                near_weights.append(nothing)
            near_columns.append(jnp.concatenate(near_weights, axis=0))
            if far_there:
                far_weights = [weights_of(s, top) for s in far_pieces]
                if half == 1:
                    far_weights.insert(0, nothing)
                far_columns.append(jnp.concatenate(far_weights, axis=0))
            queries = slice(i * TILE + half * HALF, i * TILE + (half + 1) * HALF)
            tops[h : h + 1, queries] = top
        if far_there:
            weights_far[h, i * TILE :, blocks[i]] = jnp.concatenate(far_columns, axis=1)
        return jnp.concatenate(near_columns, axis=1)

    def multiply(unit, weights):
        h, i = unit
        out[head_rows(h), blocks[i]] = dot(v_t[h // group][:, : (i + 1) * TILE], weights, 1, 0)

    in_steps(units_of(group, tok, kv_heads), [score, weigh, multiply])


def middle_kernel(group, *refs):
    place = lax.axis_index("seq")

    @pl.when(place >= 2)
    def _():
        middle_steps(group, True, *refs)

    @pl.when(place == 1)
    def _():
        middle_steps(group, False, *refs)

    @pl.when(place == 0)
    def _():
        q, own, k, out, stage, sems = refs[0], refs[1], refs[4], refs[10], refs[11], refs[12]
        kv_heads = range(k.shape[1] // HEAD_WIDTH)
        write_steps(
            group, kv_heads, q.shape[0], lambda h, b: own[head_rows(h), b], out, stage, sems
        )


def middle_steps(
    group, far_there, q, own, weights_far, tops, k_1, k_2, v_a, v_b, rest, weights, *_
):
    k, v_far = (k_1, k_2), (v_a, v_b)
    tok = q.shape[0]
    kv_heads = range(k_1.shape[1] // HEAD_WIDTH)
    v_t = []
    if far_there:
        v_t = [values_and_ones(v_far[g // PAIR], head_columns(g % PAIR)) for g in kv_heads]
    tiles = tok // TILE
    blocks = [slice(i * TILE, (i + 1) * TILE) for i in range(tiles)]

    def score(unit, _):
        h, i = unit
        qh = q[blocks[i], head_columns(h)]
        return [dot(tile(k, j, head_columns(h // group)), qh, 1, 1) for j in range(tiles)]

    def weigh(unit, scores):
        h, i = unit
        before = tops[h : h + 1, blocks[i]]
        top = jnp.maximum(before, top_of(scores))
        for j, s in enumerate(scores):
            weights[h, blocks[j], blocks[i]] = weights_of(s, top)
        return jnp.exp2((before - top) * EXPONENT)

    def multiply(unit, less):
        h, i = unit
        total = own[head_rows(h), blocks[i]]
        if far_there:
            total += dot(v_t[h // group][:, i * TILE :], weights_far[h, i * TILE :, blocks[i]], 1, 0)
        rest[head_rows(h), blocks[i]] = total * less

    in_steps(units_of(group, tok, kv_heads), [score, weigh, multiply])


def write_steps(group, kv_heads, tok, total_of, out, stage, sems):
    copies = []
    for h, i in units_of(group, tok, kv_heads):
        b = slice(i * TILE, (i + 1) * TILE)
        total = total_of(h, b)
        normal = total[:HEAD_WIDTH] * (1.0 / total[HEAD_WIDTH : HEAD_WIDTH + 1])
        stage[b, head_columns(h)] = normal.astype(jnp.bfloat16).T
        if h % group == group - 1:
            width = group * HEAD_WIDTH
            part = (pl.ds(i * TILE, TILE), pl.ds((h + 1) * HEAD_WIDTH - width, width))
            copies.append(
                pltpu.make_async_copy(stage.at[part], out.at[part], sems.at[len(copies)])
            )
            copies[-1].start()
    for copy in copies:
        copy.wait()


def finish_kernel(group, rest, weights, v, _, out, stage, sems, part):
    tok = weights.shape[1]
    kv_heads = range(part * PAIR, (part + 1) * PAIR)

    @pl.when(lax.axis_index("seq") >= 1)
    def _():
        v_t = [values_and_ones(v, head_columns(g % PAIR)) for g in kv_heads]
        units = units_of(group, tok, kv_heads)
        held = []

        def total_of(h, b):
            at = units.index((h, b.start // TILE))
            for m, i in units[len(held) : at + 2]:
                c = slice(i * TILE, (i + 1) * TILE)
                held.append(dot(v_t[m // group - part * PAIR], weights[m, :, c], 1, 0))
            return rest[head_rows(h), b] + held[at]

        write_steps(group, kv_heads, tok, total_of, out, stage, sems)


def by_heads(
    kernel, name, query_shape, columns, arrays, out_kinds, into=None, own_copies=False
):
    tok, width = query_shape
    heads = width // HEAD_WIDTH
    shapes = dict(
        queries=((tok, width), jnp.bfloat16),
        rest=((heads * (HEAD_WIDTH + ONES), tok), jnp.float32),
        weights=((heads, tok, tok), jnp.bfloat16),
        stat=((heads, tok), jnp.float32),
        output=((tok, width), jnp.bfloat16),
    )
    in_vmem, anywhere = pl.BlockSpec(memory_space=pltpu.VMEM), pl.BlockSpec(memory_space=pl.ANY)
    in_specs = [in_vmem] * len(arrays)
    aliases, scratch = {}, []
    if own_copies:
        in_specs[0] = pl.BlockSpec(memory_space=pltpu.HBM)
        scratch = [pltpu.SemaphoreType.DMA((columns // HEAD_WIDTH,))]
    if into is not None:
        aliases = {len(arrays): out_kinds.index("output")}
        arrays.append(into)
        in_specs.append(anywhere)
    if "output" in out_kinds:
        copies = columns // HEAD_WIDTH * (tok // TILE)
        scratch = [
            pltpu.VMEM((tok, width), jnp.bfloat16),
            pltpu.SemaphoreType.DMA((copies,)),
        ]
    return pl.pallas_call(
        functools.partial(kernel, width // columns),
        in_specs=in_specs,
        out_specs=[anywhere if kind == "output" else in_vmem for kind in out_kinds],
        scratch_shapes=scratch,
        out_shape=[jax.ShapeDtypeStruct(*shapes[kind]) for kind in out_kinds],
        input_output_aliases=aliases,
        compiler_params=pltpu.CompilerParams(vmem_limit_bytes=24 * 1024 * 1024),
        name=name,
    )(*arrays)


def shifted(array, steps):
    count = lax.axis_size("seq")
    return lax.ppermute(array, "seq", [(source, source + steps) for source in range(count - steps)])


def exchanged(array, axis, bit):
    count = lax.axis_size(axis)
    return lax.ppermute(array, axis, [(source, source ^ bit) for source in range(count)])


def on_device(
    normed_input, query, key, value, adapter_down_maps, adapter_up_maps, block_adapter_choice
):
    tok = query.shape[0]
    assert 2 * tok == WINDOW and SEG_LEN % tok == 0
    where = lax.axis_index("seq")
    choice = block_adapter_choice

    even = where % 2 == 0
    barrier = lax.optimization_barrier
    call = functools.partial(by_heads, query_shape=query.shape, columns=key.shape[1])

    def from_one_back(own, far):
        return exchanged(jnp.where(even, own, far), "seq", 1)

    key_1 = first_half(key)
    key_far_1 = shifted(key_1, 2)
    latent, up, key_2 = latent_share(
        choice, normed_input.T, adapter_down_maps, adapter_up_maps, key
    )
    key_far_2 = shifted(key_2, 2)
    bit = 1
    while 2 * bit < lax.axis_size("tp"):
        latent = latent + exchanged(latent, "tp", bit)
        bit *= 2
    key_1, latent = barrier((key_1, latent))
    theirs = exchanged(latent, "tp", bit)
    key_mid_1 = from_one_back(key_1, key_far_1)
    values = adapt(latent, theirs, up, value)
    value_far = [shifted(part, 2) for part in values]
    key_2, values = barrier((key_2, values))
    key_mid_2 = from_one_back(key_2, key_far_2)
    values, key_mid_1 = barrier((values, key_mid_1))
    queries, own, weights_far, tops = call(
        near_far_kernel,
        "near_far",
        arrays=[in_hbm(query), key_1, key_2, *values, key_far_1, key_far_2],
        out_kinds=["queries", "rest", "weights", "stat"],
        own_copies=True,
    )
    values, own = barrier((values, own))
    value_mid = [from_one_back(mine, theirs) for mine, theirs in zip(values, value_far)]
    rest, weights_mid, done = call(
        middle_kernel,
        "middle",
        arrays=[queries, own, weights_far, tops, key_mid_1, key_mid_2, *value_far],
        out_kinds=["rest", "weights", "output"],
    )
    for n, part in enumerate(value_mid):
        [done] = call(
            functools.partial(finish_kernel, part=n),
            "finish",
                arrays=[rest, weights_mid, part],
            out_kinds=["output"],
            into=done,
        )
    return done


def solution(mesh):
    placed = (
        P("seq", "tp"),
        P("seq", "tp"),
        P("seq", "tp"),
        P("seq", "tp"),
        P(None, None, "tp"),
        P(None, None, "tp"),
        P(),
    )
    return jax.shard_map(
        on_device, mesh=mesh, in_specs=placed, out_specs=P("seq", "tp"), check_vma=False
    )
```

```python
import functools

import jax
import jax.numpy as jnp
from jax import lax
from jax.experimental import pallas as pl
from jax.experimental.pallas import tpu as pltpu
from jax.sharding import PartitionSpec as P

HEAD_WIDTH = 128
WINDOW = 1024
SEG_LEN = 2048
SCALE = 168.0 ** (-0.5)
LOG2_E = 1.4426950408889634
EXPONENT = SCALE * LOG2_E
MASKED = -1e30
TILE = 256
HALF = 128
ONES = 16
PAIR = 2
PIECE = 256


def params(steps, mib):
    return pltpu.CompilerParams(
        vmem_limit_bytes=mib * 1024 * 1024, dimension_semantics=("arbitrary",) * steps
    )


def dot(left, right, left_dim, right_dim):
    return lax.dot_general(
        left, right, (((left_dim,), (right_dim,)), ((), ())), preferred_element_type=jnp.float32
    )


def in_hbm(array):
    return pltpu.with_memory_space_constraint(array, pltpu.HBM)


def adapter_of(choice, tok):
    return choice[lax.div(lax.axis_index("seq") * tok, SEG_LEN)]


def first_half_kernel(key, out, sem):
    copy = pltpu.make_async_copy(key.at[pl.ds(0, out.shape[0])], out, sem)
    copy.start()
    copy.wait()


def first_half(key):
    rows, columns = key.shape
    return pl.pallas_call(
        first_half_kernel,
        in_specs=[pl.BlockSpec(memory_space=pltpu.HBM)],
        out_specs=pl.BlockSpec(memory_space=pltpu.VMEM),
        out_shape=jax.ShapeDtypeStruct((rows // 2, columns), key.dtype),
        scratch_shapes=[pltpu.SemaphoreType.DMA],
        compiler_params=pltpu.CompilerParams(vmem_limit_bytes=8 * 1024 * 1024),
        name="first_half",
    )(in_hbm(key))


def latent_kernel(
    pieces, choice, input_t, down, up, key, out, up_out, key_out, ids, rows, map_rows, sems
):
    half = key_out.shape[0]
    ids_copy = pltpu.make_async_copy(choice, ids, sems.at[0])
    ids_copy.start()
    copies = []
    for n, (first, last) in enumerate(pieces):
        part = pl.ds(first, last - first)
        copies.append(pltpu.make_async_copy(input_t.at[part], rows.at[part], sems.at[n + 4]))
        copies[-1].start()
    key_copy = pltpu.make_async_copy(key.at[pl.ds(half, half)], key_out, sems.at[1])
    key_copy.start()
    ids_copy.wait()
    chosen = adapter_of(ids, out.shape[1])
    down_copy = pltpu.make_async_copy(down.at[chosen], map_rows, sems.at[2])
    up_copy = pltpu.make_async_copy(up.at[chosen], up_out, sems.at[3])
    down_copy.start()
    up_copy.start()
    down_copy.wait()
    total = None
    for (first, last), copy in zip(pieces, copies):
        copy.wait()
        product = dot(map_rows[:, first:last], rows[first:last, :], 1, 0)
        total = product if total is None else total + product
    out[...] = total
    up_copy.wait()
    key_copy.wait()


def latent_share(choice, input_t, down_maps, up_maps, key):
    features, tok = input_t.shape
    rank, columns = up_maps.shape[1:]
    pieces = [(first, min(first + PIECE, features)) for first in range(0, features, PIECE)]
    return pl.pallas_call(
        functools.partial(latent_kernel, pieces),
        in_specs=[pl.BlockSpec(memory_space=pltpu.HBM)] * 5,
        out_specs=[pl.BlockSpec(memory_space=pltpu.VMEM)] * 3,
        out_shape=[
            jax.ShapeDtypeStruct((rank, tok), jnp.float32),
            jax.ShapeDtypeStruct((rank, columns), up_maps.dtype),
            jax.ShapeDtypeStruct((tok // 2, columns), key.dtype),
        ],
        scratch_shapes=[
            pltpu.SMEM(choice.shape, choice.dtype),
            pltpu.VMEM((features, tok), input_t.dtype),
            pltpu.VMEM((rank, features), down_maps.dtype),
            pltpu.SemaphoreType.DMA((len(pieces) + 4,)),
        ],
        compiler_params=pltpu.CompilerParams(vmem_limit_bytes=8 * 1024 * 1024),
        name="latent_share",
    )(*(in_hbm(array) for array in (choice, input_t, down_maps, up_maps, key)))


def adapt_kernel(mine, theirs, up, value, *outs):
    latent = (mine[...] + theirs[...]).astype(jnp.bfloat16)
    update = dot(latent, up[...], 0, 0)
    total = (value[...].astype(jnp.float32) + update).astype(jnp.bfloat16)
    for n, out in enumerate(outs):
        width = out.shape[1]
        out[...] = total[:, n * width : (n + 1) * width]


def adapt(mine, theirs, up, value):
    tok, columns = value.shape
    width = PAIR * HEAD_WIDTH
    return pl.pallas_call(
        adapt_kernel,
        out_shape=[jax.ShapeDtypeStruct((tok, width), jnp.bfloat16)] * (columns // width),
        compiler_params=pltpu.CompilerParams(vmem_limit_bytes=8 * 1024 * 1024),
        name="adapt_values",
    )(mine, theirs, up, value)


def weights_of(scores, top):
    return jnp.exp2(((scores - top) * EXPONENT).astype(jnp.bfloat16))


def tree(operation, items):
    items = list(items)
    while len(items) > 1:
        items = [
            operation(items[n], items[n + 1]) if n + 1 < len(items) else items[n]
            for n in range(0, len(items), 2)
        ]
    return items[0]


def top_of(scores):
    pieces = [s[n : n + 32] for s in scores for n in range(0, s.shape[0], 32)]
    pieces = tree(jnp.maximum, pieces)
    pieces = tree(jnp.maximum, [pieces[n : n + 8] for n in range(0, 32, 8)])
    return jnp.max(pieces, axis=0, keepdims=True)


def values_and_ones(v, columns):
    turned = v[:, columns].T
    return jnp.concatenate([turned, jnp.ones((ONES, v.shape[0]), jnp.bfloat16)], axis=0)


def tile(halves, j, columns):
    rows = halves[0].shape[0]
    first = j * TILE % rows
    return halves[j * TILE // rows][first : first + TILE, columns]


def head_rows(h):
    return slice(h * (HEAD_WIDTH + ONES), (h + 1) * (HEAD_WIDTH + ONES))


def head_columns(h):
    return slice(h * HEAD_WIDTH, (h + 1) * HEAD_WIDTH)


def in_steps(units, stages):
    held = [None] * len(units)
    for step in range(len(units) + len(stages) - 1):
        for n, stage in enumerate(stages):
            if 0 <= step - n < len(units):
                held[step - n] = stage(units[step - n], held[step - n])


def units_of(group, tok, kv_heads):
    return [
        (h, i)
        for g in kv_heads
        for i in range(tok // TILE)
        for h in range(g * group, (g + 1) * group)
    ]


def near_far_kernel(group, *refs):
    place = lax.axis_index("seq")

    @pl.when(place >= 2)
    def _():
        near_far_steps(group, True, *refs)

    @pl.when(place < 2)
    def _():
        near_far_steps(group, False, *refs)


def near_far_steps(
    group, far_there, query, k_1, k_2, v_a, v_b, k_far_1, k_far_2, q, out, weights_far, tops, sems
):
    k, v, k_far = (k_1, k_2), (v_a, v_b), (k_far_1, k_far_2)
    copies = []
    for g in range(k_1.shape[1] // HEAD_WIDTH):
        part = (slice(None), pl.ds(g * group * HEAD_WIDTH, group * HEAD_WIDTH))
        copies.append(pltpu.make_async_copy(query.at[part], q.at[part], sems.at[g]))
        copies[-1].start()
    tok = q.shape[0]
    kv_heads = range(k_1.shape[1] // HEAD_WIDTH)
    causal = lax.broadcasted_iota(jnp.int32, (HALF, HALF), 0) <= lax.broadcasted_iota(
        jnp.int32, (HALF, HALF), 1
    )
    v_t = [values_and_ones(v[g // PAIR], head_columns(g % PAIR)) for g in kv_heads]
    nothing = jnp.zeros((HALF, HALF), jnp.bfloat16)
    tiles = tok // TILE
    blocks = [slice(i * TILE, (i + 1) * TILE) for i in range(tiles)]

    def score(unit, _):
        h, i = unit
        if h % group == 0 and i == 0:
            copies[h // group].wait()
        qh = q[blocks[i], head_columns(h)]
        columns = head_columns(h // group)
        near = [dot(tile(k, j, columns), qh, 1, 1) for j in range(i + 1)]
        far = []
        if far_there:
            far = [dot(tile(k_far, j, columns), qh, 1, 1) for j in range(i, tiles)]
        return near, far

    def weigh(unit, scores):
        h, i = unit
        near, far = scores
        near_columns, far_columns = [], []
        for half in range(2):
            a = slice(half * HALF, (half + 1) * HALF)
            near_edge = near[i][: (half + 1) * HALF, a]
            near_pieces = [s[:, a] for s in near[:i]]
            if half == 1:
                near_pieces.append(near_edge[:HALF])
            near_pieces.append(jnp.where(causal, near_edge[half * HALF :], MASKED))
            far_pieces = []
            if far_there:
                far_edge = far[0][half * HALF :, a]
                far_pieces.append(jnp.where(causal, MASKED, far_edge[:HALF]))
                if half == 0:
                    far_pieces.append(far_edge[HALF:])
                far_pieces += [s[:, a] for s in far[1:]]
            top = top_of(near_pieces + far_pieces)
            near_weights = [weights_of(s, top) for s in near_pieces]
            if half == 0:
                near_weights.append(nothing)
            near_columns.append(jnp.concatenate(near_weights, axis=0))
            if far_there:
                far_weights = [weights_of(s, top) for s in far_pieces]
                if half == 1:
                    far_weights.insert(0, nothing)
                far_columns.append(jnp.concatenate(far_weights, axis=0))
            queries = slice(i * TILE + half * HALF, i * TILE + (half + 1) * HALF)
            tops[h : h + 1, queries] = top
        if far_there:
            weights_far[h, i * TILE :, blocks[i]] = jnp.concatenate(far_columns, axis=1)
        return jnp.concatenate(near_columns, axis=1)

    def multiply(unit, weights):
        h, i = unit
        out[head_rows(h), blocks[i]] = dot(v_t[h // group][:, : (i + 1) * TILE], weights, 1, 0)

    in_steps(units_of(group, tok, kv_heads), [score, weigh, multiply])


def middle_kernel(group, *refs):
    place = lax.axis_index("seq")

    @pl.when(place >= 2)
    def _():
        middle_steps(group, True, *refs)

    @pl.when(place == 1)
    def _():
        middle_steps(group, False, *refs)

    @pl.when(place == 0)
    def _():
        q, own, k, out, stage, sems = refs[0], refs[1], refs[4], refs[10], refs[11], refs[12]
        kv_heads = range(k.shape[1] // HEAD_WIDTH)
        write_steps(
            group, kv_heads, q.shape[0], lambda h, b: own[head_rows(h), b], out, stage, sems
        )


def middle_steps(
    group, far_there, q, own, weights_far, tops, k_1, k_2, v_a, v_b, rest, weights, *_
):
    k, v_far = (k_1, k_2), (v_a, v_b)
    tok = q.shape[0]
    kv_heads = range(k_1.shape[1] // HEAD_WIDTH)
    v_t = []
    if far_there:
        v_t = [values_and_ones(v_far[g // PAIR], head_columns(g % PAIR)) for g in kv_heads]
    tiles = tok // TILE
    blocks = [slice(i * TILE, (i + 1) * TILE) for i in range(tiles)]

    def score(unit, _):
        h, i = unit
        qh = q[blocks[i], head_columns(h)]
        return [dot(tile(k, j, head_columns(h // group)), qh, 1, 1) for j in range(tiles)]

    def weigh(unit, scores):
        h, i = unit
        before = tops[h : h + 1, blocks[i]]
        top = jnp.maximum(before, top_of(scores))
        for j, s in enumerate(scores):
            weights[h, blocks[j], blocks[i]] = weights_of(s, top)
        return jnp.exp2((before - top) * EXPONENT)

    def multiply(unit, less):
        h, i = unit
        total = own[head_rows(h), blocks[i]]
        if far_there:
            total += dot(v_t[h // group][:, i * TILE :], weights_far[h, i * TILE :, blocks[i]], 1, 0)
        rest[head_rows(h), blocks[i]] = total * less

    in_steps(units_of(group, tok, kv_heads), [score, weigh, multiply])


def write_steps(group, kv_heads, tok, total_of, out, stage, sems):
    copies = []
    for h, i in units_of(group, tok, kv_heads):
        b = slice(i * TILE, (i + 1) * TILE)
        total = total_of(h, b)
        normal = total[:HEAD_WIDTH] * (1.0 / total[HEAD_WIDTH : HEAD_WIDTH + 1])
        stage[b, head_columns(h)] = normal.astype(jnp.bfloat16).T
        if h % group == group - 1:
            width = group * HEAD_WIDTH
            part = (pl.ds(i * TILE, TILE), pl.ds((h + 1) * HEAD_WIDTH - width, width))
            copies.append(
                pltpu.make_async_copy(stage.at[part], out.at[part], sems.at[len(copies)])
            )
            copies[-1].start()
    for copy in copies:
        copy.wait()


def finish_kernel(group, rest, weights, v, _, out, stage, sems, part):
    tok = weights.shape[1]
    kv_heads = range(part * PAIR, (part + 1) * PAIR)

    @pl.when(lax.axis_index("seq") >= 1)
    def _():
        v_t = [values_and_ones(v, head_columns(g % PAIR)) for g in kv_heads]
        units = units_of(group, tok, kv_heads)
        held = []

        def total_of(h, b):
            at = units.index((h, b.start // TILE))
            for m, i in units[len(held) : at + 5]:
                c = slice(i * TILE, (i + 1) * TILE)
                held.append(dot(v_t[m // group - part * PAIR], weights[m, :, c], 1, 0))
            return rest[head_rows(h), b] + held[at]

        write_steps(group, kv_heads, tok, total_of, out, stage, sems)


def by_heads(
    kernel, name, query_shape, columns, arrays, out_kinds, into=None, own_copies=False
):
    tok, width = query_shape
    heads = width // HEAD_WIDTH
    shapes = dict(
        queries=((tok, width), jnp.bfloat16),
        rest=((heads * (HEAD_WIDTH + ONES), tok), jnp.float32),
        weights=((heads, tok, tok), jnp.bfloat16),
        stat=((heads, tok), jnp.float32),
        output=((tok, width), jnp.bfloat16),
    )
    in_vmem, anywhere = pl.BlockSpec(memory_space=pltpu.VMEM), pl.BlockSpec(memory_space=pl.ANY)
    in_specs = [in_vmem] * len(arrays)
    aliases, scratch = {}, []
    if own_copies:
        in_specs[0] = pl.BlockSpec(memory_space=pltpu.HBM)
        scratch = [pltpu.SemaphoreType.DMA((columns // HEAD_WIDTH,))]
    if into is not None:
        aliases = {len(arrays): out_kinds.index("output")}
        arrays.append(into)
        in_specs.append(anywhere)
    if "output" in out_kinds:
        copies = columns // HEAD_WIDTH * (tok // TILE)
        scratch = [
            pltpu.VMEM((tok, width), jnp.bfloat16),
            pltpu.SemaphoreType.DMA((copies,)),
        ]
    return pl.pallas_call(
        functools.partial(kernel, width // columns),
        in_specs=in_specs,
        out_specs=[anywhere if kind == "output" else in_vmem for kind in out_kinds],
        scratch_shapes=scratch,
        out_shape=[jax.ShapeDtypeStruct(*shapes[kind]) for kind in out_kinds],
        input_output_aliases=aliases,
        cost_estimate=pl.CostEstimate(
            flops=16 * heads * tok * tok * HEAD_WIDTH, transcendentals=0, bytes_accessed=1 << 20
        ),
        compiler_params=pltpu.CompilerParams(vmem_limit_bytes=24 * 1024 * 1024),
        name=name,
    )(*arrays)


def shifted(array, steps):
    count = lax.axis_size("seq")
    return lax.ppermute(array, "seq", [(source, source + steps) for source in range(count - steps)])


def exchanged(array, axis, bit):
    count = lax.axis_size(axis)
    return lax.ppermute(array, axis, [(source, source ^ bit) for source in range(count)])


def on_device(
    normed_input, query, key, value, adapter_down_maps, adapter_up_maps, block_adapter_choice
):
    tok = query.shape[0]
    assert 2 * tok == WINDOW and SEG_LEN % tok == 0
    where = lax.axis_index("seq")
    choice = block_adapter_choice

    even = where % 2 == 0
    barrier = lax.optimization_barrier
    call = functools.partial(by_heads, query_shape=query.shape, columns=key.shape[1])

    def from_one_back(own, far):
        return exchanged(jnp.where(even, own, far), "seq", 1)

    key_1 = first_half(key)
    key_far_1 = shifted(key_1, 2)
    latent, up, key_2 = latent_share(
        choice, normed_input.T, adapter_down_maps, adapter_up_maps, key
    )
    key_far_2 = shifted(key_2, 2)
    bit = 1
    while 2 * bit < lax.axis_size("tp"):
        latent = latent + exchanged(latent, "tp", bit)
        bit *= 2
    key_1, latent = barrier((key_1, latent))
    theirs = exchanged(latent, "tp", bit)
    key_mid_1 = from_one_back(key_1, key_far_1)
    values = adapt(latent, theirs, up, value)
    value_far = [shifted(values[0], 2)]
    key_2, values = barrier((key_2, values))
    payload, values = barrier((jnp.where(even, key_2, key_far_2), values))
    key_mid_2 = exchanged(payload, "seq", 1)
    value_far.append(shifted(values[1], 2))
    values, key_mid_1 = barrier((values, key_mid_1))
    queries, own, weights_far, tops = call(
        near_far_kernel,
        "near_far",
        arrays=[in_hbm(query), key_1, key_2, *values, key_far_1, key_far_2],
        out_kinds=["queries", "rest", "weights", "stat"],
        own_copies=True,
    )
    values, own = barrier((values, own))
    value_mid = [from_one_back(mine, theirs) for mine, theirs in zip(values, value_far)]
    rest, weights_mid, done = call(
        middle_kernel,
        "middle",
        arrays=[queries, own, weights_far, tops, key_mid_1, key_mid_2, *value_far],
        out_kinds=["rest", "weights", "output"],
    )
    for n, part in enumerate(value_mid):
        [done] = call(
            functools.partial(finish_kernel, part=n),
            "finish",
                arrays=[rest, weights_mid, part],
            out_kinds=["output"],
            into=done,
        )
    return done


def solution(mesh):
    placed = (
        P("seq", "tp"),
        P("seq", "tp"),
        P("seq", "tp"),
        P("seq", "tp"),
        P(None, None, "tp"),
        P(None, None, "tp"),
        P(),
    )
    return jax.shard_map(
        on_device, mesh=mesh, in_specs=placed, out_specs=P("seq", "tp"), check_vma=False
    )
```

```python
import functools

import jax
import jax.numpy as jnp
from jax import lax
from jax.experimental import pallas as pl
from jax.experimental.pallas import tpu as pltpu
from jax.sharding import PartitionSpec as P

HEAD_WIDTH = 128
WINDOW = 1024
SEG_LEN = 2048
SCALE = 168.0 ** (-0.5)
LOG2_E = 1.4426950408889634
EXPONENT = SCALE * LOG2_E
MASKED = -1e30
TILE = 256
HALF = 128
ONES = 16
PAIR = 2
PIECE = 256
COPIES = 4


def params(steps, mib):
    return pltpu.CompilerParams(
        vmem_limit_bytes=mib * 1024 * 1024, dimension_semantics=("arbitrary",) * steps
    )


def dot(left, right, left_dim, right_dim):
    return lax.dot_general(
        left, right, (((left_dim,), (right_dim,)), ((), ())), preferred_element_type=jnp.float32
    )


def in_hbm(array):
    return pltpu.with_memory_space_constraint(array, pltpu.HBM)


def adapter_of(choice, tok):
    return choice[lax.div(lax.axis_index("seq") * tok, SEG_LEN)]


def first_half_kernel(key, out, sems):
    copies = []
    for n in range(COPIES):
        rows = out.shape[0] // COPIES
        part = pl.ds(n * rows, rows)
        copies.append(pltpu.make_async_copy(key.at[part], out.at[part], sems.at[n]))
        copies[-1].start()
    for copy in copies:
        copy.wait()


def first_half(key):
    rows, columns = key.shape
    return pl.pallas_call(
        first_half_kernel,
        in_specs=[pl.BlockSpec(memory_space=pltpu.HBM)],
        out_specs=pl.BlockSpec(memory_space=pltpu.VMEM),
        out_shape=jax.ShapeDtypeStruct((rows // 2, columns), key.dtype),
        scratch_shapes=[pltpu.SemaphoreType.DMA((COPIES,))],
        compiler_params=pltpu.CompilerParams(vmem_limit_bytes=8 * 1024 * 1024),
        name="first_half",
    )(in_hbm(key))


def latent_kernel(
    pieces, choice, input_t, down, up, key, out, up_out, key_out, ids, rows, map_rows, sems
):
    half = key_out.shape[0]
    ids_copy = pltpu.make_async_copy(choice, ids, sems.at[0])
    ids_copy.start()
    copies = []
    for n, (first, last) in enumerate(pieces):
        part = pl.ds(first, last - first)
        copies.append(pltpu.make_async_copy(input_t.at[part], rows.at[part], sems.at[n + 4]))
        copies[-1].start()
    key_copy = pltpu.make_async_copy(key.at[pl.ds(half, half)], key_out, sems.at[1])
    key_copy.start()
    ids_copy.wait()
    chosen = adapter_of(ids, out.shape[1])
    down_copy = pltpu.make_async_copy(down.at[chosen], map_rows, sems.at[2])
    up_copy = pltpu.make_async_copy(up.at[chosen], up_out, sems.at[3])
    down_copy.start()
    up_copy.start()
    down_copy.wait()
    total = None
    for (first, last), copy in zip(pieces, copies):
        copy.wait()
        product = dot(map_rows[:, first:last], rows[first:last, :], 1, 0)
        total = product if total is None else total + product
    out[...] = total
    up_copy.wait()
    key_copy.wait()


def latent_share(choice, input_t, down_maps, up_maps, key):
    features, tok = input_t.shape
    rank, columns = up_maps.shape[1:]
    pieces = [(first, min(first + PIECE, features)) for first in range(0, features, PIECE)]
    return pl.pallas_call(
        functools.partial(latent_kernel, pieces),
        in_specs=[pl.BlockSpec(memory_space=pltpu.HBM)] * 5,
        out_specs=[pl.BlockSpec(memory_space=pltpu.VMEM)] * 3,
        out_shape=[
            jax.ShapeDtypeStruct((rank, tok), jnp.float32),
            jax.ShapeDtypeStruct((rank, columns), up_maps.dtype),
            jax.ShapeDtypeStruct((tok // 2, columns), key.dtype),
        ],
        scratch_shapes=[
            pltpu.SMEM(choice.shape, choice.dtype),
            pltpu.VMEM((features, tok), input_t.dtype),
            pltpu.VMEM((rank, features), down_maps.dtype),
            pltpu.SemaphoreType.DMA((len(pieces) + 4,)),
        ],
        compiler_params=pltpu.CompilerParams(vmem_limit_bytes=8 * 1024 * 1024),
        name="latent_share",
    )(*(in_hbm(array) for array in (choice, input_t, down_maps, up_maps, key)))


def adapt_kernel(mine, theirs, up, value, *outs):
    latent = (mine[...] + theirs[...].astype(jnp.float32)).astype(jnp.bfloat16)
    update = dot(latent, up[...], 0, 0)
    total = (value[...].astype(jnp.float32) + update).astype(jnp.bfloat16)
    for n, out in enumerate(outs):
        width = out.shape[1]
        out[...] = total[:, n * width : (n + 1) * width]


def adapt(mine, theirs, up, value):
    tok, columns = value.shape
    width = PAIR * HEAD_WIDTH
    return pl.pallas_call(
        adapt_kernel,
        out_shape=[jax.ShapeDtypeStruct((tok, width), jnp.bfloat16)] * (columns // width),
        compiler_params=pltpu.CompilerParams(vmem_limit_bytes=8 * 1024 * 1024),
        name="adapt_values",
    )(mine, theirs, up, value)


def weights_of(scores, top):
    return jnp.exp2(((scores - top) * EXPONENT).astype(jnp.bfloat16))


def tree(operation, items):
    items = list(items)
    while len(items) > 1:
        items = [
            operation(items[n], items[n + 1]) if n + 1 < len(items) else items[n]
            for n in range(0, len(items), 2)
        ]
    return items[0]


def top_of(scores):
    pieces = [s[n : n + 32] for s in scores for n in range(0, s.shape[0], 32)]
    pieces = tree(jnp.maximum, pieces)
    pieces = tree(jnp.maximum, [pieces[n : n + 8] for n in range(0, 32, 8)])
    return jnp.max(pieces, axis=0, keepdims=True)


def values_and_ones(v, columns):
    turned = v[:, columns].T
    return jnp.concatenate([turned, jnp.ones((ONES, v.shape[0]), jnp.bfloat16)], axis=0)


def tile(halves, j, columns):
    rows = halves[0].shape[0]
    first = j * TILE % rows
    return halves[j * TILE // rows][first : first + TILE, columns]


def head_rows(h):
    return slice(h * (HEAD_WIDTH + ONES), (h + 1) * (HEAD_WIDTH + ONES))


def head_columns(h):
    return slice(h * HEAD_WIDTH, (h + 1) * HEAD_WIDTH)


def in_steps(units, stages):
    held = [None] * len(units)
    for step in range(len(units) + len(stages) - 1):
        for n, stage in enumerate(stages):
            if 0 <= step - n < len(units):
                held[step - n] = stage(units[step - n], held[step - n])


def units_of(group, tok, kv_heads):
    return [
        (h, i)
        for g in kv_heads
        for i in range(tok // TILE)
        for h in range(g * group, (g + 1) * group)
    ]


def near_far_kernel(group, *refs):
    place = lax.axis_index("seq")

    @pl.when(place >= 2)
    def _():
        near_far_steps(group, True, *refs)

    @pl.when(place < 2)
    def _():
        near_far_steps(group, False, *refs)


def near_far_steps(
    group, far_there, query, k_1, k_2, v_a, v_b, k_far_1, k_far_2, q, out, weights_far, tops, sems
):
    k, v, k_far = (k_1, k_2), (v_a, v_b), (k_far_1, k_far_2)
    copies = []
    for g in range(k_1.shape[1] // HEAD_WIDTH):
        part = (slice(None), pl.ds(g * group * HEAD_WIDTH, group * HEAD_WIDTH))
        copies.append(pltpu.make_async_copy(query.at[part], q.at[part], sems.at[g]))
        copies[-1].start()
    tok = q.shape[0]
    kv_heads = range(k_1.shape[1] // HEAD_WIDTH)
    causal = lax.broadcasted_iota(jnp.int32, (HALF, HALF), 0) <= lax.broadcasted_iota(
        jnp.int32, (HALF, HALF), 1
    )
    v_t = [values_and_ones(v[g // PAIR], head_columns(g % PAIR)) for g in kv_heads]
    nothing = jnp.zeros((HALF, HALF), jnp.bfloat16)
    tiles = tok // TILE
    blocks = [slice(i * TILE, (i + 1) * TILE) for i in range(tiles)]

    def score(unit, _):
        h, i = unit
        if h % group == 0 and i == 0:
            copies[h // group].wait()
        qh = q[blocks[i], head_columns(h)]
        columns = head_columns(h // group)
        near = [dot(tile(k, j, columns), qh, 1, 1) for j in range(i + 1)]
        far = []
        if far_there:
            far = [dot(tile(k_far, j, columns), qh, 1, 1) for j in range(i, tiles)]
        return near, far

    def weigh(unit, scores):
        h, i = unit
        near, far = scores
        near_columns, far_columns = [], []
        for half in range(2):
            a = slice(half * HALF, (half + 1) * HALF)
            near_edge = near[i][: (half + 1) * HALF, a]
            near_pieces = [s[:, a] for s in near[:i]]
            if half == 1:
                near_pieces.append(near_edge[:HALF])
            near_pieces.append(jnp.where(causal, near_edge[half * HALF :], MASKED))
            far_pieces = []
            if far_there:
                far_edge = far[0][half * HALF :, a]
                far_pieces.append(jnp.where(causal, MASKED, far_edge[:HALF]))
                if half == 0:
                    far_pieces.append(far_edge[HALF:])
                far_pieces += [s[:, a] for s in far[1:]]
            top = top_of(near_pieces + far_pieces)
            near_weights = [weights_of(s, top) for s in near_pieces]
            if half == 0:
                near_weights.append(nothing)
            near_columns.append(jnp.concatenate(near_weights, axis=0))
            if far_there:
                far_weights = [weights_of(s, top) for s in far_pieces]
                if half == 1:
                    far_weights.insert(0, nothing)
                far_columns.append(jnp.concatenate(far_weights, axis=0))
            queries = slice(i * TILE + half * HALF, i * TILE + (half + 1) * HALF)
            tops[h : h + 1, queries] = top
        if far_there:
            weights_far[h, i * TILE :, blocks[i]] = jnp.concatenate(far_columns, axis=1)
        return jnp.concatenate(near_columns, axis=1)

    def multiply(unit, weights):
        h, i = unit
        out[head_rows(h), blocks[i]] = dot(v_t[h // group][:, : (i + 1) * TILE], weights, 1, 0)

    in_steps(units_of(group, tok, kv_heads), [score, weigh, multiply])


def middle_kernel(group, *refs):
    place = lax.axis_index("seq")

    @pl.when(place >= 2)
    def _():
        middle_steps(group, True, *refs)

    @pl.when(place == 1)
    def _():
        middle_steps(group, False, *refs)

    @pl.when(place == 0)
    def _():
        q, own, k, out, stage, sems = refs[0], refs[1], refs[4], refs[10], refs[11], refs[12]
        kv_heads = range(k.shape[1] // HEAD_WIDTH)
        write_steps(
            group, kv_heads, q.shape[0], lambda h, b: own[head_rows(h), b], out, stage, sems
        )


def middle_steps(
    group, far_there, q, own, weights_far, tops, k_1, k_2, v_a, v_b, rest, weights, *_
):
    k, v_far = (k_1, k_2), (v_a, v_b)
    tok = q.shape[0]
    kv_heads = range(k_1.shape[1] // HEAD_WIDTH)
    v_t = []
    if far_there:
        v_t = [values_and_ones(v_far[g // PAIR], head_columns(g % PAIR)) for g in kv_heads]
    tiles = tok // TILE
    blocks = [slice(i * TILE, (i + 1) * TILE) for i in range(tiles)]

    def score(unit, _):
        h, i = unit
        qh = q[blocks[i], head_columns(h)]
        return [dot(tile(k, j, head_columns(h // group)), qh, 1, 1) for j in range(tiles)]

    def weigh(unit, scores):
        h, i = unit
        before = tops[h : h + 1, blocks[i]]
        top = jnp.maximum(before, top_of(scores))
        for j, s in enumerate(scores):
            weights[h, blocks[j], blocks[i]] = weights_of(s, top)
        return jnp.exp2((before - top) * EXPONENT)

    def multiply(unit, less):
        h, i = unit
        total = own[head_rows(h), blocks[i]]
        if far_there:
            total += dot(v_t[h // group][:, i * TILE :], weights_far[h, i * TILE :, blocks[i]], 1, 0)
        rest[head_rows(h), blocks[i]] = total * less

    in_steps(units_of(group, tok, kv_heads), [score, weigh, multiply])


def write_steps(group, kv_heads, tok, total_of, out, stage, sems):
    copies = []
    for h, i in units_of(group, tok, kv_heads):
        b = slice(i * TILE, (i + 1) * TILE)
        total = total_of(h, b)
        normal = total[:HEAD_WIDTH] * (1.0 / total[HEAD_WIDTH : HEAD_WIDTH + 1])
        stage[b, head_columns(h)] = normal.astype(jnp.bfloat16).T
        if h % group == group - 1:
            width = group * HEAD_WIDTH
            part = (pl.ds(i * TILE, TILE), pl.ds((h + 1) * HEAD_WIDTH - width, width))
            copies.append(
                pltpu.make_async_copy(stage.at[part], out.at[part], sems.at[len(copies)])
            )
            copies[-1].start()
    for copy in copies:
        copy.wait()


def finish_kernel(group, rest, weights, v, _, out, stage, sems, part):
    tok = weights.shape[1]
    kv_heads = range(part * PAIR, (part + 1) * PAIR)

    @pl.when(lax.axis_index("seq") >= 1)
    def _():
        v_t = [values_and_ones(v, head_columns(g % PAIR)) for g in kv_heads]
        units = units_of(group, tok, kv_heads)
        held = []

        def total_of(h, b):
            at = units.index((h, b.start // TILE))
            for m, i in units[len(held) : at + 2]:
                c = slice(i * TILE, (i + 1) * TILE)
                held.append(dot(v_t[m // group - part * PAIR], weights[m, :, c], 1, 0))
            return rest[head_rows(h), b] + held[at]

        write_steps(group, kv_heads, tok, total_of, out, stage, sems)


def by_heads(
    kernel, name, query_shape, columns, arrays, out_kinds, into=None, own_copies=False
):
    tok, width = query_shape
    heads = width // HEAD_WIDTH
    shapes = dict(
        queries=((tok, width), jnp.bfloat16),
        rest=((heads * (HEAD_WIDTH + ONES), tok), jnp.float32),
        weights=((heads, tok, tok), jnp.bfloat16),
        stat=((heads, tok), jnp.float32),
        output=((tok, width), jnp.bfloat16),
    )
    in_vmem, anywhere = pl.BlockSpec(memory_space=pltpu.VMEM), pl.BlockSpec(memory_space=pl.ANY)
    in_specs = [in_vmem] * len(arrays)
    aliases, scratch = {}, []
    if own_copies:
        in_specs[0] = pl.BlockSpec(memory_space=pltpu.HBM)
        scratch = [pltpu.SemaphoreType.DMA((columns // HEAD_WIDTH,))]
    if into is not None:
        aliases = {len(arrays): out_kinds.index("output")}
        arrays.append(into)
        in_specs.append(anywhere)
    if "output" in out_kinds:
        copies = columns // HEAD_WIDTH * (tok // TILE)
        scratch = [
            pltpu.VMEM((tok, width), jnp.bfloat16),
            pltpu.SemaphoreType.DMA((copies,)),
        ]
    return pl.pallas_call(
        functools.partial(kernel, width // columns),
        in_specs=in_specs,
        out_specs=[anywhere if kind == "output" else in_vmem for kind in out_kinds],
        scratch_shapes=scratch,
        out_shape=[jax.ShapeDtypeStruct(*shapes[kind]) for kind in out_kinds],
        input_output_aliases=aliases,
        compiler_params=pltpu.CompilerParams(vmem_limit_bytes=24 * 1024 * 1024),
        name=name,
    )(*arrays)


def shifted(array, steps):
    count = lax.axis_size("seq")
    return lax.ppermute(array, "seq", [(source, source + steps) for source in range(count - steps)])


def exchanged(array, axis, bit):
    count = lax.axis_size(axis)
    return lax.ppermute(array, axis, [(source, source ^ bit) for source in range(count)])


def on_device(
    normed_input, query, key, value, adapter_down_maps, adapter_up_maps, block_adapter_choice
):
    tok = query.shape[0]
    assert 2 * tok == WINDOW and SEG_LEN % tok == 0
    where = lax.axis_index("seq")
    choice = block_adapter_choice

    even = where % 2 == 0
    barrier = lax.optimization_barrier
    call = functools.partial(by_heads, query_shape=query.shape, columns=key.shape[1])

    def from_one_back(own, far):
        return exchanged(jnp.where(even, own, far), "seq", 1)

    key_1 = first_half(key)
    key_far_1 = shifted(key_1, 2)
    latent, up, key_2 = latent_share(
        choice, normed_input.T, adapter_down_maps, adapter_up_maps, key
    )
    key_far_2 = shifted(key_2, 2)
    bit = 1
    while 2 * bit < lax.axis_size("tp"):
        latent = latent + exchanged(latent, "tp", bit)
        bit *= 2
    key_1, latent = barrier((key_1, latent))
    theirs = exchanged(latent.astype(jnp.bfloat16), "tp", bit)
    key_mid_1 = from_one_back(key_1, key_far_1)
    values = adapt(latent, theirs, up, value)
    value_far = [shifted(part, 2) for part in values]
    key_2, values = barrier((key_2, values))
    key_mid_2 = from_one_back(key_2, key_far_2)
    values, key_mid_1 = barrier((values, key_mid_1))
    queries, own, weights_far, tops = call(
        near_far_kernel,
        "near_far",
        arrays=[in_hbm(query), key_1, key_2, *values, key_far_1, key_far_2],
        out_kinds=["queries", "rest", "weights", "stat"],
        own_copies=True,
    )
    values, own = barrier((values, own))
    value_mid = [from_one_back(mine, theirs) for mine, theirs in zip(values, value_far)]
    rest, weights_mid, done = call(
        middle_kernel,
        "middle",
        arrays=[queries, own, weights_far, tops, key_mid_1, key_mid_2, *value_far],
        out_kinds=["rest", "weights", "output"],
    )
    for n, part in enumerate(value_mid):
        [done] = call(
            functools.partial(finish_kernel, part=n),
            "finish",
                arrays=[rest, weights_mid, part],
            out_kinds=["output"],
            into=done,
        )
    return done


def solution(mesh):
    placed = (
        P("seq", "tp"),
        P("seq", "tp"),
        P("seq", "tp"),
        P("seq", "tp"),
        P(None, None, "tp"),
        P(None, None, "tp"),
        P(),
    )
    return jax.shard_map(
        on_device, mesh=mesh, in_specs=placed, out_specs=P("seq", "tp"), check_vma=False
    )
```

```python
import functools

import jax
import jax.numpy as jnp
from jax import lax
from jax.experimental import pallas as pl
from jax.experimental.pallas import tpu as pltpu
from jax.sharding import PartitionSpec as P

HEAD_WIDTH = 128
WINDOW = 1024
SEG_LEN = 2048
SCALE = 168.0 ** (-0.5)
LOG2_E = 1.4426950408889634
EXPONENT = SCALE * LOG2_E
MASKED = -1e30
TILE = 256
HALF = 128
ONES = 16
PAIR = 2
PIECE = 256


def params(steps, mib):
    return pltpu.CompilerParams(
        vmem_limit_bytes=mib * 1024 * 1024, dimension_semantics=("arbitrary",) * steps
    )


def dot(left, right, left_dim, right_dim):
    return lax.dot_general(
        left, right, (((left_dim,), (right_dim,)), ((), ())), preferred_element_type=jnp.float32
    )


def in_hbm(array):
    return pltpu.with_memory_space_constraint(array, pltpu.HBM)


def adapter_of(choice, tok):
    return choice[lax.div(lax.axis_index("seq") * tok, SEG_LEN)]


def first_half_kernel(key, out, sem):
    copy = pltpu.make_async_copy(key.at[pl.ds(0, out.shape[0])], out, sem)
    copy.start()
    copy.wait()


def first_half(key):
    rows, columns = key.shape
    return pl.pallas_call(
        first_half_kernel,
        in_specs=[pl.BlockSpec(memory_space=pltpu.HBM)],
        out_specs=pl.BlockSpec(memory_space=pltpu.VMEM),
        out_shape=jax.ShapeDtypeStruct((rows // 2, columns), key.dtype),
        scratch_shapes=[pltpu.SemaphoreType.DMA],
        compiler_params=pltpu.CompilerParams(vmem_limit_bytes=8 * 1024 * 1024),
        name="first_half",
    )(in_hbm(key))


def latent_kernel(
    pieces, choice, input_t, down, up, key, out, up_out, key_out, ids, rows, map_rows, sems
):
    half = key_out.shape[0]
    ids_copy = pltpu.make_async_copy(choice, ids, sems.at[0])
    ids_copy.start()
    copies = []
    for n, (first, last) in enumerate(pieces):
        part = pl.ds(first, last - first)
        copies.append(pltpu.make_async_copy(input_t.at[part], rows.at[part], sems.at[n + 4]))
        copies[-1].start()
    key_copy = pltpu.make_async_copy(key.at[pl.ds(half, half)], key_out, sems.at[1])
    key_copy.start()
    ids_copy.wait()
    chosen = adapter_of(ids, out.shape[1])
    down_copy = pltpu.make_async_copy(down.at[chosen], map_rows, sems.at[2])
    up_copy = pltpu.make_async_copy(up.at[chosen], up_out, sems.at[3])
    down_copy.start()
    up_copy.start()
    down_copy.wait()
    total = None
    for (first, last), copy in zip(pieces, copies):
        copy.wait()
        product = dot(map_rows[:, first:last], rows[first:last, :], 1, 0)
        total = product if total is None else total + product
    out[...] = total
    up_copy.wait()
    key_copy.wait()


def latent_share(choice, input_t, down_maps, up_maps, key):
    features, tok = input_t.shape
    rank, columns = up_maps.shape[1:]
    pieces = [(first, min(first + PIECE, features)) for first in range(0, features, PIECE)]
    return pl.pallas_call(
        functools.partial(latent_kernel, pieces),
        in_specs=[pl.BlockSpec(memory_space=pltpu.HBM)] * 5,
        out_specs=[pl.BlockSpec(memory_space=pltpu.VMEM)] * 3,
        out_shape=[
            jax.ShapeDtypeStruct((rank, tok), jnp.float32),
            jax.ShapeDtypeStruct((rank, columns), up_maps.dtype),
            jax.ShapeDtypeStruct((tok // 2, columns), key.dtype),
        ],
        scratch_shapes=[
            pltpu.SMEM(choice.shape, choice.dtype),
            pltpu.VMEM((features, tok), input_t.dtype),
            pltpu.VMEM((rank, features), down_maps.dtype),
            pltpu.SemaphoreType.DMA((len(pieces) + 4,)),
        ],
        compiler_params=pltpu.CompilerParams(vmem_limit_bytes=8 * 1024 * 1024),
        name="latent_share",
    )(*(in_hbm(array) for array in (choice, input_t, down_maps, up_maps, key)))


def adapt_kernel(mine, theirs, up, value, *outs):
    latent = (mine[...] + theirs[...]).astype(jnp.bfloat16)
    update = dot(latent, up[...], 0, 0)
    total = (value[...].astype(jnp.float32) + update).astype(jnp.bfloat16)
    for n, out in enumerate(outs):
        width = out.shape[1]
        out[...] = total[:, n * width : (n + 1) * width]


def adapt(mine, theirs, up, value):
    tok, columns = value.shape
    width = PAIR * HEAD_WIDTH
    return pl.pallas_call(
        adapt_kernel,
        out_shape=[jax.ShapeDtypeStruct((tok, width), jnp.bfloat16)] * (columns // width),
        compiler_params=pltpu.CompilerParams(vmem_limit_bytes=8 * 1024 * 1024),
        name="adapt_values",
    )(mine, theirs, up, value)


def weights_of(scores, top):
    return jnp.exp2(((scores - top) * EXPONENT).astype(jnp.bfloat16))


def tree(operation, items):
    items = list(items)
    while len(items) > 1:
        items = [
            operation(items[n], items[n + 1]) if n + 1 < len(items) else items[n]
            for n in range(0, len(items), 2)
        ]
    return items[0]


def top_of(scores):
    pieces = [s[n : n + 32] for s in scores for n in range(0, s.shape[0], 32)]
    pieces = tree(jnp.maximum, pieces)
    pieces = tree(jnp.maximum, [pieces[n : n + 8] for n in range(0, 32, 8)])
    return jnp.max(pieces, axis=0, keepdims=True)


def values_and_ones(v, columns):
    turned = v[:, columns].T
    return jnp.concatenate([turned, jnp.ones((ONES, v.shape[0]), jnp.bfloat16)], axis=0)


def tile(halves, j, columns):
    rows = halves[0].shape[0]
    first = j * TILE % rows
    return halves[j * TILE // rows][first : first + TILE, columns]


def head_rows(h):
    return slice(h * (HEAD_WIDTH + ONES), (h + 1) * (HEAD_WIDTH + ONES))


def head_columns(h):
    return slice(h * HEAD_WIDTH, (h + 1) * HEAD_WIDTH)


def in_steps(units, stages):
    held = [None] * len(units)
    for step in range(len(units) + len(stages) - 1):
        for n, stage in enumerate(stages):
            if 0 <= step - n < len(units):
                held[step - n] = stage(units[step - n], held[step - n])


def units_of(group, tok, kv_heads):
    return [
        (h, i)
        for g in kv_heads
        for i in range(tok // TILE)
        for h in range(g * group, (g + 1) * group)
    ]


def near_far_kernel(group, *refs):
    place = lax.axis_index("seq")

    @pl.when(place >= 2)
    def _():
        near_far_steps(group, True, *refs)

    @pl.when(place < 2)
    def _():
        near_far_steps(group, False, *refs)


def near_far_steps(
    group, far_there, query, k_1, k_2, v_a, v_b, k_far_1, k_far_2, q, out, weights_far, tops, sems
):
    k, v, k_far = (k_1, k_2), (v_a, v_b), (k_far_1, k_far_2)
    copies = []
    for g in range(k_1.shape[1] // HEAD_WIDTH):
        part = (slice(None), pl.ds(g * group * HEAD_WIDTH, group * HEAD_WIDTH))
        copies.append(pltpu.make_async_copy(query.at[part], q.at[part], sems.at[g]))
        copies[-1].start()
    tok = q.shape[0]
    kv_heads = range(k_1.shape[1] // HEAD_WIDTH)
    causal = lax.broadcasted_iota(jnp.int32, (HALF, HALF), 0) <= lax.broadcasted_iota(
        jnp.int32, (HALF, HALF), 1
    )
    v_t = [values_and_ones(v[g // PAIR], head_columns(g % PAIR)) for g in kv_heads]
    nothing = jnp.zeros((HALF, HALF), jnp.bfloat16)
    tiles = tok // TILE
    blocks = [slice(i * TILE, (i + 1) * TILE) for i in range(tiles)]

    def score(unit, _):
        h, i = unit
        if h % group == 0 and i == 0:
            copies[h // group].wait()
        qh = q[blocks[i], head_columns(h)]
        columns = head_columns(h // group)
        near = [dot(tile(k, j, columns), qh, 1, 1) for j in range(i + 1)]
        far = []
        if far_there:
            far = [dot(tile(k_far, j, columns), qh, 1, 1) for j in range(i, tiles)]
        return near, far

    def weigh(unit, scores):
        h, i = unit
        near, far = scores
        near_columns, far_columns = [], []
        for half in range(2):
            a = slice(half * HALF, (half + 1) * HALF)
            near_edge = near[i][: (half + 1) * HALF, a]
            near_pieces = [s[:, a] for s in near[:i]]
            if half == 1:
                near_pieces.append(near_edge[:HALF])
            near_pieces.append(jnp.where(causal, near_edge[half * HALF :], MASKED))
            far_pieces = []
            if far_there:
                far_edge = far[0][half * HALF :, a]
                far_pieces.append(jnp.where(causal, MASKED, far_edge[:HALF]))
                if half == 0:
                    far_pieces.append(far_edge[HALF:])
                far_pieces += [s[:, a] for s in far[1:]]
            top = top_of(near_pieces + far_pieces)
            near_weights = [weights_of(s, top) for s in near_pieces]
            if half == 0:
                near_weights.append(nothing)
            near_columns.append(jnp.concatenate(near_weights, axis=0))
            if far_there:
                far_weights = [weights_of(s, top) for s in far_pieces]
                if half == 1:
                    far_weights.insert(0, nothing)
                far_columns.append(jnp.concatenate(far_weights, axis=0))
            queries = slice(i * TILE + half * HALF, i * TILE + (half + 1) * HALF)
            tops[h : h + 1, queries] = top
        if far_there:
            weights_far[h, i * TILE :, blocks[i]] = jnp.concatenate(far_columns, axis=1)
        return jnp.concatenate(near_columns, axis=1)

    def multiply(unit, weights):
        h, i = unit
        out[head_rows(h), blocks[i]] = dot(v_t[h // group][:, : (i + 1) * TILE], weights, 1, 0)

    in_steps(units_of(group, tok, kv_heads), [score, weigh, multiply])


def middle_kernel(group, *refs):
    place = lax.axis_index("seq")

    @pl.when(place >= 2)
    def _():
        middle_steps(group, True, *refs)

    @pl.when(place == 1)
    def _():
        middle_steps(group, False, *refs)

    @pl.when(place == 0)
    def _():
        q, own, k, out, stage, sems = refs[0], refs[1], refs[4], refs[10], refs[11], refs[12]
        kv_heads = range(k.shape[1] // HEAD_WIDTH)
        write_steps(
            group, kv_heads, q.shape[0], lambda h, b: own[head_rows(h), b], out, stage, sems
        )


def middle_steps(
    group, far_there, q, own, weights_far, tops, k_1, k_2, v_a, v_b, rest, weights, *_
):
    k, v_far = (k_1, k_2), (v_a, v_b)
    tok = q.shape[0]
    kv_heads = range(k_1.shape[1] // HEAD_WIDTH)
    v_t = []
    if far_there:
        v_t = [values_and_ones(v_far[g // PAIR], head_columns(g % PAIR)) for g in kv_heads]
    tiles = tok // TILE
    blocks = [slice(i * TILE, (i + 1) * TILE) for i in range(tiles)]

    def score(unit, _):
        h, i = unit
        qh = q[blocks[i], head_columns(h)]
        return [dot(tile(k, j, head_columns(h // group)), qh, 1, 1) for j in range(tiles)]

    def weigh(unit, scores):
        h, i = unit
        before = tops[h : h + 1, blocks[i]]
        top = jnp.maximum(before, top_of(scores))
        for j, s in enumerate(scores):
            weights[h, blocks[j], blocks[i]] = weights_of(s, top)
        return jnp.exp2((before - top) * EXPONENT)

    def multiply(unit, less):
        h, i = unit
        total = own[head_rows(h), blocks[i]]
        if far_there:
            total += dot(v_t[h // group][:, i * TILE :], weights_far[h, i * TILE :, blocks[i]], 1, 0)
        rest[head_rows(h), blocks[i]] = total * less

    in_steps(units_of(group, tok, kv_heads), [score, weigh, multiply])


def write_steps(group, kv_heads, tok, total_of, out, stage, sems):
    copies = []
    for h, i in units_of(group, tok, kv_heads):
        b = slice(i * TILE, (i + 1) * TILE)
        total = total_of(h, b)
        normal = total[:HEAD_WIDTH] * (1.0 / total[HEAD_WIDTH : HEAD_WIDTH + 1])
        stage[b, head_columns(h)] = normal.astype(jnp.bfloat16).T
        if h % group == group - 1:
            width = group * HEAD_WIDTH
            part = (pl.ds(i * TILE, TILE), pl.ds((h + 1) * HEAD_WIDTH - width, width))
            copies.append(
                pltpu.make_async_copy(stage.at[part], out.at[part], sems.at[len(copies)])
            )
            copies[-1].start()
    for copy in copies:
        copy.wait()


def finish_kernel(group, rest, weights, v, _, out, stage, sems, part):
    tok = weights.shape[1]
    kv_heads = range(part * PAIR, (part + 1) * PAIR)

    @pl.when(lax.axis_index("seq") >= 1)
    def _():
        v_t = [values_and_ones(v, head_columns(g % PAIR)) for g in kv_heads]
        units = units_of(group, tok, kv_heads)
        held = []

        def total_of(h, b):
            at = units.index((h, b.start // TILE))
            for m, i in units[len(held) : at + 2]:
                c = slice(i * TILE, (i + 1) * TILE)
                held.append(dot(v_t[m // group - part * PAIR], weights[m, :, c], 1, 0))
            return rest[head_rows(h), b] + held[at]

        write_steps(group, kv_heads, tok, total_of, out, stage, sems)


def by_heads(
    kernel, name, query_shape, columns, arrays, out_kinds, into=None, own_copies=False
):
    tok, width = query_shape
    heads = width // HEAD_WIDTH
    shapes = dict(
        queries=((tok, width), jnp.bfloat16),
        rest=((heads * (HEAD_WIDTH + ONES), tok), jnp.float32),
        weights=((heads, tok, tok), jnp.bfloat16),
        stat=((heads, tok), jnp.float32),
        output=((tok, width), jnp.bfloat16),
    )
    in_vmem, anywhere = pl.BlockSpec(memory_space=pltpu.VMEM), pl.BlockSpec(memory_space=pl.ANY)
    in_specs = [in_vmem] * len(arrays)
    aliases, scratch = {}, []
    if own_copies:
        in_specs[0] = pl.BlockSpec(memory_space=pltpu.HBM)
        scratch = [pltpu.SemaphoreType.DMA((columns // HEAD_WIDTH,))]
    if into is not None:
        aliases = {len(arrays): out_kinds.index("output")}
        arrays.append(into)
        in_specs.append(anywhere)
    if "output" in out_kinds:
        copies = columns // HEAD_WIDTH * (tok // TILE)
        scratch = [
            pltpu.VMEM((tok, width), jnp.bfloat16),
            pltpu.SemaphoreType.DMA((copies,)),
        ]
    return pl.pallas_call(
        functools.partial(kernel, width // columns),
        in_specs=in_specs,
        out_specs=[anywhere if kind == "output" else in_vmem for kind in out_kinds],
        scratch_shapes=scratch,
        out_shape=[jax.ShapeDtypeStruct(*shapes[kind]) for kind in out_kinds],
        input_output_aliases=aliases,
        compiler_params=pltpu.CompilerParams(vmem_limit_bytes=24 * 1024 * 1024),
        name=name,
    )(*arrays)


def shifted(array, steps):
    count = lax.axis_size("seq")
    return lax.ppermute(array, "seq", [(source, source + steps) for source in range(count - steps)])


def exchanged(array, axis, bit):
    count = lax.axis_size(axis)
    return lax.ppermute(array, axis, [(source, source ^ bit) for source in range(count)])


def on_device(
    normed_input, query, key, value, adapter_down_maps, adapter_up_maps, block_adapter_choice
):
    tok = query.shape[0]
    assert 2 * tok == WINDOW and SEG_LEN % tok == 0
    where = lax.axis_index("seq")
    choice = block_adapter_choice

    even = where % 2 == 0
    barrier = lax.optimization_barrier
    call = functools.partial(by_heads, query_shape=query.shape, columns=key.shape[1])

    def from_one_back(own, far):
        return exchanged(jnp.where(even, own, far), "seq", 1)

    key_1 = first_half(key)
    key_far_1 = shifted(key_1, 2)
    latent, up, key_2 = latent_share(
        choice, normed_input.T, adapter_down_maps, adapter_up_maps, key
    )
    key_far_2 = shifted(key_2, 2)
    bit = lax.axis_size("tp") // 2
    while bit > 1:
        latent = latent + exchanged(latent, "tp", bit)
        bit //= 2
    key_1, latent = barrier((key_1, latent))
    theirs = exchanged(latent, "tp", bit)
    key_mid_1 = from_one_back(key_1, key_far_1)
    values = adapt(latent, theirs, up, value)
    value_far = [shifted(part, 2) for part in values]
    key_2, values = barrier((key_2, values))
    key_mid_2 = from_one_back(key_2, key_far_2)
    values, key_mid_1 = barrier((values, key_mid_1))
    queries, own, weights_far, tops = call(
        near_far_kernel,
        "near_far",
        arrays=[in_hbm(query), key_1, key_2, *values, key_far_1, key_far_2],
        out_kinds=["queries", "rest", "weights", "stat"],
        own_copies=True,
    )
    values, own = barrier((values, own))
    value_mid = [from_one_back(mine, theirs) for mine, theirs in zip(values, value_far)]
    rest, weights_mid, done = call(
        middle_kernel,
        "middle",
        arrays=[queries, own, weights_far, tops, key_mid_1, key_mid_2, *value_far],
        out_kinds=["rest", "weights", "output"],
    )
    for n, part in enumerate(value_mid):
        [done] = call(
            functools.partial(finish_kernel, part=n),
            "finish",
                arrays=[rest, weights_mid, part],
            out_kinds=["output"],
            into=done,
        )
    return done


def solution(mesh):
    placed = (
        P("seq", "tp"),
        P("seq", "tp"),
        P("seq", "tp"),
        P("seq", "tp"),
        P(None, None, "tp"),
        P(None, None, "tp"),
        P(),
    )
    return jax.shard_map(
        on_device, mesh=mesh, in_specs=placed, out_specs=P("seq", "tp"), check_vma=False
    )
```

```python
import functools

import jax
import jax.numpy as jnp
from jax import lax
from jax.experimental import pallas as pl
from jax.experimental.pallas import tpu as pltpu
from jax.sharding import PartitionSpec as P

HEAD_WIDTH = 128
WINDOW = 1024
SEG_LEN = 2048
SCALE = 168.0 ** (-0.5)
LOG2_E = 1.4426950408889634
EXPONENT = SCALE * LOG2_E
MASKED = -1e30
TILE = 256
HALF = 128
ONES = 16
PAIR = 2
PIECE = 256


def params(steps, mib):
    return pltpu.CompilerParams(
        vmem_limit_bytes=mib * 1024 * 1024, dimension_semantics=("arbitrary",) * steps
    )


def dot(left, right, left_dim, right_dim):
    return lax.dot_general(
        left, right, (((left_dim,), (right_dim,)), ((), ())), preferred_element_type=jnp.float32
    )


def in_hbm(array):
    return pltpu.with_memory_space_constraint(array, pltpu.HBM)


def adapter_of(choice, tok):
    return choice[lax.div(lax.axis_index("seq") * tok, SEG_LEN)]


def first_half_kernel(key, out, sem):
    copy = pltpu.make_async_copy(key.at[pl.ds(0, out.shape[0])], out, sem)
    copy.start()
    copy.wait()


def first_half(key):
    rows, columns = key.shape
    return pl.pallas_call(
        first_half_kernel,
        in_specs=[pl.BlockSpec(memory_space=pltpu.HBM)],
        out_specs=pl.BlockSpec(memory_space=pltpu.VMEM),
        out_shape=jax.ShapeDtypeStruct((rows // 2, columns), key.dtype),
        scratch_shapes=[pltpu.SemaphoreType.DMA],
        compiler_params=pltpu.CompilerParams(vmem_limit_bytes=8 * 1024 * 1024),
        name="first_half",
    )(in_hbm(key))


def latent_kernel(
    pieces, choice, input_t, down, up, key, out, up_out, key_out, ids, rows, map_rows, sems
):
    half = key_out.shape[0]
    ids_copy = pltpu.make_async_copy(choice, ids, sems.at[0])
    ids_copy.start()
    copies = []
    for n, (first, last) in enumerate(pieces):
        part = pl.ds(first, last - first)
        copies.append(pltpu.make_async_copy(input_t.at[part], rows.at[part], sems.at[n + 4]))
        copies[-1].start()
    key_copy = pltpu.make_async_copy(key.at[pl.ds(half, half)], key_out, sems.at[1])
    key_copy.start()
    ids_copy.wait()
    chosen = adapter_of(ids, out.shape[1])
    down_copy = pltpu.make_async_copy(down.at[chosen], map_rows, sems.at[2])
    up_copy = pltpu.make_async_copy(up.at[chosen], up_out, sems.at[3])
    down_copy.start()
    up_copy.start()
    down_copy.wait()
    total = None
    for (first, last), copy in zip(pieces, copies):
        copy.wait()
        product = dot(map_rows[:, first:last], rows[first:last, :], 1, 0)
        total = product if total is None else total + product
    out[...] = total
    up_copy.wait()
    key_copy.wait()


def latent_share(choice, input_t, down_maps, up_maps, key):
    features, tok = input_t.shape
    rank, columns = up_maps.shape[1:]
    pieces = [(first, min(first + PIECE, features)) for first in range(0, features, PIECE)]
    return pl.pallas_call(
        functools.partial(latent_kernel, pieces),
        in_specs=[pl.BlockSpec(memory_space=pltpu.HBM)] * 5,
        out_specs=[pl.BlockSpec(memory_space=pltpu.VMEM)] * 3,
        out_shape=[
            jax.ShapeDtypeStruct((rank, tok), jnp.float32),
            jax.ShapeDtypeStruct((rank, columns), up_maps.dtype),
            jax.ShapeDtypeStruct((tok // 2, columns), key.dtype),
        ],
        scratch_shapes=[
            pltpu.SMEM(choice.shape, choice.dtype),
            pltpu.VMEM((features, tok), input_t.dtype),
            pltpu.VMEM((rank, features), down_maps.dtype),
            pltpu.SemaphoreType.DMA((len(pieces) + 4,)),
        ],
        compiler_params=pltpu.CompilerParams(vmem_limit_bytes=8 * 1024 * 1024),
        name="latent_share",
    )(*(in_hbm(array) for array in (choice, input_t, down_maps, up_maps, key)))


def adapt_kernel(mine, theirs, up, value, *outs):
    latent = (mine[...] + theirs[...]).astype(jnp.bfloat16)
    update = dot(latent, up[...], 0, 0)
    total = (value[...].astype(jnp.float32) + update).astype(jnp.bfloat16)
    for n, out in enumerate(outs):
        width = out.shape[1]
        out[...] = total[:, n * width : (n + 1) * width]


def adapt(mine, theirs, up, value):
    tok, columns = value.shape
    width = PAIR * HEAD_WIDTH
    return pl.pallas_call(
        adapt_kernel,
        out_shape=[jax.ShapeDtypeStruct((tok, width), jnp.bfloat16)] * (columns // width),
        compiler_params=pltpu.CompilerParams(vmem_limit_bytes=8 * 1024 * 1024),
        name="adapt_values",
    )(mine, theirs, up, value)


def weights_of(scores, top):
    return jnp.exp2(((scores - top) * EXPONENT).astype(jnp.bfloat16))


def tree(operation, items):
    items = list(items)
    while len(items) > 1:
        items = [
            operation(items[n], items[n + 1]) if n + 1 < len(items) else items[n]
            for n in range(0, len(items), 2)
        ]
    return items[0]


def top_of(scores):
    pieces = [s[n : n + 32] for s in scores for n in range(0, s.shape[0], 32)]
    pieces = tree(jnp.maximum, pieces)
    pieces = tree(jnp.maximum, [pieces[n : n + 8] for n in range(0, 32, 8)])
    return jnp.max(pieces, axis=0, keepdims=True)


def values_and_ones(v, columns):
    turned = v[:, columns].T
    return jnp.concatenate([turned, jnp.ones((ONES, v.shape[0]), jnp.bfloat16)], axis=0)


def tile(halves, j, columns):
    rows = halves[0].shape[0]
    first = j * TILE % rows
    return halves[j * TILE // rows][first : first + TILE, columns]


def head_rows(h):
    return slice(h * (HEAD_WIDTH + ONES), (h + 1) * (HEAD_WIDTH + ONES))


def head_columns(h):
    return slice(h * HEAD_WIDTH, (h + 1) * HEAD_WIDTH)


def in_steps(units, stages):
    held = [None] * len(units)
    for step in range(len(units) + len(stages) - 1):
        for n, stage in enumerate(stages):
            if 0 <= step - n < len(units):
                held[step - n] = stage(units[step - n], held[step - n])


def units_of(group, tok, kv_heads):
    return [
        (h, i)
        for g in kv_heads
        for i in range(tok // TILE)
        for h in range(g * group, (g + 1) * group)
    ]


def near_far_kernel(group, *refs):
    place = lax.axis_index("seq")

    @pl.when(place >= 2)
    def _():
        near_far_steps(group, True, *refs)

    @pl.when(place < 2)
    def _():
        near_far_steps(group, False, *refs)


def near_far_steps(
    group, far_there, q, k_1, k_2, v_a, v_b, k_far_1, k_far_2, out, weights_far, tops
):
    k, v, k_far = (k_1, k_2), (v_a, v_b), (k_far_1, k_far_2)
    tok = q.shape[0]
    kv_heads = range(k_1.shape[1] // HEAD_WIDTH)
    causal = lax.broadcasted_iota(jnp.int32, (HALF, HALF), 0) <= lax.broadcasted_iota(
        jnp.int32, (HALF, HALF), 1
    )
    v_t = [values_and_ones(v[g // PAIR], head_columns(g % PAIR)) for g in kv_heads]
    nothing = jnp.zeros((HALF, HALF), jnp.bfloat16)
    tiles = tok // TILE
    blocks = [slice(i * TILE, (i + 1) * TILE) for i in range(tiles)]

    def score(unit, _):
        h, i = unit
        qh = q[blocks[i], head_columns(h)]
        columns = head_columns(h // group)
        near = [dot(tile(k, j, columns), qh, 1, 1) for j in range(i + 1)]
        far = []
        if far_there:
            far = [dot(tile(k_far, j, columns), qh, 1, 1) for j in range(i, tiles)]
        return near, far

    def weigh(unit, scores):
        h, i = unit
        near, far = scores
        near_columns, far_columns = [], []
        for half in range(2):
            a = slice(half * HALF, (half + 1) * HALF)
            near_edge = near[i][: (half + 1) * HALF, a]
            near_pieces = [s[:, a] for s in near[:i]]
            if half == 1:
                near_pieces.append(near_edge[:HALF])
            near_pieces.append(jnp.where(causal, near_edge[half * HALF :], MASKED))
            far_pieces = []
            if far_there:
                far_edge = far[0][half * HALF :, a]
                far_pieces.append(jnp.where(causal, MASKED, far_edge[:HALF]))
                if half == 0:
                    far_pieces.append(far_edge[HALF:])
                far_pieces += [s[:, a] for s in far[1:]]
            top = top_of(near_pieces + far_pieces)
            near_weights = [weights_of(s, top) for s in near_pieces]
            if half == 0:
                near_weights.append(nothing)
            near_columns.append(jnp.concatenate(near_weights, axis=0))
            if far_there:
                far_weights = [weights_of(s, top) for s in far_pieces]
                if half == 1:
                    far_weights.insert(0, nothing)
                far_columns.append(jnp.concatenate(far_weights, axis=0))
            queries = slice(i * TILE + half * HALF, i * TILE + (half + 1) * HALF)
            tops[h : h + 1, queries] = top
        if far_there:
            weights_far[h, i * TILE :, blocks[i]] = jnp.concatenate(far_columns, axis=1)
        return jnp.concatenate(near_columns, axis=1)

    def multiply(unit, weights):
        h, i = unit
        out[head_rows(h), blocks[i]] = dot(v_t[h // group][:, : (i + 1) * TILE], weights, 1, 0)

    in_steps(units_of(group, tok, kv_heads), [score, weigh, multiply])


def middle_kernel(group, *refs):
    place = lax.axis_index("seq")

    @pl.when(place >= 2)
    def _():
        middle_steps(group, True, *refs)

    @pl.when(place == 1)
    def _():
        middle_steps(group, False, *refs)

    @pl.when(place == 0)
    def _():
        q, own, k, out, stage, sems = refs[0], refs[1], refs[4], refs[10], refs[11], refs[12]
        kv_heads = range(k.shape[1] // HEAD_WIDTH)
        write_steps(
            group, kv_heads, q.shape[0], lambda h, b: own[head_rows(h), b], out, stage, sems
        )


def middle_steps(
    group, far_there, q, own, weights_far, tops, k_1, k_2, v_a, v_b, rest, weights, *_
):
    k, v_far = (k_1, k_2), (v_a, v_b)
    tok = q.shape[0]
    kv_heads = range(k_1.shape[1] // HEAD_WIDTH)
    v_t = []
    if far_there:
        v_t = [values_and_ones(v_far[g // PAIR], head_columns(g % PAIR)) for g in kv_heads]
    tiles = tok // TILE
    blocks = [slice(i * TILE, (i + 1) * TILE) for i in range(tiles)]

    def score(unit, _):
        h, i = unit
        qh = q[blocks[i], head_columns(h)]
        return [dot(tile(k, j, head_columns(h // group)), qh, 1, 1) for j in range(tiles)]

    def weigh(unit, scores):
        h, i = unit
        before = tops[h : h + 1, blocks[i]]
        top = jnp.maximum(before, top_of(scores))
        for j, s in enumerate(scores):
            weights[h, blocks[j], blocks[i]] = weights_of(s, top)
        return jnp.exp2((before - top) * EXPONENT)

    def multiply(unit, less):
        h, i = unit
        total = own[head_rows(h), blocks[i]]
        if far_there:
            total += dot(v_t[h // group][:, i * TILE :], weights_far[h, i * TILE :, blocks[i]], 1, 0)
        rest[head_rows(h), blocks[i]] = total * less

    in_steps(units_of(group, tok, kv_heads), [score, weigh, multiply])


def write_steps(group, kv_heads, tok, total_of, out, stage, sems):
    copies = []
    for h, i in units_of(group, tok, kv_heads):
        b = slice(i * TILE, (i + 1) * TILE)
        total = total_of(h, b)
        normal = total[:HEAD_WIDTH] * (1.0 / total[HEAD_WIDTH : HEAD_WIDTH + 1])
        stage[b, head_columns(h)] = normal.astype(jnp.bfloat16).T
        if h % group == group - 1:
            width = group * HEAD_WIDTH
            part = (pl.ds(i * TILE, TILE), pl.ds((h + 1) * HEAD_WIDTH - width, width))
            copies.append(
                pltpu.make_async_copy(stage.at[part], out.at[part], sems.at[len(copies)])
            )
            copies[-1].start()
    for copy in copies:
        copy.wait()


def finish_kernel(group, rest, weights, v, _, out, stage, sems, part):
    tok = weights.shape[1]
    kv_heads = range(part * PAIR, (part + 1) * PAIR)

    @pl.when(lax.axis_index("seq") >= 1)
    def _():
        v_t = [values_and_ones(v, head_columns(g % PAIR)) for g in kv_heads]
        units = units_of(group, tok, kv_heads)
        held = []

        def total_of(h, b):
            at = units.index((h, b.start // TILE))
            for m, i in units[len(held) : at + 2]:
                c = slice(i * TILE, (i + 1) * TILE)
                held.append(dot(v_t[m // group - part * PAIR], weights[m, :, c], 1, 0))
            return rest[head_rows(h), b] + held[at]

        write_steps(group, kv_heads, tok, total_of, out, stage, sems)


def by_heads(
    kernel, name, query_shape, columns, arrays, out_kinds, into=None
):
    tok, width = query_shape
    heads = width // HEAD_WIDTH
    shapes = dict(
        rest=((heads * (HEAD_WIDTH + ONES), tok), jnp.float32),
        weights=((heads, tok, tok), jnp.bfloat16),
        stat=((heads, tok), jnp.float32),
        output=((tok, width), jnp.bfloat16),
    )
    in_vmem, anywhere = pl.BlockSpec(memory_space=pltpu.VMEM), pl.BlockSpec(memory_space=pl.ANY)
    in_specs = [in_vmem] * len(arrays)
    aliases, scratch = {}, []
    if into is not None:
        aliases = {len(arrays): out_kinds.index("output")}
        arrays.append(into)
        in_specs.append(anywhere)
    if "output" in out_kinds:
        copies = columns // HEAD_WIDTH * (tok // TILE)
        scratch = [
            pltpu.VMEM((tok, width), jnp.bfloat16),
            pltpu.SemaphoreType.DMA((copies,)),
        ]
    return pl.pallas_call(
        functools.partial(kernel, width // columns),
        in_specs=in_specs,
        out_specs=[anywhere if kind == "output" else in_vmem for kind in out_kinds],
        scratch_shapes=scratch,
        out_shape=[jax.ShapeDtypeStruct(*shapes[kind]) for kind in out_kinds],
        input_output_aliases=aliases,
        compiler_params=pltpu.CompilerParams(vmem_limit_bytes=24 * 1024 * 1024),
        name=name,
    )(*arrays)


def shifted(array, steps):
    count = lax.axis_size("seq")
    return lax.ppermute(array, "seq", [(source, source + steps) for source in range(count - steps)])


def exchanged(array, axis, bit):
    count = lax.axis_size(axis)
    return lax.ppermute(array, axis, [(source, source ^ bit) for source in range(count)])


def on_device(
    normed_input, query, key, value, adapter_down_maps, adapter_up_maps, block_adapter_choice
):
    tok = query.shape[0]
    assert 2 * tok == WINDOW and SEG_LEN % tok == 0
    where = lax.axis_index("seq")
    choice = block_adapter_choice

    even = where % 2 == 0
    barrier = lax.optimization_barrier
    call = functools.partial(by_heads, query_shape=query.shape, columns=key.shape[1])

    def from_one_back(own, far):
        return exchanged(jnp.where(even, own, far), "seq", 1)

    key_1 = first_half(key)
    key_far_1 = shifted(key_1, 2)
    latent, up, key_2 = latent_share(
        choice, normed_input.T, adapter_down_maps, adapter_up_maps, key
    )
    key_far_2 = shifted(key_2, 2)
    bit = lax.axis_size("tp") // 2
    while bit > 1:
        latent = latent + exchanged(latent, "tp", bit)
        bit //= 2
    key_1, latent = barrier((key_1, latent))
    theirs = exchanged(latent, "tp", bit)
    key_mid_1 = from_one_back(key_1, key_far_1)
    values = adapt(latent, theirs, up, value)
    value_far = [shifted(part, 2) for part in values]
    key_2, values = barrier((key_2, values))
    key_mid_2 = from_one_back(key_2, key_far_2)
    values, key_mid_1 = barrier((values, key_mid_1))
    own, weights_far, tops = call(
        near_far_kernel,
        "near_far",
        arrays=[query, key_1, key_2, *values, key_far_1, key_far_2],
        out_kinds=["rest", "weights", "stat"],
    )
    values, own = barrier((values, own))
    value_mid = [from_one_back(mine, theirs) for mine, theirs in zip(values, value_far)]
    rest, weights_mid, done = call(
        middle_kernel,
        "middle",
        arrays=[query, own, weights_far, tops, key_mid_1, key_mid_2, *value_far],
        out_kinds=["rest", "weights", "output"],
    )
    for n, part in enumerate(value_mid):
        [done] = call(
            functools.partial(finish_kernel, part=n),
            "finish",
            arrays=[rest, weights_mid, part],
            out_kinds=["output"],
            into=done,
        )
    return done


def solution(mesh):
    placed = (
        P("seq", "tp"),
        P("seq", "tp"),
        P("seq", "tp"),
        P("seq", "tp"),
        P(None, None, "tp"),
        P(None, None, "tp"),
        P(),
    )
    return jax.shard_map(
        on_device, mesh=mesh, in_specs=placed, out_specs=P("seq", "tp"), check_vma=False
    )
```

```python
import functools

import jax
import jax.numpy as jnp
from jax import lax
from jax.experimental import pallas as pl
from jax.experimental.pallas import tpu as pltpu
from jax.sharding import PartitionSpec as P

HEAD_WIDTH = 128
WINDOW = 1024
SEG_LEN = 2048
SCALE = 168.0 ** (-0.5)
LOG2_E = 1.4426950408889634
EXPONENT = SCALE * LOG2_E
MASKED = -1e30
TILE = 256
HALF = 128
ONES = 16
PAIR = 2
PIECE = 256


def params(steps, mib):
    return pltpu.CompilerParams(
        vmem_limit_bytes=mib * 1024 * 1024, dimension_semantics=("arbitrary",) * steps
    )


def dot(left, right, left_dim, right_dim):
    return lax.dot_general(
        left, right, (((left_dim,), (right_dim,)), ((), ())), preferred_element_type=jnp.float32
    )


def in_hbm(array):
    return pltpu.with_memory_space_constraint(array, pltpu.HBM)


def adapter_of(choice, tok):
    return choice[lax.div(lax.axis_index("seq") * tok, SEG_LEN)]


def first_half_kernel(key, out, sem):
    copy = pltpu.make_async_copy(key.at[pl.ds(0, out.shape[0])], out, sem)
    copy.start()
    copy.wait()


def first_half(key):
    rows, columns = key.shape
    return pl.pallas_call(
        first_half_kernel,
        in_specs=[pl.BlockSpec(memory_space=pltpu.HBM)],
        out_specs=pl.BlockSpec(memory_space=pltpu.VMEM),
        out_shape=jax.ShapeDtypeStruct((rows // 2, columns), key.dtype),
        scratch_shapes=[pltpu.SemaphoreType.DMA],
        compiler_params=pltpu.CompilerParams(vmem_limit_bytes=8 * 1024 * 1024),
        name="first_half",
    )(in_hbm(key))


def latent_kernel(
    pieces, choice, input_t, down, up, key, out, up_out, key_out, ids, rows, map_rows, sems
):
    half = key_out.shape[0]
    ids_copy = pltpu.make_async_copy(choice, ids, sems.at[0])
    ids_copy.start()
    copies = []
    for n, (first, last) in enumerate(pieces):
        part = pl.ds(first, last - first)
        copies.append(pltpu.make_async_copy(input_t.at[part], rows.at[part], sems.at[n + 4]))
        copies[-1].start()
    key_copy = pltpu.make_async_copy(key.at[pl.ds(half, half)], key_out, sems.at[1])
    key_copy.start()
    ids_copy.wait()
    chosen = adapter_of(ids, out.shape[1])
    down_copy = pltpu.make_async_copy(down.at[chosen], map_rows, sems.at[2])
    up_copy = pltpu.make_async_copy(up.at[chosen], up_out, sems.at[3])
    down_copy.start()
    up_copy.start()
    down_copy.wait()
    total = None
    for (first, last), copy in zip(pieces, copies):
        copy.wait()
        product = dot(map_rows[:, first:last], rows[first:last, :], 1, 0)
        total = product if total is None else total + product
    out[...] = total
    up_copy.wait()
    key_copy.wait()


def latent_share(choice, input_t, down_maps, up_maps, key):
    features, tok = input_t.shape
    rank, columns = up_maps.shape[1:]
    pieces = [(first, min(first + PIECE, features)) for first in range(0, features, PIECE)]
    return pl.pallas_call(
        functools.partial(latent_kernel, pieces),
        in_specs=[pl.BlockSpec(memory_space=pltpu.HBM)] * 5,
        out_specs=[pl.BlockSpec(memory_space=pltpu.VMEM)] * 3,
        out_shape=[
            jax.ShapeDtypeStruct((rank, tok), jnp.float32),
            jax.ShapeDtypeStruct((rank, columns), up_maps.dtype),
            jax.ShapeDtypeStruct((tok // 2, columns), key.dtype),
        ],
        scratch_shapes=[
            pltpu.SMEM(choice.shape, choice.dtype),
            pltpu.VMEM((features, tok), input_t.dtype),
            pltpu.VMEM((rank, features), down_maps.dtype),
            pltpu.SemaphoreType.DMA((len(pieces) + 4,)),
        ],
        compiler_params=pltpu.CompilerParams(vmem_limit_bytes=8 * 1024 * 1024),
        name="latent_share",
    )(*(in_hbm(array) for array in (choice, input_t, down_maps, up_maps, key)))


def adapt_kernel(mine, theirs, up, value, *outs):
    latent = (mine[...] + theirs[...]).astype(jnp.bfloat16)
    update = dot(latent, up[...], 0, 0)
    total = (value[...].astype(jnp.float32) + update).astype(jnp.bfloat16)
    for n, out in enumerate(outs):
        width = out.shape[1]
        out[...] = total[:, n * width : (n + 1) * width]


def adapt(mine, theirs, up, value):
    tok, columns = value.shape
    width = PAIR * HEAD_WIDTH
    return pl.pallas_call(
        adapt_kernel,
        out_shape=[jax.ShapeDtypeStruct((tok, width), jnp.bfloat16)] * (columns // width),
        compiler_params=pltpu.CompilerParams(vmem_limit_bytes=8 * 1024 * 1024),
        name="adapt_values",
    )(mine, theirs, up, value)


def weights_of(scores, top):
    return jnp.exp2(((scores - top) * EXPONENT).astype(jnp.bfloat16))


def tree(operation, items):
    items = list(items)
    while len(items) > 1:
        items = [
            operation(items[n], items[n + 1]) if n + 1 < len(items) else items[n]
            for n in range(0, len(items), 2)
        ]
    return items[0]


def top_of(scores):
    pieces = [s[n : n + 32] for s in scores for n in range(0, s.shape[0], 32)]
    pieces = tree(jnp.maximum, pieces)
    pieces = tree(jnp.maximum, [pieces[n : n + 8] for n in range(0, 32, 8)])
    return jnp.max(pieces, axis=0, keepdims=True)


def values_and_ones(v, columns):
    turned = v[:, columns].T
    return jnp.concatenate([turned, jnp.ones((ONES, v.shape[0]), jnp.bfloat16)], axis=0)


def tile(halves, j, columns):
    rows = halves[0].shape[0]
    first = j * TILE % rows
    return halves[j * TILE // rows][first : first + TILE, columns]


def head_rows(h):
    return slice(h * (HEAD_WIDTH + ONES), (h + 1) * (HEAD_WIDTH + ONES))


def head_columns(h):
    return slice(h * HEAD_WIDTH, (h + 1) * HEAD_WIDTH)


def in_steps(units, stages):
    held = [None] * len(units)
    for step in range(len(units) + len(stages) - 1):
        for n, stage in enumerate(stages):
            if 0 <= step - n < len(units):
                held[step - n] = stage(units[step - n], held[step - n])


def units_of(group, tok, kv_heads):
    return [
        (h, i)
        for g in kv_heads
        for i in range(tok // TILE)
        for h in range(g * group, (g + 1) * group)
    ]


def near_far_kernel(group, *refs):
    place = lax.axis_index("seq")

    @pl.when(place >= 2)
    def _():
        near_far_steps(group, True, *refs)

    @pl.when(place < 2)
    def _():
        near_far_steps(group, False, *refs)


def near_far_steps(
    group, far_there, q, k_1, k_2, v_a, v_b, k_far_1, k_far_2, out, weights_far, tops
):
    k, v, k_far = (k_1, k_2), (v_a, v_b), (k_far_1, k_far_2)
    tok = q.shape[0]
    kv_heads = range(k_1.shape[1] // HEAD_WIDTH)
    causal = lax.broadcasted_iota(jnp.int32, (HALF, HALF), 0) <= lax.broadcasted_iota(
        jnp.int32, (HALF, HALF), 1
    )
    v_t = [values_and_ones(v[g // PAIR], head_columns(g % PAIR)) for g in kv_heads]
    nothing = jnp.zeros((HALF, HALF), jnp.bfloat16)
    tiles = tok // TILE
    blocks = [slice(i * TILE, (i + 1) * TILE) for i in range(tiles)]

    def score(unit, _):
        h, i = unit
        qh = q[blocks[i], head_columns(h)]
        columns = head_columns(h // group)
        near = [dot(tile(k, j, columns), qh, 1, 1) for j in range(i + 1)]
        far = []
        if far_there:
            far = [dot(tile(k_far, j, columns), qh, 1, 1) for j in range(i, tiles)]
        return near, far

    def weigh(unit, scores):
        h, i = unit
        near, far = scores
        near_columns, far_columns = [], []
        for half in range(2):
            a = slice(half * HALF, (half + 1) * HALF)
            near_edge = near[i][: (half + 1) * HALF, a]
            near_pieces = [s[:, a] for s in near[:i]]
            if half == 1:
                near_pieces.append(near_edge[:HALF])
            near_pieces.append(jnp.where(causal, near_edge[half * HALF :], MASKED))
            far_pieces = []
            if far_there:
                far_edge = far[0][half * HALF :, a]
                far_pieces.append(jnp.where(causal, MASKED, far_edge[:HALF]))
                if half == 0:
                    far_pieces.append(far_edge[HALF:])
                far_pieces += [s[:, a] for s in far[1:]]
            top = top_of(near_pieces + far_pieces)
            near_weights = [weights_of(s, top) for s in near_pieces]
            if half == 0:
                near_weights.append(nothing)
            near_columns.append(jnp.concatenate(near_weights, axis=0))
            if far_there:
                far_weights = [weights_of(s, top) for s in far_pieces]
                if half == 1:
                    far_weights.insert(0, nothing)
                far_columns.append(jnp.concatenate(far_weights, axis=0))
            queries = slice(i * TILE + half * HALF, i * TILE + (half + 1) * HALF)
            tops[h : h + 1, queries] = top
        if far_there:
            weights_far[h, i * TILE :, blocks[i]] = jnp.concatenate(far_columns, axis=1)
        return jnp.concatenate(near_columns, axis=1)

    def multiply(unit, weights):
        h, i = unit
        out[head_rows(h), blocks[i]] = dot(v_t[h // group][:, : (i + 1) * TILE], weights, 1, 0)

    in_steps(units_of(group, tok, kv_heads), [score, weigh, multiply])


def middle_kernel(group, *refs):
    place = lax.axis_index("seq")

    @pl.when(place >= 2)
    def _():
        middle_steps(group, True, *refs)

    @pl.when(place == 1)
    def _():
        middle_steps(group, False, *refs)

    @pl.when(place == 0)
    def _():
        q, own, k, out, stage, sems = refs[0], refs[1], refs[4], refs[10], refs[11], refs[12]
        kv_heads = range(k.shape[1] // HEAD_WIDTH)
        write_steps(
            group, kv_heads, q.shape[0], lambda h, b: own[head_rows(h), b], out, stage, sems
        )


def middle_steps(
    group, far_there, q, own, weights_far, tops, k_1, k_2, v_a, v_b, rest, weights, *_
):
    k, v_far = (k_1, k_2), (v_a, v_b)
    tok = q.shape[0]
    kv_heads = range(k_1.shape[1] // HEAD_WIDTH)
    v_t = []
    if far_there:
        v_t = [values_and_ones(v_far[g // PAIR], head_columns(g % PAIR)) for g in kv_heads]
    tiles = tok // TILE
    blocks = [slice(i * TILE, (i + 1) * TILE) for i in range(tiles)]

    def score(unit, _):
        h, i = unit
        qh = q[blocks[i], head_columns(h)]
        return [dot(tile(k, j, head_columns(h // group)), qh, 1, 1) for j in range(tiles)]

    def weigh(unit, scores):
        h, i = unit
        before = tops[h : h + 1, blocks[i]]
        top = jnp.maximum(before, top_of(scores))
        for j, s in enumerate(scores):
            weights[h, blocks[j], blocks[i]] = weights_of(s, top)
        return jnp.exp2((before - top) * EXPONENT)

    def multiply(unit, less):
        h, i = unit
        total = own[head_rows(h), blocks[i]]
        if far_there:
            total += dot(v_t[h // group][:, i * TILE :], weights_far[h, i * TILE :, blocks[i]], 1, 0)
        rest[head_rows(h), blocks[i]] = total * less

    in_steps(units_of(group, tok, kv_heads), [score, weigh, multiply])


def write_steps(group, kv_heads, tok, total_of, out, stage, sems):
    copies = []
    for h, i in units_of(group, tok, kv_heads):
        b = slice(i * TILE, (i + 1) * TILE)
        total = total_of(h, b)
        normal = total[:HEAD_WIDTH] * (1.0 / total[HEAD_WIDTH : HEAD_WIDTH + 1])
        stage[b, head_columns(h)] = normal.astype(jnp.bfloat16).T
        if h % group == group - 1:
            width = group * HEAD_WIDTH
            part = (pl.ds(i * TILE, TILE), pl.ds((h + 1) * HEAD_WIDTH - width, width))
            copies.append(
                pltpu.make_async_copy(stage.at[part], out.at[part], sems.at[len(copies)])
            )
            copies[-1].start()
    for copy in copies:
        copy.wait()


def finish_kernel(group, rest, weights, v, _, out, stage, sems, part):
    tok = weights.shape[1]
    kv_heads = range(part * PAIR, (part + 1) * PAIR)

    @pl.when(lax.axis_index("seq") >= 1)
    def _():
        v_t = [values_and_ones(v, head_columns(g % PAIR)) for g in kv_heads]
        units = units_of(group, tok, kv_heads)
        held = []

        def total_of(h, b):
            at = units.index((h, b.start // TILE))
            for m, i in units[len(held) : at + 2]:
                c = slice(i * TILE, (i + 1) * TILE)
                held.append(dot(v_t[m // group - part * PAIR], weights[m, :, c], 1, 0))
            return rest[head_rows(h), b] + held[at]

        write_steps(group, kv_heads, tok, total_of, out, stage, sems)


def by_heads(
    kernel, name, query_shape, columns, arrays, out_kinds, into=None
):
    tok, width = query_shape
    heads = width // HEAD_WIDTH
    shapes = dict(
        rest=((heads * (HEAD_WIDTH + ONES), tok), jnp.float32),
        weights=((heads, tok, tok), jnp.bfloat16),
        stat=((heads, tok), jnp.float32),
        output=((tok, width), jnp.bfloat16),
    )
    in_vmem, anywhere = pl.BlockSpec(memory_space=pltpu.VMEM), pl.BlockSpec(memory_space=pl.ANY)
    in_specs = [in_vmem] * len(arrays)
    aliases, scratch = {}, []
    if into is not None:
        aliases = {len(arrays): out_kinds.index("output")}
        arrays.append(into)
        in_specs.append(anywhere)
    if "output" in out_kinds:
        copies = columns // HEAD_WIDTH * (tok // TILE)
        scratch = [
            pltpu.VMEM((tok, width), jnp.bfloat16),
            pltpu.SemaphoreType.DMA((copies,)),
        ]
    return pl.pallas_call(
        functools.partial(kernel, width // columns),
        in_specs=in_specs,
        out_specs=[anywhere if kind == "output" else in_vmem for kind in out_kinds],
        scratch_shapes=scratch,
        out_shape=[jax.ShapeDtypeStruct(*shapes[kind]) for kind in out_kinds],
        input_output_aliases=aliases,
        cost_estimate=pl.CostEstimate(
            flops=16 * heads * tok * tok * HEAD_WIDTH, transcendentals=0, bytes_accessed=1 << 20
        ),
        compiler_params=pltpu.CompilerParams(vmem_limit_bytes=24 * 1024 * 1024),
        name=name,
    )(*arrays)


def shifted(array, steps):
    count = lax.axis_size("seq")
    return lax.ppermute(array, "seq", [(source, source + steps) for source in range(count - steps)])


def exchanged(array, axis, bit):
    count = lax.axis_size(axis)
    return lax.ppermute(array, axis, [(source, source ^ bit) for source in range(count)])


def on_device(
    normed_input, query, key, value, adapter_down_maps, adapter_up_maps, block_adapter_choice
):
    tok = query.shape[0]
    assert 2 * tok == WINDOW and SEG_LEN % tok == 0
    where = lax.axis_index("seq")
    choice = block_adapter_choice

    even = where % 2 == 0
    barrier = lax.optimization_barrier
    call = functools.partial(by_heads, query_shape=query.shape, columns=key.shape[1])

    def from_one_back(own, far):
        return exchanged(jnp.where(even, own, far), "seq", 1)

    key_1 = first_half(key)
    key_far_1 = shifted(key_1, 2)
    latent, up, key_2 = latent_share(
        choice, normed_input.T, adapter_down_maps, adapter_up_maps, key
    )
    key_far_2 = shifted(key_2, 2)
    bit = lax.axis_size("tp") // 2
    while bit > 1:
        latent = latent + exchanged(latent, "tp", bit)
        bit //= 2
    key_1, latent = barrier((key_1, latent))
    theirs = exchanged(latent, "tp", bit)
    key_mid_1 = from_one_back(key_1, key_far_1)
    values = adapt(latent, theirs, up, value)
    value_far = [shifted(values[0], 2)]
    key_2, values = barrier((key_2, values))
    payload, values = barrier((jnp.where(even, key_2, key_far_2), values))
    key_mid_2 = exchanged(payload, "seq", 1)
    value_far.append(shifted(values[1], 2))
    values, key_mid_1 = barrier((values, key_mid_1))
    own, weights_far, tops = call(
        near_far_kernel,
        "near_far",
        arrays=[query, key_1, key_2, *values, key_far_1, key_far_2],
        out_kinds=["rest", "weights", "stat"],
    )
    values, own = barrier((values, own))
    value_mid = [from_one_back(mine, theirs) for mine, theirs in zip(values, value_far)]
    rest, weights_mid, done = call(
        middle_kernel,
        "middle",
        arrays=[query, own, weights_far, tops, key_mid_1, key_mid_2, *value_far],
        out_kinds=["rest", "weights", "output"],
    )
    for n, part in enumerate(value_mid):
        [done] = call(
            functools.partial(finish_kernel, part=n),
            "finish",
            arrays=[rest, weights_mid, part],
            out_kinds=["output"],
            into=done,
        )
    return done


def solution(mesh):
    placed = (
        P("seq", "tp"),
        P("seq", "tp"),
        P("seq", "tp"),
        P("seq", "tp"),
        P(None, None, "tp"),
        P(None, None, "tp"),
        P(),
    )
    return jax.shard_map(
        on_device, mesh=mesh, in_specs=placed, out_specs=P("seq", "tp"), check_vma=False
    )
```

```python
import functools

import jax
import jax.numpy as jnp
from jax import lax
from jax.experimental import pallas as pl
from jax.experimental.pallas import tpu as pltpu
from jax.sharding import PartitionSpec as P

HEAD_WIDTH = 128
WINDOW = 1024
SEG_LEN = 2048
SCALE = 168.0 ** (-0.5)
LOG2_E = 1.4426950408889634
EXPONENT = SCALE * LOG2_E
MASKED = -1e30
TILE = 256
HALF = 128
ONES = 16
PAIR = 2
PIECE = 256


def params(steps, mib):
    return pltpu.CompilerParams(
        vmem_limit_bytes=mib * 1024 * 1024, dimension_semantics=("arbitrary",) * steps
    )


def dot(left, right, left_dim, right_dim):
    return lax.dot_general(
        left, right, (((left_dim,), (right_dim,)), ((), ())), preferred_element_type=jnp.float32
    )


def in_hbm(array):
    return pltpu.with_memory_space_constraint(array, pltpu.HBM)


def adapter_of(choice, tok):
    return choice[lax.div(lax.axis_index("seq") * tok, SEG_LEN)]


def first_half_kernel(key, out, sem):
    copy = pltpu.make_async_copy(key.at[pl.ds(0, out.shape[0])], out, sem)
    copy.start()
    copy.wait()


def first_half(key):
    rows, columns = key.shape
    return pl.pallas_call(
        first_half_kernel,
        in_specs=[pl.BlockSpec(memory_space=pltpu.HBM)],
        out_specs=pl.BlockSpec(memory_space=pltpu.VMEM),
        out_shape=jax.ShapeDtypeStruct((rows // 2, columns), key.dtype),
        scratch_shapes=[pltpu.SemaphoreType.DMA],
        compiler_params=pltpu.CompilerParams(vmem_limit_bytes=8 * 1024 * 1024),
        name="first_half",
    )(in_hbm(key))


def latent_kernel(
    pieces, choice, input_t, down, up, key, out, up_out, key_out, ids, rows, map_rows, sems
):
    half = key_out.shape[0]
    ids_copy = pltpu.make_async_copy(choice, ids, sems.at[0])
    ids_copy.start()
    copies = []
    for n, (first, last) in enumerate(pieces):
        part = pl.ds(first, last - first)
        copies.append(pltpu.make_async_copy(input_t.at[part], rows.at[part], sems.at[n + 4]))
        copies[-1].start()
    key_copy = pltpu.make_async_copy(key.at[pl.ds(half, half)], key_out, sems.at[1])
    key_copy.start()
    ids_copy.wait()
    chosen = adapter_of(ids, out.shape[1])
    down_copy = pltpu.make_async_copy(down.at[chosen], map_rows, sems.at[2])
    up_copy = pltpu.make_async_copy(up.at[chosen], up_out, sems.at[3])
    down_copy.start()
    up_copy.start()
    down_copy.wait()
    total = None
    for (first, last), copy in zip(pieces, copies):
        copy.wait()
        product = dot(map_rows[:, first:last], rows[first:last, :], 1, 0)
        total = product if total is None else total + product
    out[...] = total
    up_copy.wait()
    key_copy.wait()


def latent_share(choice, input_t, down_maps, up_maps, key):
    features, tok = input_t.shape
    rank, columns = up_maps.shape[1:]
    pieces = [(first, min(first + PIECE, features)) for first in range(0, features, PIECE)]
    return pl.pallas_call(
        functools.partial(latent_kernel, pieces),
        in_specs=[pl.BlockSpec(memory_space=pltpu.HBM)] * 5,
        out_specs=[pl.BlockSpec(memory_space=pltpu.VMEM)] * 3,
        out_shape=[
            jax.ShapeDtypeStruct((rank, tok), jnp.float32),
            jax.ShapeDtypeStruct((rank, columns), up_maps.dtype),
            jax.ShapeDtypeStruct((tok // 2, columns), key.dtype),
        ],
        scratch_shapes=[
            pltpu.SMEM(choice.shape, choice.dtype),
            pltpu.VMEM((features, tok), input_t.dtype),
            pltpu.VMEM((rank, features), down_maps.dtype),
            pltpu.SemaphoreType.DMA((len(pieces) + 4,)),
        ],
        compiler_params=pltpu.CompilerParams(vmem_limit_bytes=8 * 1024 * 1024),
        name="latent_share",
    )(*(in_hbm(array) for array in (choice, input_t, down_maps, up_maps, key)))


def adapt_kernel(mine, theirs, up, value, *outs):
    latent = (mine[...] + theirs[...]).astype(jnp.bfloat16)
    update = dot(latent, up[...], 0, 0)
    total = (value[...].astype(jnp.float32) + update).astype(jnp.bfloat16)
    for n, out in enumerate(outs):
        width = out.shape[1]
        out[...] = total[:, n * width : (n + 1) * width]


def adapt(mine, theirs, up, value):
    tok, columns = value.shape
    width = PAIR * HEAD_WIDTH
    return pl.pallas_call(
        adapt_kernel,
        out_shape=[jax.ShapeDtypeStruct((tok, width), jnp.bfloat16)] * (columns // width),
        compiler_params=pltpu.CompilerParams(vmem_limit_bytes=8 * 1024 * 1024),
        name="adapt_values",
    )(mine, theirs, up, value)


def weights_of(scores, top):
    return jnp.exp2(((scores - top) * EXPONENT).astype(jnp.bfloat16))


def tree(operation, items):
    items = list(items)
    while len(items) > 1:
        items = [
            operation(items[n], items[n + 1]) if n + 1 < len(items) else items[n]
            for n in range(0, len(items), 2)
        ]
    return items[0]


def top_of(scores):
    pieces = [s[n : n + 32] for s in scores for n in range(0, s.shape[0], 32)]
    pieces = tree(jnp.maximum, pieces)
    pieces = tree(jnp.maximum, [pieces[n : n + 8] for n in range(0, 32, 8)])
    return jnp.max(pieces, axis=0, keepdims=True)


def values_and_ones(v, columns):
    turned = v[:, columns].T
    return jnp.concatenate([turned, jnp.ones((ONES, v.shape[0]), jnp.bfloat16)], axis=0)


def tile(halves, j, columns):
    rows = halves[0].shape[0]
    first = j * TILE % rows
    return halves[j * TILE // rows][first : first + TILE, columns]


def head_rows(h):
    return slice(h * (HEAD_WIDTH + ONES), (h + 1) * (HEAD_WIDTH + ONES))


def head_columns(h):
    return slice(h * HEAD_WIDTH, (h + 1) * HEAD_WIDTH)


def in_steps(units, stages):
    held = [None] * len(units)
    for step in range(len(units) + len(stages) - 1):
        for n, stage in enumerate(stages):
            if 0 <= step - n < len(units):
                held[step - n] = stage(units[step - n], held[step - n])


def units_of(group, tok, kv_heads):
    return [
        (h, i)
        for g in kv_heads
        for i in range(tok // TILE)
        for h in range(g * group, (g + 1) * group)
    ]


def near_far_kernel(group, *refs):
    place = lax.axis_index("seq")

    @pl.when(place >= 2)
    def _():
        near_far_steps(group, True, *refs)

    @pl.when(place < 2)
    def _():
        near_far_steps(group, False, *refs)


def near_far_steps(
    group, far_there, q, k_1, k_2, v_a, v_b, k_far_1, k_far_2, out, weights_far, tops
):
    k, v, k_far = (k_1, k_2), (v_a, v_b), (k_far_1, k_far_2)
    tok = q.shape[0]
    kv_heads = range(k_1.shape[1] // HEAD_WIDTH)
    causal = lax.broadcasted_iota(jnp.int32, (HALF, HALF), 0) <= lax.broadcasted_iota(
        jnp.int32, (HALF, HALF), 1
    )
    v_t = [values_and_ones(v[g // PAIR], head_columns(g % PAIR)) for g in kv_heads]
    nothing = jnp.zeros((HALF, HALF), jnp.bfloat16)
    tiles = tok // TILE
    blocks = [slice(i * TILE, (i + 1) * TILE) for i in range(tiles)]

    def score(unit, _):
        h, i = unit
        qh = q[blocks[i], head_columns(h)]
        columns = head_columns(h // group)
        near = [dot(tile(k, j, columns), qh, 1, 1) for j in range(i + 1)]
        far = []
        if far_there:
            far = [dot(tile(k_far, j, columns), qh, 1, 1) for j in range(i, tiles)]
        return near, far

    def weigh(unit, scores):
        h, i = unit
        near, far = scores
        near_columns, far_columns = [], []
        for half in range(2):
            a = slice(half * HALF, (half + 1) * HALF)
            near_edge = near[i][: (half + 1) * HALF, a]
            near_pieces = [s[:, a] for s in near[:i]]
            if half == 1:
                near_pieces.append(near_edge[:HALF])
            near_pieces.append(jnp.where(causal, near_edge[half * HALF :], MASKED))
            far_pieces = []
            if far_there:
                far_edge = far[0][half * HALF :, a]
                far_pieces.append(jnp.where(causal, MASKED, far_edge[:HALF]))
                if half == 0:
                    far_pieces.append(far_edge[HALF:])
                far_pieces += [s[:, a] for s in far[1:]]
            top = top_of(near_pieces + far_pieces)
            near_weights = [weights_of(s, top) for s in near_pieces]
            if half == 0:
                near_weights.append(nothing)
            near_columns.append(jnp.concatenate(near_weights, axis=0))
            if far_there:
                far_weights = [weights_of(s, top) for s in far_pieces]
                if half == 1:
                    far_weights.insert(0, nothing)
                far_columns.append(jnp.concatenate(far_weights, axis=0))
            queries = slice(i * TILE + half * HALF, i * TILE + (half + 1) * HALF)
            tops[h : h + 1, queries] = top
        if far_there:
            weights_far[h, i * TILE :, blocks[i]] = jnp.concatenate(far_columns, axis=1)
        return jnp.concatenate(near_columns, axis=1)

    def multiply(unit, weights):
        h, i = unit
        out[head_rows(h), blocks[i]] = dot(v_t[h // group][:, : (i + 1) * TILE], weights, 1, 0)

    in_steps(units_of(group, tok, kv_heads), [score, weigh, multiply])


def middle_kernel(group, *refs):
    place = lax.axis_index("seq")

    @pl.when(place >= 2)
    def _():
        middle_steps(group, True, *refs)

    @pl.when(place == 1)
    def _():
        middle_steps(group, False, *refs)

    @pl.when(place == 0)
    def _():
        q, own, k, out, stage, sems = refs[0], refs[1], refs[4], refs[10], refs[11], refs[12]
        kv_heads = range(k.shape[1] // HEAD_WIDTH)
        write_steps(
            group, kv_heads, q.shape[0], lambda h, b: own[head_rows(h), b], out, stage, sems
        )


def middle_steps(
    group, far_there, q, own, weights_far, tops, k_1, k_2, v_a, v_b, rest, weights, *_
):
    k, v_far = (k_1, k_2), (v_a, v_b)
    tok = q.shape[0]
    kv_heads = range(k_1.shape[1] // HEAD_WIDTH)
    v_t = []
    if far_there:
        v_t = [values_and_ones(v_far[g // PAIR], head_columns(g % PAIR)) for g in kv_heads]
    tiles = tok // TILE
    blocks = [slice(i * TILE, (i + 1) * TILE) for i in range(tiles)]

    def score(unit, _):
        h, i = unit
        qh = q[blocks[i], head_columns(h)]
        return [dot(tile(k, j, head_columns(h // group)), qh, 1, 1) for j in range(tiles)]

    def weigh(unit, scores):
        h, i = unit
        before = tops[h : h + 1, blocks[i]]
        top = jnp.maximum(before, top_of(scores))
        for j, s in enumerate(scores):
            weights[h, blocks[j], blocks[i]] = weights_of(s, top)
        return jnp.exp2((before - top) * EXPONENT)

    def multiply(unit, less):
        h, i = unit
        total = own[head_rows(h), blocks[i]]
        if far_there:
            total += dot(v_t[h // group][:, i * TILE :], weights_far[h, i * TILE :, blocks[i]], 1, 0)
        rest[head_rows(h), blocks[i]] = total * less

    in_steps(units_of(group, tok, kv_heads), [score, weigh, multiply])


def write_steps(group, kv_heads, tok, total_of, out, stage, sems):
    copies = []
    for h, i in units_of(group, tok, kv_heads):
        b = slice(i * TILE, (i + 1) * TILE)
        total = total_of(h, b)
        normal = total[:HEAD_WIDTH] * (1.0 / total[HEAD_WIDTH : HEAD_WIDTH + 1])
        stage[b, head_columns(h)] = normal.astype(jnp.bfloat16).T
        if h % group == group - 1:
            width = group * HEAD_WIDTH
            part = (pl.ds(i * TILE, TILE), pl.ds((h + 1) * HEAD_WIDTH - width, width))
            copies.append(
                pltpu.make_async_copy(stage.at[part], out.at[part], sems.at[len(copies)])
            )
            copies[-1].start()
    for copy in copies:
        copy.wait()


def finish_kernel(group, rest, weights, v, _, out, stage, sems, part):
    tok = weights.shape[1]
    kv_heads = range(part * PAIR, (part + 1) * PAIR)

    @pl.when(lax.axis_index("seq") >= 1)
    def _():
        v_t = [values_and_ones(v, head_columns(g % PAIR)) for g in kv_heads]
        units = units_of(group, tok, kv_heads)
        held = []

        def total_of(h, b):
            at = units.index((h, b.start // TILE))
            for m, i in units[len(held) : at + 2]:
                c = slice(i * TILE, (i + 1) * TILE)
                held.append(dot(v_t[m // group - part * PAIR], weights[m, :, c], 1, 0))
            return rest[head_rows(h), b] + held[at]

        write_steps(group, kv_heads, tok, total_of, out, stage, sems)


def by_heads(
    kernel, name, query_shape, columns, arrays, out_kinds, into=None
):
    tok, width = query_shape
    heads = width // HEAD_WIDTH
    shapes = dict(
        rest=((heads * (HEAD_WIDTH + ONES), tok), jnp.float32),
        weights=((heads, tok, tok), jnp.bfloat16),
        stat=((heads, tok), jnp.float32),
        output=((tok, width), jnp.bfloat16),
    )
    in_vmem, anywhere = pl.BlockSpec(memory_space=pltpu.VMEM), pl.BlockSpec(memory_space=pl.ANY)
    in_specs = [in_vmem] * len(arrays)
    aliases, scratch = {}, []
    if into is not None:
        aliases = {len(arrays): out_kinds.index("output")}
        arrays.append(into)
        in_specs.append(anywhere)
    if "output" in out_kinds:
        copies = columns // HEAD_WIDTH * (tok // TILE)
        scratch = [
            pltpu.VMEM((tok, width), jnp.bfloat16),
            pltpu.SemaphoreType.DMA((copies,)),
        ]
    return pl.pallas_call(
        functools.partial(kernel, width // columns),
        in_specs=in_specs,
        out_specs=[anywhere if kind == "output" else in_vmem for kind in out_kinds],
        scratch_shapes=scratch,
        out_shape=[jax.ShapeDtypeStruct(*shapes[kind]) for kind in out_kinds],
        input_output_aliases=aliases,
        cost_estimate=pl.CostEstimate(
            flops=16 * heads * tok * tok * HEAD_WIDTH, transcendentals=0, bytes_accessed=1 << 20
        ),
        compiler_params=pltpu.CompilerParams(vmem_limit_bytes=24 * 1024 * 1024),
        name=name,
    )(*arrays)


def shifted(array, steps):
    count = lax.axis_size("seq")
    return lax.ppermute(array, "seq", [(source, source + steps) for source in range(count - steps)])


def exchanged(array, axis, bit):
    count = lax.axis_size(axis)
    return lax.ppermute(array, axis, [(source, source ^ bit) for source in range(count)])


def on_device(
    normed_input, query, key, value, adapter_down_maps, adapter_up_maps, block_adapter_choice
):
    tok = query.shape[0]
    assert 2 * tok == WINDOW and SEG_LEN % tok == 0
    where = lax.axis_index("seq")
    choice = block_adapter_choice

    even = where % 2 == 0
    barrier = lax.optimization_barrier
    call = functools.partial(by_heads, query_shape=query.shape, columns=key.shape[1])

    def from_one_back(own, far):
        return exchanged(jnp.where(even, own, far), "seq", 1)

    key_1 = first_half(key)
    key_far_1 = shifted(key_1, 2)
    latent, up, key_2 = latent_share(
        choice, normed_input.T, adapter_down_maps, adapter_up_maps, key
    )
    key_far_2 = shifted(key_2, 2)
    bit = 1
    while 2 * bit < lax.axis_size("tp"):
        latent = latent + exchanged(latent, "tp", bit)
        bit *= 2
    key_1, latent = barrier((key_1, latent))
    theirs = exchanged(latent, "tp", bit)
    key_mid_1 = from_one_back(key_1, key_far_1)
    values = adapt(latent, theirs, up, value)
    value_far = [shifted(values[0], 2)]
    key_2, values = barrier((key_2, values))
    payload, values = barrier((jnp.where(even, key_2, key_far_2), values))
    key_mid_2 = exchanged(payload, "seq", 1)
    value_far.append(shifted(values[1], 2))
    values, key_mid_1 = barrier((values, key_mid_1))
    own, weights_far, tops = call(
        near_far_kernel,
        "near_far",
        arrays=[query, key_1, key_2, *values, key_far_1, key_far_2],
        out_kinds=["rest", "weights", "stat"],
    )
    values, own = barrier((values, own))
    value_mid = [from_one_back(mine, theirs) for mine, theirs in zip(values, value_far)]
    rest, weights_mid, done = call(
        middle_kernel,
        "middle",
        arrays=[query, own, weights_far, tops, key_mid_1, key_mid_2, *value_far],
        out_kinds=["rest", "weights", "output"],
    )
    for n, part in enumerate(value_mid):
        [done] = call(
            functools.partial(finish_kernel, part=n),
            "finish",
            arrays=[rest, weights_mid, part],
            out_kinds=["output"],
            into=done,
        )
    return done


def solution(mesh):
    placed = (
        P("seq", "tp"),
        P("seq", "tp"),
        P("seq", "tp"),
        P("seq", "tp"),
        P(None, None, "tp"),
        P(None, None, "tp"),
        P(),
    )
    return jax.shard_map(
        on_device, mesh=mesh, in_specs=placed, out_specs=P("seq", "tp"), check_vma=False
    )
```

```python
import functools

import jax
import jax.numpy as jnp
from jax import lax
from jax.experimental import pallas as pl
from jax.experimental.pallas import tpu as pltpu
from jax.sharding import PartitionSpec as P

HEAD_WIDTH = 128
WINDOW = 1024
SEG_LEN = 2048
SCALE = 168.0 ** (-0.5)
LOG2_E = 1.4426950408889634
EXPONENT = SCALE * LOG2_E
MASKED = -1e30
TILE = 256
HALF = 128
ONES = 16
PAIR = 2
PIECE = 256


def params(steps, mib):
    return pltpu.CompilerParams(
        vmem_limit_bytes=mib * 1024 * 1024, dimension_semantics=("arbitrary",) * steps
    )


def dot(left, right, left_dim, right_dim):
    return lax.dot_general(
        left, right, (((left_dim,), (right_dim,)), ((), ())), preferred_element_type=jnp.float32
    )


def in_hbm(array):
    return pltpu.with_memory_space_constraint(array, pltpu.HBM)


def adapter_of(choice, tok):
    return choice[lax.div(lax.axis_index("seq") * tok, SEG_LEN)]


def first_half_kernel(key, out, sem):
    copy = pltpu.make_async_copy(key.at[pl.ds(0, out.shape[0])], out, sem)
    copy.start()
    copy.wait()


def first_half(key):
    rows, columns = key.shape
    return pl.pallas_call(
        first_half_kernel,
        in_specs=[pl.BlockSpec(memory_space=pltpu.HBM)],
        out_specs=pl.BlockSpec(memory_space=pltpu.VMEM),
        out_shape=jax.ShapeDtypeStruct((rows // 2, columns), key.dtype),
        scratch_shapes=[pltpu.SemaphoreType.DMA],
        compiler_params=pltpu.CompilerParams(vmem_limit_bytes=8 * 1024 * 1024),
        name="first_half",
    )(in_hbm(key))


def latent_kernel(
    pieces, choice, input_t, down, up, key, out, up_out, key_out, ids, rows, map_rows, sems
):
    half = key_out.shape[0]
    ids_copy = pltpu.make_async_copy(choice, ids, sems.at[0])
    ids_copy.start()
    copies = []
    for n, (first, last) in enumerate(pieces):
        part = pl.ds(first, last - first)
        copies.append(pltpu.make_async_copy(input_t.at[part], rows.at[part], sems.at[n + 4]))
        copies[-1].start()
    key_copy = pltpu.make_async_copy(key.at[pl.ds(half, half)], key_out, sems.at[1])
    key_copy.start()
    ids_copy.wait()
    chosen = adapter_of(ids, out.shape[1])
    down_copy = pltpu.make_async_copy(down.at[chosen], map_rows, sems.at[2])
    up_copy = pltpu.make_async_copy(up.at[chosen], up_out, sems.at[3])
    down_copy.start()
    up_copy.start()
    down_copy.wait()
    total = None
    for (first, last), copy in zip(pieces, copies):
        copy.wait()
        product = dot(map_rows[:, first:last], rows[first:last, :], 1, 0)
        total = product if total is None else total + product
    out[...] = total
    up_copy.wait()
    key_copy.wait()


def latent_share(choice, input_t, down_maps, up_maps, key):
    features, tok = input_t.shape
    rank, columns = up_maps.shape[1:]
    pieces = [(first, min(first + PIECE, features)) for first in range(0, features, PIECE)]
    return pl.pallas_call(
        functools.partial(latent_kernel, pieces),
        in_specs=[pl.BlockSpec(memory_space=pltpu.HBM)] * 5,
        out_specs=[pl.BlockSpec(memory_space=pltpu.VMEM)] * 3,
        out_shape=[
            jax.ShapeDtypeStruct((rank, tok), jnp.float32),
            jax.ShapeDtypeStruct((rank, columns), up_maps.dtype),
            jax.ShapeDtypeStruct((tok // 2, columns), key.dtype),
        ],
        scratch_shapes=[
            pltpu.SMEM(choice.shape, choice.dtype),
            pltpu.VMEM((features, tok), input_t.dtype),
            pltpu.VMEM((rank, features), down_maps.dtype),
            pltpu.SemaphoreType.DMA((len(pieces) + 4,)),
        ],
        compiler_params=pltpu.CompilerParams(vmem_limit_bytes=8 * 1024 * 1024),
        name="latent_share",
    )(*(in_hbm(array) for array in (choice, input_t, down_maps, up_maps, key)))


def adapt_kernel(mine, theirs, up, value, *outs):
    latent = (mine[...] + theirs[...]).astype(jnp.bfloat16)
    update = dot(latent, up[...], 0, 0)
    total = (value[...].astype(jnp.float32) + update).astype(jnp.bfloat16)
    for n, out in enumerate(outs):
        width = out.shape[1]
        out[...] = total[:, n * width : (n + 1) * width]


def adapt(mine, theirs, up, value):
    tok, columns = value.shape
    width = PAIR * HEAD_WIDTH
    return pl.pallas_call(
        adapt_kernel,
        out_shape=[jax.ShapeDtypeStruct((tok, width), jnp.bfloat16)] * (columns // width),
        compiler_params=pltpu.CompilerParams(vmem_limit_bytes=8 * 1024 * 1024),
        name="adapt_values",
    )(mine, theirs, up, value)


def weights_of(scores, top):
    return jnp.exp2(((scores - top) * EXPONENT).astype(jnp.bfloat16))


def tree(operation, items):
    items = list(items)
    while len(items) > 1:
        items = [
            operation(items[n], items[n + 1]) if n + 1 < len(items) else items[n]
            for n in range(0, len(items), 2)
        ]
    return items[0]


def top_of(scores):
    pieces = [s[n : n + 32] for s in scores for n in range(0, s.shape[0], 32)]
    pieces = tree(jnp.maximum, pieces)
    pieces = tree(jnp.maximum, [pieces[n : n + 8] for n in range(0, 32, 8)])
    return jnp.max(pieces, axis=0, keepdims=True)


def values_and_ones(v, columns):
    turned = v[:, columns].T
    return jnp.concatenate([turned, jnp.ones((ONES, v.shape[0]), jnp.bfloat16)], axis=0)


def tile(halves, j, columns):
    rows = halves[0].shape[0]
    first = j * TILE % rows
    return halves[j * TILE // rows][first : first + TILE, columns]


def head_rows(h):
    return slice(h * (HEAD_WIDTH + ONES), (h + 1) * (HEAD_WIDTH + ONES))


def head_columns(h):
    return slice(h * HEAD_WIDTH, (h + 1) * HEAD_WIDTH)


def in_steps(units, stages):
    held = [None] * len(units)
    for step in range(len(units) + len(stages) - 1):
        for n, stage in enumerate(stages):
            if 0 <= step - n < len(units):
                held[step - n] = stage(units[step - n], held[step - n])


def units_of(group, tok, kv_heads):
    return [
        (h, i)
        for g in kv_heads
        for i in range(tok // TILE)
        for h in range(g * group, (g + 1) * group)
    ]


def near_far_kernel(group, *refs):
    place = lax.axis_index("seq")

    @pl.when(place >= 2)
    def _():
        near_far_steps(group, True, *refs)

    @pl.when(place < 2)
    def _():
        near_far_steps(group, False, *refs)


def near_far_steps(
    group, far_there, q, k_1, k_2, v_a, v_b, k_far_1, k_far_2, out, weights_far, tops
):
    k, v, k_far = (k_1, k_2), (v_a, v_b), (k_far_1, k_far_2)
    tok = q.shape[0]
    kv_heads = range(k_1.shape[1] // HEAD_WIDTH)
    causal = lax.broadcasted_iota(jnp.int32, (HALF, HALF), 0) <= lax.broadcasted_iota(
        jnp.int32, (HALF, HALF), 1
    )
    v_t = [values_and_ones(v[g // PAIR], head_columns(g % PAIR)) for g in kv_heads]
    nothing = jnp.zeros((HALF, HALF), jnp.bfloat16)
    tiles = tok // TILE
    blocks = [slice(i * TILE, (i + 1) * TILE) for i in range(tiles)]

    def score(unit, _):
        h, i = unit
        qh = q[blocks[i], head_columns(h)]
        columns = head_columns(h // group)
        near = [dot(tile(k, j, columns), qh, 1, 1) for j in range(i + 1)]
        far = []
        if far_there:
            far = [dot(tile(k_far, j, columns), qh, 1, 1) for j in range(i, tiles)]
        return near, far

    def weigh(unit, scores):
        h, i = unit
        near, far = scores
        near_columns, far_columns = [], []
        for half in range(2):
            a = slice(half * HALF, (half + 1) * HALF)
            near_edge = near[i][: (half + 1) * HALF, a]
            near_pieces = [s[:, a] for s in near[:i]]
            if half == 1:
                near_pieces.append(near_edge[:HALF])
            near_pieces.append(jnp.where(causal, near_edge[half * HALF :], MASKED))
            far_pieces = []
            if far_there:
                far_edge = far[0][half * HALF :, a]
                far_pieces.append(jnp.where(causal, MASKED, far_edge[:HALF]))
                if half == 0:
                    far_pieces.append(far_edge[HALF:])
                far_pieces += [s[:, a] for s in far[1:]]
            top = top_of(near_pieces + far_pieces)
            near_weights = [weights_of(s, top) for s in near_pieces]
            if half == 0:
                near_weights.append(nothing)
            near_columns.append(jnp.concatenate(near_weights, axis=0))
            if far_there:
                far_weights = [weights_of(s, top) for s in far_pieces]
                if half == 1:
                    far_weights.insert(0, nothing)
                far_columns.append(jnp.concatenate(far_weights, axis=0))
            queries = slice(i * TILE + half * HALF, i * TILE + (half + 1) * HALF)
            tops[h : h + 1, queries] = top
        if far_there:
            weights_far[h, i * TILE :, blocks[i]] = jnp.concatenate(far_columns, axis=1)
        return jnp.concatenate(near_columns, axis=1)

    def multiply(unit, weights):
        h, i = unit
        out[head_rows(h), blocks[i]] = dot(v_t[h // group][:, : (i + 1) * TILE], weights, 1, 0)

    in_steps(units_of(group, tok, kv_heads), [score, weigh, multiply])


def middle_kernel(group, *refs):
    place = lax.axis_index("seq")

    @pl.when(place >= 2)
    def _():
        middle_steps(group, True, *refs)

    @pl.when(place == 1)
    def _():
        middle_steps(group, False, *refs)

    @pl.when(place == 0)
    def _():
        q, own, k, out, stage, sems = refs[0], refs[1], refs[4], refs[10], refs[11], refs[12]
        kv_heads = range(k.shape[1] // HEAD_WIDTH)
        write_steps(
            group, kv_heads, q.shape[0], lambda h, b: own[head_rows(h), b], out, stage, sems
        )


def middle_steps(
    group, far_there, q, own, weights_far, tops, k_1, k_2, v_a, v_b, rest, weights, *_
):
    k, v_far = (k_1, k_2), (v_a, v_b)
    tok = q.shape[0]
    kv_heads = range(k_1.shape[1] // HEAD_WIDTH)
    v_t = []
    if far_there:
        v_t = [values_and_ones(v_far[g // PAIR], head_columns(g % PAIR)) for g in kv_heads]
    tiles = tok // TILE
    blocks = [slice(i * TILE, (i + 1) * TILE) for i in range(tiles)]

    def score(unit, _):
        h, i = unit
        qh = q[blocks[i], head_columns(h)]
        return [dot(tile(k, j, head_columns(h // group)), qh, 1, 1) for j in range(tiles)]

    def weigh(unit, scores):
        h, i = unit
        before = tops[h : h + 1, blocks[i]]
        top = jnp.maximum(before, top_of(scores))
        for j, s in enumerate(scores):
            weights[h, blocks[j], blocks[i]] = weights_of(s, top)
        return jnp.exp2((before - top) * EXPONENT)

    def multiply(unit, less):
        h, i = unit
        total = own[head_rows(h), blocks[i]]
        if far_there:
            total += dot(v_t[h // group][:, i * TILE :], weights_far[h, i * TILE :, blocks[i]], 1, 0)
        rest[head_rows(h), blocks[i]] = total * less

    in_steps(units_of(group, tok, kv_heads), [score, weigh, multiply])


def write_steps(group, kv_heads, tok, total_of, out, stage, sems):
    copies = []
    for h, i in units_of(group, tok, kv_heads):
        b = slice(i * TILE, (i + 1) * TILE)
        total = total_of(h, b)
        normal = total[:HEAD_WIDTH] * (1.0 / total[HEAD_WIDTH : HEAD_WIDTH + 1])
        stage[b, head_columns(h)] = normal.astype(jnp.bfloat16).T
        if h % group == group - 1:
            width = group * HEAD_WIDTH
            part = (pl.ds(i * TILE, TILE), pl.ds((h + 1) * HEAD_WIDTH - width, width))
            copies.append(
                pltpu.make_async_copy(stage.at[part], out.at[part], sems.at[len(copies)])
            )
            copies[-1].start()
    for copy in copies:
        copy.wait()


def finish_kernel(group, rest, weights, v, _, out, stage, sems, part):
    tok = weights.shape[1]
    kv_heads = range(part * PAIR, (part + 1) * PAIR)

    @pl.when(lax.axis_index("seq") >= 1)
    def _():
        v_t = [values_and_ones(v, head_columns(g % PAIR)) for g in kv_heads]
        units = units_of(group, tok, kv_heads)
        held = []

        def total_of(h, b):
            at = units.index((h, b.start // TILE))
            for m, i in units[len(held) : at + 2]:
                c = slice(i * TILE, (i + 1) * TILE)
                held.append(dot(v_t[m // group - part * PAIR], weights[m, :, c], 1, 0))
            return rest[head_rows(h), b] + held[at]

        write_steps(group, kv_heads, tok, total_of, out, stage, sems)


def by_heads(
    kernel, name, query_shape, columns, arrays, out_kinds, into=None
):
    tok, width = query_shape
    heads = width // HEAD_WIDTH
    shapes = dict(
        rest=((heads * (HEAD_WIDTH + ONES), tok), jnp.float32),
        weights=((heads, tok, tok), jnp.bfloat16),
        stat=((heads, tok), jnp.float32),
        output=((tok, width), jnp.bfloat16),
    )
    in_vmem, anywhere = pl.BlockSpec(memory_space=pltpu.VMEM), pl.BlockSpec(memory_space=pl.ANY)
    in_specs = [in_vmem] * len(arrays)
    aliases, scratch = {}, []
    if into is not None:
        aliases = {len(arrays): out_kinds.index("output")}
        arrays.append(into)
        in_specs.append(anywhere)
    if "output" in out_kinds:
        copies = columns // HEAD_WIDTH * (tok // TILE)
        scratch = [
            pltpu.VMEM((tok, width), jnp.bfloat16),
            pltpu.SemaphoreType.DMA((copies,)),
        ]
    return pl.pallas_call(
        functools.partial(kernel, width // columns),
        in_specs=in_specs,
        out_specs=[anywhere if kind == "output" else in_vmem for kind in out_kinds],
        scratch_shapes=scratch,
        out_shape=[jax.ShapeDtypeStruct(*shapes[kind]) for kind in out_kinds],
        input_output_aliases=aliases,
        compiler_params=pltpu.CompilerParams(vmem_limit_bytes=24 * 1024 * 1024),
        name=name,
    )(*arrays)


def shifted(array, steps):
    count = lax.axis_size("seq")
    return lax.ppermute(array, "seq", [(source, source + steps) for source in range(count - steps)])


def exchanged(array, axis, bit):
    count = lax.axis_size(axis)
    return lax.ppermute(array, axis, [(source, source ^ bit) for source in range(count)])


def on_device(
    normed_input, query, key, value, adapter_down_maps, adapter_up_maps, block_adapter_choice
):
    tok = query.shape[0]
    assert 2 * tok == WINDOW and SEG_LEN % tok == 0
    where = lax.axis_index("seq")
    choice = block_adapter_choice

    even = where % 2 == 0
    barrier = lax.optimization_barrier
    call = functools.partial(by_heads, query_shape=query.shape, columns=key.shape[1])

    def from_one_back(own, far):
        return exchanged(jnp.where(even, own, far), "seq", 1)

    key_1 = first_half(key)
    key_far_1 = shifted(key_1, 2)
    latent, up, key_2 = latent_share(
        choice, normed_input.T, adapter_down_maps, adapter_up_maps, key
    )
    key_far_2 = shifted(key_2, 2)
    bit = 1
    while 2 * bit < lax.axis_size("tp"):
        latent = latent + exchanged(latent, "tp", bit)
        bit *= 2
    key_1, latent = barrier((key_1, latent))
    theirs = exchanged(latent, "tp", bit)
    key_mid_1 = from_one_back(key_1, key_far_1)
    values = adapt(latent, theirs, up, value)
    value_far = [shifted(part, 2) for part in values]
    key_2, values = barrier((key_2, values))
    key_mid_2 = from_one_back(key_2, key_far_2)
    values, key_mid_1 = barrier((values, key_mid_1))
    own, weights_far, tops = call(
        near_far_kernel,
        "near_far",
        arrays=[query, key_1, key_2, *values, key_far_1, key_far_2],
        out_kinds=["rest", "weights", "stat"],
    )
    values, own = barrier((values, own))
    value_mid = [from_one_back(mine, theirs) for mine, theirs in zip(values, value_far)]
    rest, weights_mid, done = call(
        middle_kernel,
        "middle",
        arrays=[query, own, weights_far, tops, key_mid_1, key_mid_2, *value_far],
        out_kinds=["rest", "weights", "output"],
    )
    for n, part in enumerate(value_mid):
        [done] = call(
            functools.partial(finish_kernel, part=n),
            "finish",
            arrays=[rest, weights_mid, part],
            out_kinds=["output"],
            into=done,
        )
    return done


def solution(mesh):
    placed = (
        P("seq", "tp"),
        P("seq", "tp"),
        P("seq", "tp"),
        P("seq", "tp"),
        P(None, None, "tp"),
        P(None, None, "tp"),
        P(),
    )
    return jax.shard_map(
        on_device, mesh=mesh, in_specs=placed, out_specs=P("seq", "tp"), check_vma=False
    )
```

```python
import functools

import jax
import jax.numpy as jnp
from jax import lax
from jax.experimental import pallas as pl
from jax.experimental.pallas import tpu as pltpu
from jax.sharding import PartitionSpec as P

HEAD_WIDTH = 128
WINDOW = 1024
SEG_LEN = 2048
SCALE = 168.0 ** (-0.5)
LOG2_E = 1.4426950408889634
EXPONENT = SCALE * LOG2_E
MASKED = -1e30
TILE = 256
HALF = 128
ONES = 16
PAIR = 2
PIECE = 256


def params(steps, mib):
    return pltpu.CompilerParams(
        vmem_limit_bytes=mib * 1024 * 1024, dimension_semantics=("arbitrary",) * steps
    )


def dot(left, right, left_dim, right_dim):
    return lax.dot_general(
        left, right, (((left_dim,), (right_dim,)), ((), ())), preferred_element_type=jnp.float32
    )


def in_hbm(array):
    return pltpu.with_memory_space_constraint(array, pltpu.HBM)


def adapter_of(choice, tok):
    return choice[lax.div(lax.axis_index("seq") * tok, SEG_LEN)]


def first_half_kernel(key, out, sem):
    copy = pltpu.make_async_copy(key.at[pl.ds(0, out.shape[0])], out, sem)
    copy.start()
    copy.wait()


def first_half(key):
    rows, columns = key.shape
    return pl.pallas_call(
        first_half_kernel,
        in_specs=[pl.BlockSpec(memory_space=pltpu.HBM)],
        out_specs=pl.BlockSpec(memory_space=pltpu.VMEM),
        out_shape=jax.ShapeDtypeStruct((rows // 2, columns), key.dtype),
        scratch_shapes=[pltpu.SemaphoreType.DMA],
        compiler_params=pltpu.CompilerParams(vmem_limit_bytes=8 * 1024 * 1024),
        name="first_half",
    )(in_hbm(key))


def latent_kernel(
    pieces, choice, input_t, down, up, key, out, up_out, key_out, ids, rows, map_rows, sems
):
    half = key_out.shape[0]
    ids_copy = pltpu.make_async_copy(choice, ids, sems.at[0])
    ids_copy.start()
    copies = []
    for n, (first, last) in enumerate(pieces):
        part = pl.ds(first, last - first)
        copies.append(pltpu.make_async_copy(input_t.at[part], rows.at[part], sems.at[n + 4]))
        copies[-1].start()
    key_copy = pltpu.make_async_copy(key.at[pl.ds(half, half)], key_out, sems.at[1])
    key_copy.start()
    ids_copy.wait()
    chosen = adapter_of(ids, out.shape[1])
    down_copy = pltpu.make_async_copy(down.at[chosen], map_rows, sems.at[2])
    up_copy = pltpu.make_async_copy(up.at[chosen], up_out, sems.at[3])
    down_copy.start()
    up_copy.start()
    down_copy.wait()
    total = None
    for (first, last), copy in zip(pieces, copies):
        copy.wait()
        product = dot(map_rows[:, first:last], rows[first:last, :], 1, 0)
        total = product if total is None else total + product
    out[...] = total
    up_copy.wait()
    key_copy.wait()


def latent_share(choice, input_t, down_maps, up_maps, key):
    features, tok = input_t.shape
    rank, columns = up_maps.shape[1:]
    pieces = [(first, min(first + PIECE, features)) for first in range(0, features, PIECE)]
    return pl.pallas_call(
        functools.partial(latent_kernel, pieces),
        in_specs=[pl.BlockSpec(memory_space=pltpu.HBM)] * 5,
        out_specs=[pl.BlockSpec(memory_space=pltpu.VMEM)] * 3,
        out_shape=[
            jax.ShapeDtypeStruct((rank, tok), jnp.float32),
            jax.ShapeDtypeStruct((rank, columns), up_maps.dtype),
            jax.ShapeDtypeStruct((tok // 2, columns), key.dtype),
        ],
        scratch_shapes=[
            pltpu.SMEM(choice.shape, choice.dtype),
            pltpu.VMEM((features, tok), input_t.dtype),
            pltpu.VMEM((rank, features), down_maps.dtype),
            pltpu.SemaphoreType.DMA((len(pieces) + 4,)),
        ],
        compiler_params=pltpu.CompilerParams(vmem_limit_bytes=8 * 1024 * 1024),
        name="latent_share",
    )(*(in_hbm(array) for array in (choice, input_t, down_maps, up_maps, key)))


def adapt_kernel(mine, theirs, up, value, *outs):
    latent = (mine[...] + theirs[...]).astype(jnp.bfloat16)
    update = dot(latent, up[...], 0, 0)
    total = (value[...].astype(jnp.float32) + update).astype(jnp.bfloat16)
    for n, out in enumerate(outs):
        width = out.shape[1]
        out[...] = total[:, n * width : (n + 1) * width]


def adapt(mine, theirs, up, value):
    tok, columns = value.shape
    width = PAIR * HEAD_WIDTH
    return pl.pallas_call(
        adapt_kernel,
        out_shape=[jax.ShapeDtypeStruct((tok, width), jnp.bfloat16)] * (columns // width),
        compiler_params=pltpu.CompilerParams(vmem_limit_bytes=8 * 1024 * 1024),
        name="adapt_values",
    )(mine, theirs, up, value)


def weights_of(scores, top):
    return jnp.exp2(((scores - top) * EXPONENT).astype(jnp.bfloat16))


def tree(operation, items):
    items = list(items)
    while len(items) > 1:
        items = [
            operation(items[n], items[n + 1]) if n + 1 < len(items) else items[n]
            for n in range(0, len(items), 2)
        ]
    return items[0]


def top_of(scores):
    pieces = [s[n : n + 32] for s in scores for n in range(0, s.shape[0], 32)]
    pieces = tree(jnp.maximum, pieces)
    pieces = tree(jnp.maximum, [pieces[n : n + 8] for n in range(0, 32, 8)])
    return jnp.max(pieces, axis=0, keepdims=True)


def values_and_ones(v, columns):
    turned = v[:, columns].T
    return jnp.concatenate([turned, jnp.ones((ONES, v.shape[0]), jnp.bfloat16)], axis=0)


def tile(halves, j, columns):
    rows = halves[0].shape[0]
    first = j * TILE % rows
    return halves[j * TILE // rows][first : first + TILE, columns]


def head_rows(h):
    return slice(h * (HEAD_WIDTH + ONES), (h + 1) * (HEAD_WIDTH + ONES))


def head_columns(h):
    return slice(h * HEAD_WIDTH, (h + 1) * HEAD_WIDTH)


def in_steps(units, stages):
    held = [None] * len(units)
    for step in range(len(units) + len(stages) - 1):
        for n, stage in enumerate(stages):
            if 0 <= step - n < len(units):
                held[step - n] = stage(units[step - n], held[step - n])


def units_of(group, tok, kv_heads):
    return [
        (h, i)
        for g in kv_heads
        for i in range(tok // TILE)
        for h in range(g * group, (g + 1) * group)
    ]


def near_far_kernel(group, *refs):
    place = lax.axis_index("seq")

    @pl.when(place >= 2)
    def _():
        near_far_steps(group, True, *refs)

    @pl.when(place < 2)
    def _():
        near_far_steps(group, False, *refs)


def near_far_steps(
    group, far_there, query, k_1, k_2, v_a, v_b, k_far_1, k_far_2, q, out, weights_far, tops, sems
):
    k, v, k_far = (k_1, k_2), (v_a, v_b), (k_far_1, k_far_2)
    copies = []
    for g in range(k_1.shape[1] // HEAD_WIDTH):
        part = (slice(None), pl.ds(g * group * HEAD_WIDTH, group * HEAD_WIDTH))
        copies.append(pltpu.make_async_copy(query.at[part], q.at[part], sems.at[g]))
    copies[0].start()
    copies[0].wait()
    for copy in copies[1:]:
        copy.start()
    tok = q.shape[0]
    kv_heads = range(k_1.shape[1] // HEAD_WIDTH)
    causal = lax.broadcasted_iota(jnp.int32, (HALF, HALF), 0) <= lax.broadcasted_iota(
        jnp.int32, (HALF, HALF), 1
    )
    v_t = [values_and_ones(v[g // PAIR], head_columns(g % PAIR)) for g in kv_heads]
    nothing = jnp.zeros((HALF, HALF), jnp.bfloat16)
    tiles = tok // TILE
    blocks = [slice(i * TILE, (i + 1) * TILE) for i in range(tiles)]

    def score(unit, _):
        h, i = unit
        if h % group == 0 and i == 0 and h > 0:
            copies[h // group].wait()
        qh = q[blocks[i], head_columns(h)]
        columns = head_columns(h // group)
        near = [dot(tile(k, j, columns), qh, 1, 1) for j in range(i + 1)]
        far = []
        if far_there:
            far = [dot(tile(k_far, j, columns), qh, 1, 1) for j in range(i, tiles)]
        return near, far

    def weigh(unit, scores):
        h, i = unit
        near, far = scores
        near_columns, far_columns = [], []
        for half in range(2):
            a = slice(half * HALF, (half + 1) * HALF)
            near_edge = near[i][: (half + 1) * HALF, a]
            near_pieces = [s[:, a] for s in near[:i]]
            if half == 1:
                near_pieces.append(near_edge[:HALF])
            near_pieces.append(jnp.where(causal, near_edge[half * HALF :], MASKED))
            far_pieces = []
            if far_there:
                far_edge = far[0][half * HALF :, a]
                far_pieces.append(jnp.where(causal, MASKED, far_edge[:HALF]))
                if half == 0:
                    far_pieces.append(far_edge[HALF:])
                far_pieces += [s[:, a] for s in far[1:]]
            top = top_of(near_pieces + far_pieces)
            near_weights = [weights_of(s, top) for s in near_pieces]
            if half == 0:
                near_weights.append(nothing)
            near_columns.append(jnp.concatenate(near_weights, axis=0))
            if far_there:
                far_weights = [weights_of(s, top) for s in far_pieces]
                if half == 1:
                    far_weights.insert(0, nothing)
                far_columns.append(jnp.concatenate(far_weights, axis=0))
            queries = slice(i * TILE + half * HALF, i * TILE + (half + 1) * HALF)
            tops[h : h + 1, queries] = top
        if far_there:
            weights_far[h, i * TILE :, blocks[i]] = jnp.concatenate(far_columns, axis=1)
        return jnp.concatenate(near_columns, axis=1)

    def multiply(unit, weights):
        h, i = unit
        out[head_rows(h), blocks[i]] = dot(v_t[h // group][:, : (i + 1) * TILE], weights, 1, 0)

    in_steps(units_of(group, tok, kv_heads), [score, weigh, multiply])


def middle_kernel(group, *refs):
    place = lax.axis_index("seq")

    @pl.when(place >= 2)
    def _():
        middle_steps(group, True, *refs)

    @pl.when(place == 1)
    def _():
        middle_steps(group, False, *refs)

    @pl.when(place == 0)
    def _():
        q, own, k, out, stage, sems = refs[0], refs[1], refs[4], refs[10], refs[11], refs[12]
        kv_heads = range(k.shape[1] // HEAD_WIDTH)
        write_steps(
            group, kv_heads, q.shape[0], lambda h, b: own[head_rows(h), b], out, stage, sems
        )


def middle_steps(
    group, far_there, q, own, weights_far, tops, k_1, k_2, v_a, v_b, rest, weights, *_
):
    k, v_far = (k_1, k_2), (v_a, v_b)
    tok = q.shape[0]
    kv_heads = range(k_1.shape[1] // HEAD_WIDTH)
    v_t = []
    if far_there:
        v_t = [values_and_ones(v_far[g // PAIR], head_columns(g % PAIR)) for g in kv_heads]
    tiles = tok // TILE
    blocks = [slice(i * TILE, (i + 1) * TILE) for i in range(tiles)]

    def score(unit, _):
        h, i = unit
        qh = q[blocks[i], head_columns(h)]
        return [dot(tile(k, j, head_columns(h // group)), qh, 1, 1) for j in range(tiles)]

    def weigh(unit, scores):
        h, i = unit
        before = tops[h : h + 1, blocks[i]]
        top = jnp.maximum(before, top_of(scores))
        for j, s in enumerate(scores):
            weights[h, blocks[j], blocks[i]] = weights_of(s, top)
        return jnp.exp2((before - top) * EXPONENT)

    def multiply(unit, less):
        h, i = unit
        total = own[head_rows(h), blocks[i]]
        if far_there:
            total += dot(v_t[h // group][:, i * TILE :], weights_far[h, i * TILE :, blocks[i]], 1, 0)
        rest[head_rows(h), blocks[i]] = total * less

    in_steps(units_of(group, tok, kv_heads), [score, weigh, multiply])


def write_steps(group, kv_heads, tok, total_of, out, stage, sems):
    copies = []
    for h, i in units_of(group, tok, kv_heads):
        b = slice(i * TILE, (i + 1) * TILE)
        total = total_of(h, b)
        normal = total[:HEAD_WIDTH] * (1.0 / total[HEAD_WIDTH : HEAD_WIDTH + 1])
        stage[b, head_columns(h)] = normal.astype(jnp.bfloat16).T
        if h % group == group - 1:
            width = group * HEAD_WIDTH
            part = (pl.ds(i * TILE, TILE), pl.ds((h + 1) * HEAD_WIDTH - width, width))
            copies.append(
                pltpu.make_async_copy(stage.at[part], out.at[part], sems.at[len(copies)])
            )
            copies[-1].start()
    for copy in copies:
        copy.wait()


def finish_kernel(group, rest, weights, v, _, out, stage, sems, part):
    tok = weights.shape[1]
    kv_heads = range(part * PAIR, (part + 1) * PAIR)

    @pl.when(lax.axis_index("seq") >= 1)
    def _():
        v_t = [values_and_ones(v, head_columns(g % PAIR)) for g in kv_heads]
        units = units_of(group, tok, kv_heads)
        held = []

        def total_of(h, b):
            at = units.index((h, b.start // TILE))
            for m, i in units[len(held) : at + 2]:
                c = slice(i * TILE, (i + 1) * TILE)
                held.append(dot(v_t[m // group - part * PAIR], weights[m, :, c], 1, 0))
            return rest[head_rows(h), b] + held[at]

        write_steps(group, kv_heads, tok, total_of, out, stage, sems)


def by_heads(
    kernel, name, query_shape, columns, arrays, out_kinds, into=None, own_copies=False
):
    tok, width = query_shape
    heads = width // HEAD_WIDTH
    shapes = dict(
        queries=((tok, width), jnp.bfloat16),
        rest=((heads * (HEAD_WIDTH + ONES), tok), jnp.float32),
        weights=((heads, tok, tok), jnp.bfloat16),
        stat=((heads, tok), jnp.float32),
        output=((tok, width), jnp.bfloat16),
    )
    in_vmem, anywhere = pl.BlockSpec(memory_space=pltpu.VMEM), pl.BlockSpec(memory_space=pl.ANY)
    in_specs = [in_vmem] * len(arrays)
    aliases, scratch = {}, []
    if own_copies:
        in_specs[0] = pl.BlockSpec(memory_space=pltpu.HBM)
        scratch = [pltpu.SemaphoreType.DMA((columns // HEAD_WIDTH,))]
    if into is not None:
        aliases = {len(arrays): out_kinds.index("output")}
        arrays.append(into)
        in_specs.append(anywhere)
    if "output" in out_kinds:
        copies = columns // HEAD_WIDTH * (tok // TILE)
        scratch = [
            pltpu.VMEM((tok, width), jnp.bfloat16),
            pltpu.SemaphoreType.DMA((copies,)),
        ]
    return pl.pallas_call(
        functools.partial(kernel, width // columns),
        in_specs=in_specs,
        out_specs=[anywhere if kind == "output" else in_vmem for kind in out_kinds],
        scratch_shapes=scratch,
        out_shape=[jax.ShapeDtypeStruct(*shapes[kind]) for kind in out_kinds],
        input_output_aliases=aliases,
        compiler_params=pltpu.CompilerParams(vmem_limit_bytes=24 * 1024 * 1024),
        name=name,
    )(*arrays)


def shifted(array, steps):
    count = lax.axis_size("seq")
    return lax.ppermute(array, "seq", [(source, source + steps) for source in range(count - steps)])


def exchanged(array, axis, bit):
    count = lax.axis_size(axis)
    return lax.ppermute(array, axis, [(source, source ^ bit) for source in range(count)])


def on_device(
    normed_input, query, key, value, adapter_down_maps, adapter_up_maps, block_adapter_choice
):
    tok = query.shape[0]
    assert 2 * tok == WINDOW and SEG_LEN % tok == 0
    where = lax.axis_index("seq")
    choice = block_adapter_choice

    even = where % 2 == 0
    barrier = lax.optimization_barrier
    call = functools.partial(by_heads, query_shape=query.shape, columns=key.shape[1])

    def from_one_back(own, far):
        return exchanged(jnp.where(even, own, far), "seq", 1)

    key_1 = first_half(key)
    key_far_1 = shifted(key_1, 2)
    latent, up, key_2 = latent_share(
        choice, normed_input.T, adapter_down_maps, adapter_up_maps, key
    )
    key_far_2 = shifted(key_2, 2)
    bit = 1
    while 2 * bit < lax.axis_size("tp"):
        latent = latent + exchanged(latent, "tp", bit)
        bit *= 2
    key_1, latent = barrier((key_1, latent))
    theirs = exchanged(latent, "tp", bit)
    key_mid_1 = from_one_back(key_1, key_far_1)
    values = adapt(latent, theirs, up, value)
    value_far = [shifted(part, 2) for part in values]
    key_2, values = barrier((key_2, values))
    key_mid_2 = from_one_back(key_2, key_far_2)
    values, key_mid_1 = barrier((values, key_mid_1))
    queries, own, weights_far, tops = call(
        near_far_kernel,
        "near_far",
        arrays=[in_hbm(query), key_1, key_2, *values, key_far_1, key_far_2],
        out_kinds=["queries", "rest", "weights", "stat"],
        own_copies=True,
    )
    values, own = barrier((values, own))
    value_mid = [from_one_back(mine, theirs) for mine, theirs in zip(values, value_far)]
    rest, weights_mid, done = call(
        middle_kernel,
        "middle",
        arrays=[queries, own, weights_far, tops, key_mid_1, key_mid_2, *value_far],
        out_kinds=["rest", "weights", "output"],
    )
    for n, part in enumerate(value_mid):
        [done] = call(
            functools.partial(finish_kernel, part=n),
            "finish",
                arrays=[rest, weights_mid, part],
            out_kinds=["output"],
            into=done,
        )
    return done


def solution(mesh):
    placed = (
        P("seq", "tp"),
        P("seq", "tp"),
        P("seq", "tp"),
        P("seq", "tp"),
        P(None, None, "tp"),
        P(None, None, "tp"),
        P(),
    )
    return jax.shard_map(
        on_device, mesh=mesh, in_specs=placed, out_specs=P("seq", "tp"), check_vma=False
    )
```
